128 devices in a mesh: dp: 16 (over x, y), seq: 8 (over z, core).
Axes of the slice: x: 4, y: 4, z: 4, core: 2. Of those that a mesh axis runs over, the one named last changes fastest.
Arguments:
- tokens: bfloat16 [16384, 2048], P(('dp', 'seq')), may hold values from -36 to 36
- segments: int32 [16384], P(('dp', 'seq')), may hold values from 0 to 2, as said below
- mixer_weights: bfloat16 [2048, 7680], P(('dp', 'seq')), may hold values from -0.125 to 0.125
- norm_gains: bfloat16 [2048, 2], P(('dp', 'seq')), may hold values from 0.5 to 1.5
- gate_weights: bfloat16 [5120, 160], P(('dp', 'seq')), may hold values from -0.5 to 0.5
- channel_terms: bfloat16 [2560, 8], P(('dp', 'seq')), may hold values from -1.5 to 10
- feed_weights: bfloat16 [2048, 18432], P(('dp', 'seq')), may hold values from -0.125 to 0.125
- cotangent: bfloat16 [16384, 2048], P(('dp', 'seq')), may hold values from -6 to 6
Outputs:
- activations: bfloat16 [16384, 2048], P(('dp', 'seq'))
- input_gradient: float32 [16384, 2048], P(('dp', 'seq'))
- mixer_gradient: float32 [2048, 7680], P(('dp', 'seq'))
- gain_gradient: float32 [2048, 2], P(('dp', 'seq'))
- gate_gradient: float32 [5120, 160], P(('dp', 'seq'))
- channel_gradient: float32 [2560, 8], P(('dp', 'seq'))
- feed_gradient: float32 [2048, 18432], P(('dp', 'seq'))
The draws below stay inside these ranges and needn't reach their ends.
Inputs may be any that keep to these rules, and one draw needn't show every extreme that they name: `segments`: in each group of 1024 consecutive tokens the numbers are 0, then 1, then 2, never falling; number 0 covers the first 1 to 127 tokens and number 2 the last 1 to 127.
All inputs are finite; a program needn't handle non-finite values.
Results may differ from the reference program's by a relative error of at most 0.012.
Values may be sent and summed in bfloat16 or wider, within the bound.
A program may use at most 832 MiB of HBM per device.

```python
import math
import jax
import jax.numpy as jnp
from jax import lax

D = 2048
W = 2560
FF = 6144
H = 16
CONV = 4
TOK_DEV = 128
BW = 160
GROUP_TOK = 1024
TOKENS = 16384


def draw_tokens(key, part):
    keys = jax.random.split(key, 3)
    base = jnp.clip(jax.random.normal(keys[0], (TOKENS, D), jnp.float32), -4.0, 4.0)
    row_scale = jnp.exp(jax.random.uniform(keys[1], (TOKENS, 1), jnp.float32, math.log(0.3), math.log(3.0)))
    column_scale = jnp.exp(jax.random.uniform(keys[2], (1, D), jnp.float32, math.log(0.3), math.log(3.0)))
    return (base * row_scale * column_scale).astype(jnp.bfloat16)


def draw_segments(key, part):
    keys = jax.random.split(key, 2)
    groups = TOKENS // GROUP_TOK
    first = jax.random.randint(keys[0], (groups, 1), 1, TOK_DEV)
    final = jax.random.randint(keys[1], (groups, 1), GROUP_TOK - TOK_DEV + 1, GROUP_TOK)
    position = jnp.arange(GROUP_TOK, dtype=jnp.int32)[None, :]
    labels = (position >= first).astype(jnp.int32) + (position >= final).astype(jnp.int32)
    return labels.reshape(TOKENS)


def draw_channel_terms(key, part):
    keys = jax.random.split(key, 4)
    taps = 0.5 * jnp.clip(jax.random.normal(keys[0], (W, CONV), jnp.float32), -3.0, 3.0)
    decay_terms = jax.random.uniform(keys[3], (W, 1), jnp.float32, 4.0, 10.0)
    offsets = 0.3 * jnp.clip(jax.random.normal(keys[1], (W, 1), jnp.float32), -3.0, 3.0)
    gate_offsets = 0.5 * jnp.clip(jax.random.normal(keys[2], (W, 2), jnp.float32), -3.0, 3.0)
    return jnp.concatenate([taps, offsets, gate_offsets, decay_terms], 1).astype(jnp.bfloat16)


def shard_levels(own_key, dims, cuts, least, largest):
    def one(axis_at, shards_of):
        heights = jax.random.uniform(jax.random.fold_in(jax.random.fold_in(own_key, 6), axis_at), (shards_of,), jnp.float32, least / len(cuts), largest / len(cuts))
        return jnp.repeat(jnp.exp(heights), dims[axis_at] // shards_of).reshape((-1,) + (1,) * (len(dims) - axis_at - 1))

    loudness = one(*cuts[0])
    for cut in cuts[1:]:
        loudness = loudness * one(*cut)
    return loudness


def scatter_about(key, extent, scale, reach, shards=(), kind=jnp.bfloat16):
    values = scale * jax.random.normal(key, extent, jnp.float32)
    if shards:
        values = values * shard_levels(key, extent, shards, -0.22, 0.18)
    return jnp.clip(values, -reach, reach).astype(kind)


def setup_inputs(seed: int = 0) -> dict:
    splits = jax.random.split(jax.random.key(seed), 9)
    tokens = draw_tokens(jax.random.fold_in(splits[8], 71), 0)
    segments = draw_segments(jax.random.fold_in(splits[8], 71), 0)
    mixer_weights = scatter_about(splits[2], (D, 3 * W), D ** -0.5, 0.125, ((0, 128),))
    norm_gains = jnp.clip(1.0 + 0.1 * jax.random.normal(splits[3], (D, 2), jnp.float32), 0.5, 1.5).astype(jnp.bfloat16)
    gate_weights = scatter_about(splits[4], (2 * W, BW), BW ** -0.5, 0.5, ((0, 128),))
    channel_terms = draw_channel_terms(jax.random.fold_in(splits[8], 71), 0)
    feed_weights = scatter_about(splits[6], (D, 3 * FF), D ** -0.5, 0.125, ((0, 128),))
    cotangent = scatter_about(splits[7], (TOKENS, D), 1.0, 6.0, ((0, 128),))
    return dict(tokens=tokens, segments=segments, mixer_weights=mixer_weights, norm_gains=norm_gains, gate_weights=gate_weights, channel_terms=channel_terms, feed_weights=feed_weights, cotangent=cotangent)


epsilon = 1e-06
rate_scale = 8.0
highest = lax.Precision.HIGHEST

@jax.custom_vjp
def low(v):
    return lax.optimization_barrier(v.astype(jnp.bfloat16)).astype(jnp.float32)

@jax.custom_vjp
def low_back(v):
    return v

def low_keep(v):
    return (low(v), None)

def low_pass(kept, grad):
    return (grad,)

def back_keep(v):
    return (v, None)

def back_low(kept, grad):
    return (low(grad),)
low.defvjp(low_keep, low_pass)
low_back.defvjp(back_keep, back_low)

def matmul(left, right):
    return jnp.dot(left, right, precision=highest)

def times_rows(left, right):
    return lax.dot_general(left, right, (((1,), (1,)), ((), ())), precision=highest)

def root_norm(value, gain):
    return value * lax.rsqrt(lax.optimization_barrier(jnp.mean(value * value, axis=-1, keepdims=True)) + epsilon) * gain

def combine(earlier, later):
    return (earlier[0] * later[0], later[0] * earlier[1] + later[1])

def recur_inputs(conv, gate_a, gate_x, channel, start):
    recall = jax.nn.sigmoid(gate_a + channel[:, CONV + 1])
    admit = jax.nn.sigmoid(gate_x + channel[:, CONV + 2])
    lograte = -rate_scale * jax.nn.softplus(-channel[:, CONV + 3]) * recall
    decay = jnp.exp(lograte) * (1.0 - start)
    scale = start + (1.0 - start) * jnp.sqrt(-jnp.expm1(2.0 * lograte))
    return (decay, scale * admit * conv)

def forward(inputs, mixer, gains, gates, channel, feed, segment):
    width = mixer.shape[1] // 3
    units = feed.shape[1] // 3
    length = inputs.shape[0]
    rim = CONV - 1
    normed = low(root_norm(inputs, gains[:, 0]))
    branch_x = low_back(matmul(normed, mixer[:, :width]))
    branch_y = low_back(matmul(normed, mixer[:, width:2 * width]))
    labels = segment + 1
    padded_x = jnp.concatenate([jnp.zeros((rim, width), jnp.float32), branch_x], 0)
    padded_l = jnp.concatenate([jnp.zeros((rim,), jnp.int32), labels], 0)
    conv = jnp.zeros((length, width), jnp.float32) + channel[:, CONV]
    for offset in range(CONV):
        same = (padded_l[rim - offset:rim - offset + length] == labels)[:, None]
        conv = conv + channel[:, offset] * jnp.where(same, padded_x[rim - offset:rim - offset + length], 0.0)
    start = (padded_l[rim - 1:rim - 1 + length] != labels).astype(jnp.float32)[:, None]
    lowered = low(conv).reshape(length, H, BW)
    gate_a = low_back(jnp.einsum('thi,hij->thj', lowered, gates[:width].reshape(H, BW, BW), precision=highest)).reshape(length, width)
    gate_x = low_back(jnp.einsum('thi,hij->thj', lowered, gates[width:].reshape(H, BW, BW), precision=highest)).reshape(length, width)
    decay, drive = recur_inputs(conv, gate_a, gate_x, channel, start)
    states = lax.associative_scan(combine, (decay, drive), axis=0)[1]
    mixed = low(jax.nn.gelu(branch_y) * states)
    middle = inputs + low_back(times_rows(mixed, mixer[:, 2 * width:]))
    normed_two = low(root_norm(middle, gains[:, 1]))
    gate = low_back(matmul(normed_two, feed[:, :units]))
    upward = low_back(matmul(normed_two, feed[:, units:2 * units]))
    hidden = low(jax.nn.gelu(gate) * upward)
    return middle + low_back(times_rows(hidden, feed[:, 2 * units:]))

def reference(tokens, segments, mixer_weights, norm_gains, gate_weights, channel_terms, feed_weights, cotangent):
    weights = (mixer_weights.astype(jnp.float32), norm_gains.astype(jnp.float32), gate_weights.astype(jnp.float32), channel_terms.astype(jnp.float32), feed_weights.astype(jnp.float32))
    groups = TOKENS // GROUP_TOK
    inputs = tokens.astype(jnp.float32).reshape(groups, GROUP_TOK, D)
    labels = segments.reshape(groups, GROUP_TOK)
    outer = cotangent.astype(jnp.float32).reshape(groups, GROUP_TOK, D)

    def per_group(totals, pieces):
        group_in, group_labels, group_outer = pieces

        def apply(value, mixer, gains, gates, channel, feed):
            return forward(value, mixer, gains, gates, channel, feed, group_labels)
        result, pullback = jax.vjp(apply, group_in, *weights)
        grads = pullback(group_outer)
        totals = tuple((total + grad for total, grad in zip(totals, grads[1:])))
        return (totals, (result.astype(jnp.bfloat16), grads[0]))
    start_totals = tuple((jnp.zeros(weight.shape, jnp.float32) for weight in weights))
    totals, (results, input_grads) = lax.scan(per_group, start_totals, (inputs, labels, outer))
    return (results.reshape(TOKENS, D), input_grads.reshape(TOKENS, D), totals[0], totals[1], totals[2], totals[3], totals[4])
```

```python
import functools

import jax
import jax.numpy as jnp
from jax import lax
from jax.experimental import pallas as pl
from jax.experimental.pallas import tpu as pltpu
from jax.sharding import PartitionSpec as P

D = 2048
W = 2560
FF = 6144
CONV = 4
BW = 160
SEQ = 8
DP = 16
T = 128
G = 1024
WL = W // SEQ
WP = 384
MW = 3 * WP
FL = FF // SEQ
FW = 3 * FL
HALF = T // 2

epsilon = 1e-06
rate_scale = 8.0
f32 = jnp.float32
bf16 = jnp.bfloat16
MESH = pl.DeviceIdType.MESH
ANY = pl.ANY
VMEM = pltpu.VMEM
DMA = pltpu.SemaphoreType.DMA


class Place:
    def __init__(self):
        self.dp = lax.axis_index("dp")
        self.sq = lax.axis_index("seq")
        self.x, self.y = self.dp // 4, self.dp % 4
        self.z, self.c = self.sq // 2, self.sq % 2

    def chip(self, k):
        return (self.z + k) % 4

    def slot(self, k, c):
        return 2 * self.chip(k) + c

    def z_peer(self, k):
        return (self.dp, 2 * self.chip(k) + self.c)

    def sibling(self):
        return (self.dp, 2 * self.z + 1 - self.c)

    def x_dp(self, k):
        return (self.x + k) % 4 * 4 + self.y

    def y_dp(self, k):
        return self.x * 4 + (self.y + k) % 4

    def dp_peer(self, dp):
        return (dp, self.sq)

    def seq_peer(self, k):
        return (self.dp, (self.sq + k) % SEQ)


def remote(src, dst, send, recv, device):
    return pltpu.make_async_remote_copy(
        src_ref=src, dst_ref=dst, send_sem=send, recv_sem=recv, device_id=device, device_id_type=MESH
    )


def greet(peers):
    barrier = pltpu.get_barrier_semaphore()
    for device in peers:
        pl.semaphore_signal(barrier, inc=1, device_id=device, device_id_type=MESH)
    return barrier, len(peers)


def z_peers(me):
    return [me.z_peer(1), me.z_peer(3), me.sibling()]


def dp_peers(me):
    return [me.dp_peer((me.dp + k) % DP) for k in range(1, DP)]


def seq_peers(me):
    return [me.seq_peer(k) for k in range(1, SEQ)]


class Gather:
    sems = 10

    def __init__(self, me, own, full, send, recv):
        self.me, self.own, self.full, self.send, self.recv = me, own, full, send, recv
        self.sent = []
        self.a, self.b = pl.ds(0, HALF), pl.ds(HALF, HALF)

    def push(self, n, src, dst, device):
        copy = remote(src, dst, self.send.at[n], self.recv.at[n], device)
        copy.start()
        self.sent.append(copy)

    def arrived(self, n, dst):
        remote(dst, dst, self.send.at[n], self.recv.at[n], self.me.sibling()).wait_recv()

    def start(self):
        me, full = self.me, self.full
        mine = me.sq
        right, left = me.z_peer(1), me.z_peer(3)
        self.push(0, self.own.at[self.a], full.at[mine, self.a], right)
        self.push(1, self.own.at[self.b], full.at[mine, self.b], left)
        self.push(2, self.own.at[self.b], full.at[mine, self.b], right)
        self.push(3, self.own.at[self.a], full.at[mine, self.a], left)
        self.push(4, self.own, full.at[mine], me.sibling())

    def forward(self):
        me, full = self.me, self.full
        right, left = me.z_peer(1), me.z_peer(3)
        from_left, from_right = me.slot(3, me.c), me.slot(1, me.c)
        self.arrived(0, full.at[from_left, self.a])
        self.push(5, full.at[from_left, self.a], full.at[from_left, self.a], right)
        self.arrived(1, full.at[from_right, self.b])
        self.push(6, full.at[from_right, self.b], full.at[from_right, self.b], left)

    def across(self):
        me, full = self.me, self.full
        from_left, from_right, far = me.slot(3, me.c), me.slot(1, me.c), me.slot(2, me.c)
        self.arrived(2, full.at[from_left, self.b])
        self.push(7, full.at[from_left], full.at[from_left], me.sibling())
        self.arrived(3, full.at[from_right, self.a])
        self.push(8, full.at[from_right], full.at[from_right], me.sibling())
        self.arrived(5, full.at[far, self.a])
        self.arrived(6, full.at[far, self.b])
        self.push(9, full.at[far], full.at[far], me.sibling())

    def finish(self):
        me, full = self.me, self.full
        other = 1 - me.c
        self.arrived(4, full.at[me.slot(0, other)])
        self.arrived(7, full.at[me.slot(3, other)])
        self.arrived(8, full.at[me.slot(1, other)])
        self.arrived(9, full.at[me.slot(2, other)])
        for copy in self.sent:
            copy.wait_send()


def add_rows(out, at, terms, rows, step=32):
    def body(i, carry):
        here = pl.ds(pl.multiple_of(i * step, step), step)
        total = terms[0](here)
        for term in terms[1:]:
            total = total + term(here)
        there = pl.ds(pl.multiple_of(at + i * step, step), step)
        out[there] = total.astype(out.dtype)
        return carry

    lax.fori_loop(0, rows // step, body, 0)


def reads(ref, start=0):
    def term(here):
        return ref[pl.ds(pl.multiple_of(here.start + start, 16), here.size)].astype(f32)

    return term


class Scatter:
    sems = 10

    @staticmethod
    def scratch(n):
        return [
            VMEM((4, T, n), bf16),
            VMEM((4, T, n), bf16),
            VMEM((2, HALF, n), bf16),
            VMEM((2, HALF, n), bf16),
            VMEM((4, HALF, n), bf16),
            DMA((10,)),
            DMA((10,)),
        ]

    def __init__(self, me, part, other, pair, through, passed, final, send, recv):
        self.me, self.part = me, part
        self.other, self.pair, self.through, self.passed, self.final = other, pair, through, passed, final
        self.send, self.recv = send, recv
        self.sent = []

    def push(self, n, src, dst, device):
        copy = remote(src, dst, self.send.at[n], self.recv.at[n], device)
        copy.start()
        self.sent.append(copy)

    def arrived(self, n, dst):
        remote(dst, dst, self.send.at[n], self.recv.at[n], self.me.sibling()).wait_recv()

    def start(self):
        me = self.me
        for k in (2, 1, 3, 0):
            self.push(k, self.part.at[me.slot(k, 1 - me.c)], self.other.at[k], me.sibling())

    def join(self):
        me = self.me
        a, b = pl.ds(0, HALF), pl.ds(HALF, HALF)
        right, left = me.z_peer(1), me.z_peer(3)
        for k in (2, 1, 3, 0):
            self.arrived(k, self.other.at[k])
            add_rows(
                self.pair.at[k], 0, [reads(self.part.at[me.slot(k, me.c)]), reads(self.other.at[k])], T
            )
            if k == 2:
                self.push(4, self.pair.at[2, a], self.through.at[0], right)
                self.push(5, self.pair.at[2, b], self.through.at[1], left)
            if k == 1:
                self.push(6, self.pair.at[1, b], self.final.at[0], right)
            if k == 3:
                self.push(7, self.pair.at[3, a], self.final.at[1], left)

    def relay(self):
        me = self.me
        right, left = me.z_peer(1), me.z_peer(3)
        self.arrived(4, self.through.at[0])
        add_rows(self.passed.at[0], 0, [reads(self.through.at[0]), reads(self.pair.at[1])], HALF)
        self.push(8, self.passed.at[0], self.final.at[2], right)
        self.arrived(5, self.through.at[1])
        add_rows(self.passed.at[1], 0, [reads(self.through.at[1]), reads(self.pair.at[3], HALF)], HALF)
        self.push(9, self.passed.at[1], self.final.at[3], left)

    def finish(self, out, extra=None):
        for n, k in ((6, 0), (7, 1), (8, 2), (9, 3)):
            self.arrived(n, self.final.at[k])
        more = [] if extra is None else [reads(extra)]
        add_rows(
            out, 0, [reads(self.pair.at[0]), reads(self.final.at[1]), reads(self.final.at[2])] + more, HALF
        )
        more = [] if extra is None else [reads(extra, HALF)]
        add_rows(
            out,
            HALF,
            [reads(self.pair.at[0], HALF), reads(self.final.at[0]), reads(self.final.at[3])] + more,
            HALF,
        )
        for copy in self.sent:
            copy.wait_send()


def prologue_kernel(
    tok, cot, mix, feed, small, gates, chan,
    tok_all, cot_all, mix_all, feed_own, small_all, gain_all, gate_all, chan_all,
    gain_own, gate_own, chan_own, small_in,
    ts, tr, cs, cr, ms, mr, fs, fr, ss, sr, p1s, p1r, p2s, p2r, gs, gr, es, er, hs, hr, ls,
):
    me = Place()
    quarter, at = me.dp // 8, me.dp % 8
    gate_to = (8 * quarter + me.sq, at)
    gate_self = me.sq == at
    chan_to = (8 * (me.dp % 2) + me.sq, me.dp // 2)
    chan_from = (2 * me.sq + me.dp // 8, me.dp % 8)
    chan_self = jnp.logical_and(chan_to[0] == me.dp, chan_to[1] == me.sq)
    barrier, count = greet(seq_peers(me) + dp_peers(me))

    @pl.when(jnp.logical_not(gate_self))
    def _():
        pl.semaphore_signal(barrier, inc=1, device_id=gate_to, device_id_type=MESH)

    @pl.when(jnp.logical_not(chan_self))
    def _():
        pl.semaphore_signal(barrier, inc=1, device_id=chan_from, device_id_type=MESH)

    local = [
        pltpu.make_async_copy(tok, tok_all.at[me.sq], ls.at[0]),
        pltpu.make_async_copy(cot, cot_all.at[me.sq], ls.at[1]),
        pltpu.make_async_copy(mix.at[me.sq], mix_all.at[me.dp, me.sq], ls.at[2]),
        pltpu.make_async_copy(feed.at[me.sq], feed_own.at[me.sq], ls.at[3]),
        pltpu.make_async_copy(small, small_in.at[me.sq], ls.at[4]),
    ]
    for copy in local:
        copy.start()

    pl.semaphore_wait(barrier, count + jnp.where(gate_self, 0, 1) + jnp.where(chan_self, 0, 1))

    sent = []
    order = (4, 3, 5, 2, 6, 1, 7)
    for k in order:
        device = me.seq_peer(k)
        to = (me.sq + k) % SEQ
        sent.append(remote(mix.at[to], mix_all.at[me.dp, me.sq], ms.at[k], mr.at[k], device))
        sent[-1].start()
        sent.append(remote(small, small_in.at[me.sq], ss.at[k], sr.at[k], device))
        sent[-1].start()
    gate_copy = remote(gates, gate_own, hs.at[0], hr.at[0], gate_to)
    chan_copy = remote(chan, chan_own, hs.at[1], hr.at[1], chan_to)
    gate_local = pltpu.make_async_copy(gates, gate_own, ls.at[5])
    chan_local = pltpu.make_async_copy(chan, chan_own, ls.at[6])

    @pl.when(jnp.logical_not(gate_self))
    def _():
        gate_copy.start()

    @pl.when(gate_self)
    def _():
        gate_local.start()

    @pl.when(jnp.logical_not(chan_self))
    def _():
        chan_copy.start()

    @pl.when(chan_self)
    def _():
        chan_local.start()

    first = Gather(me, tok, tok_all, ts, tr)
    first.start()
    for k in order:
        to = (me.sq + k) % SEQ
        sent.append(remote(feed.at[to], feed_own.at[me.sq], fs.at[k], fr.at[k], me.seq_peer(k)))
        sent[-1].start()

    for copy in local:
        copy.wait()
    for k in range(1, SEQ):
        source = (me.sq - k + SEQ) % SEQ
        remote(mix.at[0], mix_all.at[me.dp, source], ms.at[k], mr.at[k], me.sibling()).wait_recv()

    lo, hi = pl.ds(0, 4), pl.ds(4, 4)
    for k in (2, 1, 3):
        block = mix_all.at[me.dp, lo]
        sent.append(remote(block, block, p1s.at[k], p1r.at[k], me.dp_peer(me.x_dp(k))))
        sent[-1].start()
        block = mix_all.at[me.dp, hi]
        sent.append(remote(block, block, p1s.at[4 + k], p1r.at[4 + k], me.dp_peer(me.y_dp(k))))
        sent[-1].start()

    for k in range(1, SEQ):
        source = (me.sq - k + SEQ) % SEQ
        remote(small, small_in.at[source], ss.at[k], sr.at[k], me.sibling()).wait_recv()
    gain = small_in[0, 0:16].astype(f32)
    for k in range(1, SEQ):
        gain = gain + small_in[k, 0:16].astype(f32)
    gain_own[...] = gain.astype(bf16)
    for k in range(SEQ):
        small_all[k] = small_in[k]

    @pl.when(jnp.logical_not(gate_self))
    def _():
        gate_copy.wait()

    @pl.when(gate_self)
    def _():
        gate_local.wait()

    @pl.when(jnp.logical_not(chan_self))
    def _():
        chan_copy.wait()

    @pl.when(chan_self)
    def _():
        chan_local.wait()

    own = [
        pltpu.make_async_copy(gain_own, gain_all.at[me.dp], ls.at[0]),
        pltpu.make_async_copy(gate_own, gate_all.at[me.dp], ls.at[1]),
        pltpu.make_async_copy(chan_own, chan_all.at[me.dp], ls.at[2]),
    ]
    for copy in own:
        copy.start()
    for k in range(1, DP):
        device = me.dp_peer((me.dp + k) % DP)
        for n, (src, dst) in enumerate(((gain_own, gain_all), (gate_own, gate_all), (chan_own, chan_all))):
            sent.append(remote(src, dst.at[me.dp], es.at[n, k], er.at[n, k], device))
            sent[-1].start()

    first.forward()

    for j in (0, 2, 1, 3):
        if j:
            source = me.x_dp(4 - j)
            remote(mix_all.at[source, lo], mix_all.at[source, lo], p1s.at[j], p1r.at[j], me.sibling()).wait_recv()
            source = me.y_dp(4 - j)
            remote(
                mix_all.at[source, hi], mix_all.at[source, hi], p1s.at[4 + j], p1r.at[4 + j], me.sibling()
            ).wait_recv()
        for k in (2, 1, 3):
            block = mix_all.at[me.x_dp((4 - j) % 4), lo]
            sent.append(remote(block, block, p2s.at[j, k], p2r.at[j, k], me.dp_peer(me.y_dp(k))))
            sent[-1].start()
            block = mix_all.at[me.y_dp((4 - j) % 4), hi]
            sent.append(remote(block, block, p2s.at[4 + j, k], p2r.at[4 + j, k], me.dp_peer(me.x_dp(k))))
            sent[-1].start()

    second = Gather(me, cot, cot_all, cs, cr)
    second.start()
    first.across()
    second.forward()
    first.finish()
    second.across()
    second.finish()
    for k in range(1, SEQ):
        source = (me.sq - k + SEQ) % SEQ
        remote(feed.at[0], feed_own.at[source], fs.at[k], fr.at[k], me.sibling()).wait_recv()
    for copy in own:
        copy.wait()
    for k in range(1, DP):
        source = (me.dp - k + DP) % DP
        for n, (src, dst) in enumerate(((gain_own, gain_all), (gate_own, gate_all), (chan_own, chan_all))):
            remote(src, dst.at[source], es.at[n, k], er.at[n, k], me.sibling()).wait_recv()
    for j in range(4):
        for k in (1, 2, 3):
            row = (me.x - j + 4) % 4 * 4 + (me.y - k + 4) % 4
            block = mix_all.at[row, lo]
            remote(block, block, p2s.at[j, k], p2r.at[j, k], me.sibling()).wait_recv()
            row = (me.x - k + 4) % 4 * 4 + (me.y - j + 4) % 4
            block = mix_all.at[row, hi]
            remote(block, block, p2s.at[4 + j, k], p2r.at[4 + j, k], me.sibling()).wait_recv()
    for copy in sent:
        copy.wait_send()


def prologue(tokens, cot, mix, feed, small, gates, chan):
    sds = jax.ShapeDtypeStruct
    hbm, vmem = pl.BlockSpec(memory_space=ANY), pl.BlockSpec(memory_space=VMEM)
    return pl.pallas_call(
        prologue_kernel,
        out_shape=(
            sds((SEQ, T, D), bf16), sds((SEQ, T, D), bf16), sds((DP, SEQ, 16, MW), bf16),
            sds((SEQ, 16, FW), bf16), sds((SEQ, 32, 128), bf16), sds((DP, 16, 128), bf16),
            sds((DP, 16, 512), bf16), sds((DP, 16, 256), bf16),
        ),
        in_specs=[hbm, hbm, hbm, hbm, vmem, vmem, vmem],
        out_specs=[hbm, hbm, hbm, hbm, vmem, vmem, vmem, vmem],
        scratch_shapes=[
            VMEM((16, 128), bf16), VMEM((16, 512), bf16), VMEM((16, 256), bf16), VMEM((SEQ, 32, 128), bf16),
            DMA((10,)), DMA((10,)), DMA((10,)), DMA((10,)),
            DMA((SEQ,)), DMA((SEQ,)), DMA((SEQ,)), DMA((SEQ,)), DMA((SEQ,)), DMA((SEQ,)),
            DMA((8,)), DMA((8,)), DMA((8, 4)), DMA((8, 4)),
            DMA((1,)), DMA((1,)), DMA((3, DP)), DMA((3, DP)), DMA((2,)), DMA((2,)), DMA((8,)),
        ],
        compiler_params=pltpu.CompilerParams(collective_id=1, has_side_effects=True, vmem_limit_bytes=32 << 20),
        cost_estimate=pl.CostEstimate(flops=1000, bytes_accessed=100 << 20, transcendentals=0),
        name="prologue",
    )(tokens, cot, mix, feed, small, gates, chan)


def norm_rows(value, gain):
    return value * lax.rsqrt(jnp.mean(value * value, axis=-1, keepdims=True) + epsilon) * gain


def middle_kernel(part, tok, gain, middle, norm_all, own, *rest):
    scatter, (gs, gr, ls) = rest[:7], rest[7:]
    me = Place()
    barrier, count = greet(z_peers(me))
    pl.semaphore_wait(barrier, count)
    total = Scatter(me, part, *scatter)
    total.start()
    total.join()
    total.relay()
    total.finish(middle, tok)

    def body(i, carry):
        here = pl.ds(pl.multiple_of(i * 16, 16), 16)
        own[here] = norm_rows(middle[here], gain[...]).astype(bf16)
        return carry

    lax.fori_loop(0, T // 16, body, 0)
    keep = pltpu.make_async_copy(own, norm_all.at[me.sq], ls.at[0])
    keep.start()
    gather = Gather(me, own, norm_all, gs, gr)
    gather.start()
    gather.forward()
    gather.across()
    gather.finish()
    keep.wait()


def middle_call(part, tok, gain):
    sds = jax.ShapeDtypeStruct
    hbm, vmem = pl.BlockSpec(memory_space=ANY), pl.BlockSpec(memory_space=VMEM)
    return pl.pallas_call(
        middle_kernel,
        out_shape=(sds((T, D), f32), sds((SEQ, T, D), bf16)),
        in_specs=[vmem, vmem, vmem],
        out_specs=[vmem, hbm],
        scratch_shapes=[VMEM((T, D), bf16)] + Scatter.scratch(D) + [DMA((10,)), DMA((10,)), DMA((1,))],
        compiler_params=pltpu.CompilerParams(collective_id=2, has_side_effects=True, vmem_limit_bytes=40 << 20),
        cost_estimate=pl.CostEstimate(flops=1000, bytes_accessed=100 << 20, transcendentals=0),
        name="middle",
    )(part, tok, gain)


def norm_pull(value, gain, incoming):
    r = lax.rsqrt(jnp.mean(value * value, axis=-1, keepdims=True) + epsilon)
    scaled = incoming * gain
    inner = jnp.mean(value * scaled, axis=-1, keepdims=True)
    normed = value * r
    return r * (scaled - normed * (inner * r)), incoming * normed


def turn_kernel(part, middle, cot, gain, adj_middle, gain_grad, adj_all, adj, own, *rest):
    scatter, (gs, gr, ls) = rest[:7], rest[7:]
    me = Place()
    barrier, count = greet(z_peers(me))
    pl.semaphore_wait(barrier, count)
    total = Scatter(me, part, *scatter)
    total.start()
    total.join()
    total.relay()
    total.finish(adj)

    def body(i, carry):
        here = pl.ds(pl.multiple_of(i * 16, 16), 16)
        pulled, terms = norm_pull(middle[here], gain[...], adj[here])
        value = cot[here].astype(f32) + pulled
        adj_middle[here] = value
        own[here] = value.astype(bf16)
        return carry + jnp.sum(terms, axis=0, keepdims=True)

    gain_grad[...] = lax.fori_loop(0, T // 16, body, jnp.zeros((1, D), f32))
    keep = pltpu.make_async_copy(own, adj_all.at[me.sq], ls.at[0])
    keep.start()
    gather = Gather(me, own, adj_all, gs, gr)
    gather.start()
    gather.forward()
    gather.across()
    gather.finish()
    keep.wait()


def turn_call(part, middle, cot, gain):
    sds = jax.ShapeDtypeStruct
    hbm, vmem = pl.BlockSpec(memory_space=ANY), pl.BlockSpec(memory_space=VMEM)
    return pl.pallas_call(
        turn_kernel,
        out_shape=(sds((T, D), f32), sds((1, D), f32), sds((SEQ, T, D), bf16)),
        in_specs=[vmem] * 4,
        out_specs=[vmem, vmem, hbm],
        scratch_shapes=[VMEM((T, D), f32), VMEM((T, D), bf16)]
        + Scatter.scratch(D)
        + [DMA((10,)), DMA((10,)), DMA((1,))],
        compiler_params=pltpu.CompilerParams(collective_id=3, has_side_effects=True, vmem_limit_bytes=40 << 20),
        cost_estimate=pl.CostEstimate(flops=1000, bytes_accessed=100 << 20, transcendentals=0),
        name="turn",
    )(part, middle, cot, gain)


def close_kernel(
    part, feed_part, mg, eg, tok, adj_middle, middle, gain, gain_two,
    in_grad, act, mix_out, gate_out, chan_out, gain_out,
    adj, r1, s1, r2, last, e_in, gate_sum, chan_sum, gp, gp_in, gain_sum, gain_in, *rest,
):
    one, two = rest[:7], rest[7:14]
    m1s, m1r, m2s, m2r, m3s, m3r, es, er, gs, gr, hs, hr, qs, qr, ls = rest[14:]
    me = Place()
    quarter, at = me.dp // 8, me.dp % 8
    gate_to = (8 * quarter + me.sq, at)
    gate_self = me.sq == at
    chan_from = (8 * (me.dp % 2) + me.sq, me.dp // 2)
    chan_to = (2 * me.sq + me.dp // 8, me.dp % 8)
    chan_self = jnp.logical_and(chan_from[0] == me.dp, chan_from[1] == me.sq)
    barrier, count = greet(seq_peers(me) + dp_peers(me))

    @pl.when(jnp.logical_not(gate_self))
    def _():
        pl.semaphore_signal(barrier, inc=1, device_id=gate_to, device_id_type=MESH)

    @pl.when(jnp.logical_not(chan_self))
    def _():
        pl.semaphore_signal(barrier, inc=1, device_id=chan_from, device_id_type=MESH)

    pl.semaphore_wait(barrier, count + jnp.where(gate_self, 0, 1) + jnp.where(chan_self, 0, 1))

    sent = []

    def push(src, dst, send, recv, device):
        sent.append(remote(src, dst, send, recv, device))
        sent[-1].start()

    def arrived(dst, send, recv):
        remote(dst, dst, send, recv, me.sibling()).wait_recv()

    lo, hi = pl.ds(0, 4), pl.ds(4, 4)
    inner = Scatter(me, part, *one)
    outer = Scatter(me, feed_part, *two)
    inner.start()
    for k in (2, 1, 3):
        push(mg.at[:, (me.y + k) % 4, lo], r1.at[0, k - 1], m1s.at[k], m1r.at[k], me.dp_peer(me.y_dp(k)))
        push(mg.at[(me.x + k) % 4, :, hi], r1.at[1, k - 1], m1s.at[4 + k], m1r.at[4 + k], me.dp_peer(me.x_dp(k)))
    for k in range(1, DP):
        to = (me.dp + k) % DP
        push(eg.at[to], e_in.at[k], es.at[k], er.at[k], me.dp_peer(to))
    inner.join()
    outer.start()
    inner.relay()
    outer.join()
    inner.finish(adj)

    def pull(i, carry):
        here = pl.ds(pl.multiple_of(i * 16, 16), 16)
        pulled, terms = norm_pull(tok[here].astype(f32), gain[...], adj[here])
        in_grad[here] = adj_middle[here] + pulled
        return carry + jnp.sum(terms, axis=0, keepdims=True)

    gain_one = lax.fori_loop(0, T // 16, pull, jnp.zeros((1, D), f32))
    gp[...] = jnp.zeros(gp.shape, f32)
    for k in range(DP):
        gp[k, 0:1] = gain_one[:, k * 128 : (k + 1) * 128]
        gp[k, 1:2] = gain_two[:, k * 128 : (k + 1) * 128]
    for k in range(1, DP):
        to = (me.dp + k) % DP
        push(gp.at[to], gp_in.at[k], gs.at[k], gr.at[k], me.dp_peer(to))
    outer.relay()

    for k in range(1, DP):
        arrived(e_in.at[k], es.at[k], er.at[k])

    def small(n, carry):
        def step(k, total):
            return total + e_in[k, n].astype(f32)

        total = lax.fori_loop(1, DP, step, eg[me.dp, n].astype(f32))

        @pl.when(n < 4)
        def _():
            gate_sum[n] = total

        @pl.when(n == 4)
        def _():
            chan_sum[...] = total

        return carry

    lax.fori_loop(0, 5, small, 0)
    gate_copy = remote(gate_sum, gate_out, hs.at[0], hr.at[0], gate_to)
    chan_copy = remote(chan_sum, chan_out, hs.at[1], hr.at[1], chan_to)
    gate_local = pltpu.make_async_copy(gate_sum, gate_out, ls.at[0])
    chan_local = pltpu.make_async_copy(chan_sum, chan_out, ls.at[1])

    @pl.when(jnp.logical_not(gate_self))
    def _():
        gate_copy.start()

    @pl.when(gate_self)
    def _():
        gate_local.start()

    @pl.when(jnp.logical_not(chan_self))
    def _():
        chan_copy.start()

    @pl.when(chan_self)
    def _():
        chan_local.start()

    for k in (1, 3, 2):
        arrived(r1.at[0, k - 1], m1s.at[k], m1r.at[k])
        arrived(r1.at[1, k - 1], m1s.at[4 + k], m1r.at[4 + k])
    for j in (2, 1, 3, 0):

        def first(i, carry, j=j):
            xx, yy = (me.x + j) % 4, (me.y + j) % 4
            total = mg[xx, me.y, i].astype(f32)
            for k in range(3):
                total = total + r1[0, k, xx, i].astype(f32)
            s1[0, j, i] = total.astype(bf16)
            total = mg[me.x, yy, 4 + i].astype(f32)
            for k in range(3):
                total = total + r1[1, k, yy, i].astype(f32)
            s1[1, j, i] = total.astype(bf16)
            return carry

        lax.fori_loop(0, 4, first, 0)
        if j:
            push(s1.at[0, j], r2.at[0, j - 1], m2s.at[j], m2r.at[j], me.dp_peer(me.x_dp(j)))
            push(s1.at[1, j], r2.at[1, j - 1], m2s.at[4 + j], m2r.at[4 + j], me.dp_peer(me.y_dp(j)))

    for k in range(1, DP):
        arrived(gp_in.at[k], gs.at[k], gr.at[k])

    def gains(k, total):
        return total + gp_in[k]

    gain_sum[...] = lax.fori_loop(1, DP, gains, gp[me.dp])
    for k in range(1, SEQ):
        push(gain_sum, gain_in.at[k], qs.at[k], qr.at[k], me.seq_peer(k))

    outer.finish(adj, middle)

    def lower(i, carry):
        here = pl.ds(pl.multiple_of(i * 16, 16), 16)
        act[here] = adj[here].astype(bf16)
        return carry

    lax.fori_loop(0, T // 16, lower, 0)

    for j in (1, 3, 2):
        arrived(r2.at[0, j - 1], m2s.at[j], m2r.at[j])
        arrived(r2.at[1, j - 1], m2s.at[4 + j], m2r.at[4 + j])

    def second(i, carry):
        for h in range(2):
            total = s1[h, 0, i].astype(f32)
            for k in range(3):
                total = total + r2[h, k, i].astype(f32)
            last[4 * h + i] = total.astype(bf16)
        return carry

    lax.fori_loop(0, 4, second, 0)
    keep = pltpu.make_async_copy(last.at[me.sq], mix_out.at[me.sq], ls.at[2])
    keep.start()
    for k in (4, 3, 5, 2, 6, 1, 7):
        to = (me.sq + k) % SEQ
        push(last.at[to], mix_out.at[me.sq], m3s.at[k], m3r.at[k], me.seq_peer(k))
    for k in range(1, SEQ):
        arrived(gain_in.at[k], qs.at[k], qr.at[k])
    total = gain_sum[...]
    for k in range(1, SEQ):
        total = total + gain_in[k]
    gain_out[...] = total

    @pl.when(jnp.logical_not(gate_self))
    def _():
        gate_copy.wait()

    @pl.when(gate_self)
    def _():
        gate_local.wait()

    @pl.when(jnp.logical_not(chan_self))
    def _():
        chan_copy.wait()

    @pl.when(chan_self)
    def _():
        chan_local.wait()

    for k in range(1, SEQ):
        arrived(mix_out.at[(me.sq - k + SEQ) % SEQ], m3s.at[k], m3r.at[k])
    keep.wait()
    for copy in sent:
        copy.wait_send()


def close_call(part, feed_part, mg, eg, tok, adj_middle, middle, gain, gain_two):
    sds = jax.ShapeDtypeStruct
    vmem = pl.BlockSpec(memory_space=VMEM)
    return pl.pallas_call(
        close_kernel,
        out_shape=(
            sds((T, D), f32), sds((T, D), bf16), sds((SEQ, 16, MW), bf16),
            sds((4, 16, 128), f32), sds((16, 128), f32), sds((8, 128), f32),
        ),
        in_specs=[vmem] * 9,
        out_specs=[vmem] * 6,
        scratch_shapes=[
            VMEM((T, D), f32),
            VMEM((2, 3, 4, 4, 16, MW), bf16), VMEM((2, 4, 4, 16, MW), bf16), VMEM((2, 3, 4, 16, MW), bf16),
            VMEM((SEQ, 16, MW), bf16), VMEM((DP, 5, 16, 128), bf16), VMEM((4, 16, 128), f32),
            VMEM((16, 128), f32), VMEM((DP, 8, 128), f32), VMEM((DP, 8, 128), f32),
            VMEM((8, 128), f32), VMEM((SEQ, 8, 128), f32),
        ]
        + Scatter.scratch(D)
        + Scatter.scratch(D)
        + [
            DMA((8,)), DMA((8,)), DMA((8,)), DMA((8,)), DMA((8,)), DMA((8,)),
            DMA((DP,)), DMA((DP,)), DMA((DP,)), DMA((DP,)), DMA((2,)), DMA((2,)),
            DMA((SEQ,)), DMA((SEQ,)), DMA((3,)),
        ],
        compiler_params=pltpu.CompilerParams(collective_id=4, has_side_effects=True, vmem_limit_bytes=60 << 20),
        cost_estimate=pl.CostEstimate(flops=1000, bytes_accessed=100 << 20, transcendentals=0),
        name="close",
    )(part, feed_part, mg, eg, tok, adj_middle, middle, gain, gain_two)


def swap_kernel(src, dst, ss, sr, ls):
    me = Place()
    barrier, count = greet(seq_peers(me))
    keep = pltpu.make_async_copy(src.at[me.sq], dst.at[me.sq], ls.at[0])
    keep.start()
    pl.semaphore_wait(barrier, count)
    sent = []
    for k in (4, 3, 5, 2, 6, 1, 7):
        to = (me.sq + k) % SEQ
        sent.append(remote(src.at[to], dst.at[me.sq], ss.at[k], sr.at[k], me.seq_peer(k)))
        sent[-1].start()
    for k in range(1, SEQ):
        source = (me.sq - k + SEQ) % SEQ
        remote(dst.at[source], dst.at[source], ss.at[k], sr.at[k], me.sibling()).wait_recv()
    keep.wait()
    for copy in sent:
        copy.wait_send()


def swap_call(src):
    hbm = pl.BlockSpec(memory_space=ANY)
    return pl.pallas_call(
        swap_kernel,
        out_shape=jax.ShapeDtypeStruct(src.shape, src.dtype),
        in_specs=[hbm],
        out_specs=hbm,
        scratch_shapes=[DMA((SEQ,)), DMA((SEQ,)), DMA((1,))],
        compiler_params=pltpu.CompilerParams(collective_id=5, has_side_effects=True),
        cost_estimate=pl.CostEstimate(flops=1000, bytes_accessed=1 << 20, transcendentals=0),
        name="swap",
    )(src)


CHUNK = 256
STEPS = G // CHUNK
contract_last = (((1,), (1,)), ((), ()))
contract_first = (((0,), (0,)), ((), ()))
gelu_c = 0.7978845608028654
gelu_k = 0.044715


def gelu_parts(v):
    square = v * v
    t = jnp.tanh(gelu_c * (v + gelu_k * square * v))
    half = 0.5 * (1.0 + t)
    slope = half + 0.5 * v * (1.0 - t * t) * (gelu_c * (1.0 + 3.0 * gelu_k * square))
    return v * half, slope


def minus_expm1(z):
    series = -z * (1.0 + z * (1 / 2 + z * (1 / 6 + z * (1 / 24 + z * (1 / 120 + z * (1 / 720))))))
    return jnp.where(z > -0.25, series, 1.0 - jnp.exp(z))


def recur(conv, raw_a, raw_x, terms, start):
    recall = jax.nn.sigmoid(raw_a + terms[5:6])
    admit = jax.nn.sigmoid(raw_x + terms[6:7])
    lograte = terms[7:8] * recall
    decay = jnp.exp(lograte) * (1.0 - start)
    root = jnp.sqrt(minus_expm1(2.0 * lograte))
    scale = start + (1.0 - start) * root
    return recall, admit, lograte, decay, root, scale


def nt(left, right):
    return lax.dot_general(left, right, contract_last, preferred_element_type=f32)


def tn(left, right):
    return lax.dot_general(left, right, contract_first, preferred_element_type=f32)


def nn(left, right):
    return jnp.dot(left, right, preferred_element_type=f32)


def mix_kernel(
    tok, w, gates, terms_ref, gain, meta,
    normed, x_out, y_out, conv_out, ra_out, rx_out, prior_out, mixed, part,
    xpad, dec, drv, sts, carry,
):
    step = pl.program_id(0)

    @pl.when(step == 0)
    def _():
        xpad[0:8] = jnp.zeros((8, WP), f32)
        carry[...] = jnp.zeros((8, WP), f32)

    @pl.when(step > 0)
    def _():
        xpad[0:8] = xpad[CHUNK : CHUNK + 8]

    def body(i, c):
        here = pl.ds(pl.multiple_of(i * 16, 16), 16)
        normed[here] = norm_rows(tok[here].astype(f32), gain[...]).astype(bf16)
        return c

    lax.fori_loop(0, CHUNK // 16, body, 0)
    both = nn(normed[...], w[:, : 2 * WP])
    x_out[...] = both[:, :WP]
    xpad[8:] = both[:, :WP]
    y_out[...] = both[:, WP:]
    terms = terms_ref[...]
    start = meta[:, 0:1]
    conv = terms[4:5] + terms[0:1] * both[:, :WP]
    for k in range(1, CONV):
        conv = conv + terms[k : k + 1] * (meta[:, k : k + 1] * xpad[8 - k : 8 - k + CHUNK])
    conv_out[...] = conv
    lowered = conv.astype(bf16)
    raw_a = nn(lowered, gates[0])
    raw_x = nn(lowered, gates[1])
    ra_out[...] = raw_a
    rx_out[...] = raw_x
    recall, admit, lograte, decay, root, scale = recur(conv, raw_a, raw_x, terms, start)
    dec[...] = decay
    drv[...] = scale * admit * conv
    row = lax.broadcasted_iota(jnp.int32, (8, WP), 0)

    def scan(i, before):
        here = pl.ds(pl.multiple_of(i * 8, 8), 8)
        a, b = dec[here], drv[here]
        for s in (1, 2, 4):
            b = b + a * jnp.where(row >= s, pltpu.roll(b, s, 0), 0.0)
            a = a * jnp.where(row >= s, pltpu.roll(a, s, 0), 1.0)
        state = b + a * before
        sts[here] = state
        prior_out[here] = jnp.where(row >= 1, pltpu.roll(state, 1, 0), before)
        return jnp.broadcast_to(state[7:8], (8, WP))

    carry[...] = lax.fori_loop(0, CHUNK // 8, scan, carry[...], unroll=4)
    value, _ = gelu_parts(y_out[...])
    mixed[...] = (value * sts[...]).astype(bf16)
    part[...] = nt(mixed[...], w[:, 2 * WP :]).astype(bf16)


def rows_spec(width, back=False):
    if back:
        return pl.BlockSpec((CHUNK, width), lambda i: (STEPS - 1 - i, 0))
    return pl.BlockSpec((CHUNK, width), lambda i: (i, 0))


def whole(shape):
    return pl.BlockSpec(shape, lambda i: (0,) * len(shape))


def mix_call(tok, w, gates, terms, gain, meta):
    sds = jax.ShapeDtypeStruct
    wide = [sds((G, WP), f32)] * 6
    return pl.pallas_call(
        mix_kernel,
        grid=(STEPS,),
        out_shape=(sds((G, D), bf16), *wide, sds((G, WP), bf16), sds((G, D), bf16)),
        in_specs=[
            rows_spec(D), whole((D, MW)), whole((2, WP, WP)), whole((16, WP)), whole((1, D)), rows_spec(8),
        ],
        out_specs=[rows_spec(D)] + [rows_spec(WP)] * 6 + [rows_spec(WP), rows_spec(D)],
        scratch_shapes=[
            VMEM((CHUNK + 8, WP), f32), VMEM((CHUNK, WP), f32), VMEM((CHUNK, WP), f32),
            VMEM((CHUNK, WP), f32), VMEM((8, WP), f32),
        ],
        compiler_params=pltpu.CompilerParams(vmem_limit_bytes=50 << 20),
        cost_estimate=pl.CostEstimate(flops=2 * G * D * MW, bytes_accessed=30 << 20, transcendentals=0),
        name="mix",
    )(tok, w, gates, terms, gain, meta)


def unmix_kernel(
    adj_out, w, gates, terms_ref, meta, x_in, y_in, conv_in, ra_in, rx_in, prior_in,
    both, part, gate_grad, sums,
    dec, adj, acp, carry,
):
    step = pl.program_id(0)

    @pl.when(step == 0)
    def _():
        dec[CHUNK:] = jnp.zeros((8, WP), f32)
        acp[CHUNK:] = jnp.zeros((8, WP), f32)
        carry[...] = jnp.zeros((8, WP), f32)
        gate_grad[...] = jnp.zeros(gate_grad.shape, f32)
        sums[...] = jnp.zeros(sums.shape, f32)

    @pl.when(step > 0)
    def _():
        dec[CHUNK:] = dec[0:8]
        acp[CHUNK:] = acp[0:8]

    terms = terms_ref[...]
    start = meta[:, 0:1]
    conv, prior = conv_in[...], prior_in[...]
    recall, admit, lograte, decay, root, scale = recur(conv, ra_in[...], rx_in[...], terms, start)
    dec[0:CHUNK] = decay
    states = decay * prior + scale * admit * conv
    adj_mixed = nn(adj_out[...], w[:, 2 * WP :])
    value, slope = gelu_parts(y_in[...])
    adj[...] = adj_mixed * value
    both[:, WP:] = (adj_mixed * states * slope).astype(bf16)
    row = lax.broadcasted_iota(jnp.int32, (8, WP), 0)

    def scan(i, after):
        at = pl.multiple_of((CHUNK // 8 - 1 - i) * 8, 8)
        here = pl.ds(at, 8)
        later = dec[pl.ds(pl.multiple_of(at + 8, 8), 8)]
        a = jnp.where(row < 7, pltpu.roll(dec[here], 7, 0), later[0:1])
        b = adj[here]
        for s in (1, 2, 4):
            b = b + a * jnp.where(row < 8 - s, pltpu.roll(b, 8 - s, 0), 0.0)
            a = a * jnp.where(row < 8 - s, pltpu.roll(a, 8 - s, 0), 1.0)
        value = b + a * after
        adj[here] = value
        return jnp.broadcast_to(value[0:1], (8, WP))

    carry[...] = lax.fori_loop(0, CHUNK // 8, scan, carry[...], unroll=4)
    adjoint = adj[...]
    flow = adjoint * admit * conv
    adj_lograte = adjoint * prior * decay - (1.0 - start) * flow * (jnp.exp(2.0 * lograte) / root)
    adj_ra = adj_lograte * terms[7:8] * (recall * (1.0 - recall))
    adj_rx = flow * scale * (1.0 - admit)

    def total(v):
        return jnp.sum(v, axis=0, keepdims=True)

    sums[5:6] += total(adj_ra)
    sums[6:7] += total(adj_rx)
    sums[7:8] += total(adj_lograte * recall) * terms[8:9]
    low_a, low_x = adj_ra.astype(bf16), adj_rx.astype(bf16)
    lowered = conv.astype(bf16)
    adj_conv = adjoint * scale * admit + nt(low_a, gates[0]) + nt(low_x, gates[1])
    gate_grad[0] += tn(lowered, low_a)
    gate_grad[1] += tn(lowered, low_x)
    acp[0:CHUNK] = adj_conv
    x = x_in[...]
    adj_x = terms[0:1] * adj_conv
    sums[4:5] += total(adj_conv)
    sums[0:1] += total(adj_conv * x)
    for k in range(1, CONV):
        moved = meta[:, 3 + k : 4 + k] * acp[k : k + CHUNK]
        adj_x = adj_x + terms[k : k + 1] * moved
        sums[k : k + 1] += total(moved * x)
    both[:, :WP] = adj_x.astype(bf16)
    part[...] = nt(both[...], w[:, : 2 * WP]).astype(bf16)


def unmix_call(adj_out, w, gates, terms, meta, saved):
    sds = jax.ShapeDtypeStruct
    return pl.pallas_call(
        unmix_kernel,
        grid=(STEPS,),
        out_shape=(sds((G, 2 * WP), bf16), sds((G, D), bf16), sds((2, WP, WP), f32), sds((8, WP), f32)),
        in_specs=[
            rows_spec(D, True), whole((D, MW)), whole((2, WP, WP)), whole((16, WP)), rows_spec(8, True),
        ]
        + [rows_spec(WP, True)] * 6,
        out_specs=[rows_spec(2 * WP, True), rows_spec(D, True), whole((2, WP, WP)), whole((8, WP))],
        scratch_shapes=[
            VMEM((CHUNK + 8, WP), f32), VMEM((CHUNK, WP), f32), VMEM((CHUNK + 8, WP), f32), VMEM((8, WP), f32),
        ],
        compiler_params=pltpu.CompilerParams(vmem_limit_bytes=50 << 20),
        cost_estimate=pl.CostEstimate(flops=2 * G * D * MW, bytes_accessed=30 << 20, transcendentals=0),
        name="unmix",
    )(adj_out, w, gates, terms, meta, *saved)


def feed_kernel(n2, cot, w, part, back, hidden, adj_gu):
    gu = nn(n2[...], w[:, : 2 * FL])
    gate, up = gu[:, :FL], gu[:, FL:]
    adj_hidden = nn(cot[...], w[:, 2 * FL :])
    value, slope = gelu_parts(gate)
    hidden[...] = (value * up).astype(bf16)
    adj_gu[:, :FL] = (adj_hidden * up * slope).astype(bf16)
    adj_gu[:, FL:] = (adj_hidden * value).astype(bf16)
    part[...] = nt(hidden[...], w[:, 2 * FL :]).astype(bf16)
    back[...] = nt(adj_gu[...], w[:, : 2 * FL]).astype(bf16)


def feed_call(n2, cot, w):
    sds = jax.ShapeDtypeStruct
    return pl.pallas_call(
        feed_kernel,
        grid=(STEPS,),
        out_shape=(sds((G, D), bf16), sds((G, D), bf16), sds((G, FL), bf16), sds((G, 2 * FL), bf16)),
        in_specs=[rows_spec(D), rows_spec(D), whole((D, FW))],
        out_specs=[rows_spec(D), rows_spec(D), rows_spec(FL), rows_spec(2 * FL)],
        compiler_params=pltpu.CompilerParams(vmem_limit_bytes=60 << 20),
        cost_estimate=pl.CostEstimate(flops=4 * G * D * FW, bytes_accessed=30 << 20, transcendentals=0),
        name="feed",
    )(n2, cot, w)


def grad_kernel(left, right, left_two, right_two, out):
    width = right.shape[1]
    out[:, :width] = tn(left[...], right[...]).astype(bf16)
    out[:, width:] = tn(left_two[...], right_two[...]).astype(bf16)


def grad_call(left, right, left_two, right_two, name):
    width = right.shape[1] + right_two.shape[1]
    block = 256
    return pl.pallas_call(
        grad_kernel,
        grid=(D // block,),
        out_shape=jax.ShapeDtypeStruct((D, width), bf16),
        in_specs=[
            pl.BlockSpec((G, block), lambda i: (0, i)), whole(right.shape),
            pl.BlockSpec((G, block), lambda i: (0, i)), whole(right_two.shape),
        ],
        out_specs=pl.BlockSpec((block, width), lambda i: (i, 0)),
        compiler_params=pltpu.CompilerParams(vmem_limit_bytes=50 << 20),
        cost_estimate=pl.CostEstimate(flops=2 * G * D * width, bytes_accessed=20 << 20, transcendentals=0),
        name=name,
    )(left, right, left_two, right_two)


def shards(tokens, segments, mixer_weights, norm_gains, gate_weights, channel_terms, feed_weights, cotangent):
    sq = lax.axis_index("seq")
    mix = jnp.pad(mixer_weights.reshape(16, 3, SEQ, WL), ((0, 0), (0, 0), (0, 0), (0, WP - WL)))
    mix = mix.transpose(2, 0, 1, 3).reshape(SEQ, 16, MW)
    feed = feed_weights.reshape(16, 3, SEQ, FL).transpose(2, 0, 1, 3).reshape(SEQ, 16, FW)
    gain_rows = jnp.pad(norm_gains.T, ((0, 0), (0, 112)))
    placed = jnp.where(
        lax.broadcasted_iota(jnp.int32, (SEQ, 1, 1), 0) == sq, gain_rows[None], jnp.zeros((), bf16)
    ).reshape(16, 128)
    small = jnp.concatenate([placed, jnp.pad(segments.astype(bf16)[None], ((0, 15), (0, 0)))], 0)
    gate_block = jnp.pad(gate_weights.reshape(-1), (0, 16 * 512 - 40 * BW)).reshape(16, 512)
    chan_block = jnp.pad(channel_terms.reshape(-1), (0, 16 * 256 - 160)).reshape(16, 256)
    tok_all, cot_all, mix_all, feed_own, small_all, gain_all, gate_all, chan_all = prologue(
        tokens, cotangent, mix, feed, small, gate_block, chan_block
    )
    feed_w = lax.all_gather(feed_own.reshape(T, FW), "dp", axis=0, tiled=True)
    gains = gain_all[:, :, :16].reshape(DP, SEQ, 2, 16).transpose(2, 0, 1, 3).reshape(2, 1, D).astype(f32)
    gate_pair = gate_all.reshape(DP, -1)[:, : 40 * BW].reshape(2, 2, BW, BW)
    gates = jnp.pad(gate_pair[:, 0], ((0, 0), (0, WP - BW), (0, WP - BW))) + jnp.pad(
        gate_pair[:, 1], ((0, 0), (BW, WP - 2 * BW), (BW, WP - 2 * BW))
    )
    channel = chan_all.reshape(DP, -1)[:, :160].reshape(WL, 8).T.astype(f32)
    channel = jnp.pad(channel, ((0, 0), (0, WP - WL)))
    lam = channel[7:8]
    terms = jnp.concatenate(
        [channel[:7], -rate_scale * jax.nn.softplus(-lam), rate_scale * jax.nn.sigmoid(-lam), jnp.zeros((7, WP), f32)], 0
    )
    labels = small_all[:, 16].reshape(G).astype(f32)
    behind = [jnp.concatenate([jnp.full((k,), -1.0, f32), labels[: G - k]]) == labels for k in range(1, CONV)]
    ahead = [jnp.concatenate([behind[k - 1][k:], jnp.zeros((k,), bool)]) for k in range(1, CONV)]
    meta = jnp.stack([jnp.logical_not(behind[0])] + behind + ahead + [behind[0]], 1).astype(f32)
    w = mix_all.reshape(D, MW)
    tok_group, cot_group = tok_all.reshape(G, D), cot_all.reshape(G, D)

    normed, *saved, mixed, part = mix_call(tok_group, w, gates, terms, gains[0], meta)
    middle, norm_two = middle_call(part.reshape(SEQ, T, D), tokens, gains[1])
    norm_two = norm_two.reshape(G, D)
    feed_part, back_part, hidden, adj_gu = feed_call(norm_two, cot_group, feed_w)
    feed_grad = grad_call(norm_two, adj_gu, cot_group, hidden, "feedgrad")
    feed_sum = lax.psum_scatter(feed_grad, "dp", scatter_dimension=0, tiled=True)
    adj_middle, gain_two, adj_all = turn_call(back_part.reshape(SEQ, T, D), middle, cotangent, gains[1])
    adj_all = adj_all.reshape(G, D)
    both, in_part, gate_grad, sums = unmix_call(adj_all, w, gates, terms, meta, saved)
    mix_grad = grad_call(normed, both, adj_all, mixed, "mixgrad")

    gate_piece = jnp.stack([gate_grad[:, :BW, :BW], gate_grad[:, BW : 2 * BW, BW : 2 * BW]], 1)
    gate_piece = jnp.pad(gate_piece.reshape(DP, 40 * BW), ((0, 0), (0, 16 * 512 - 40 * BW))).reshape(DP, 4, 16, 128)
    chan_piece = jnp.pad(sums[:, :WL].T.reshape(DP, 160), ((0, 0), (0, 16 * 128 - 160))).reshape(DP, 1, 16, 128)
    extra = jnp.concatenate([gate_piece, chan_piece], 1).astype(bf16)
    input_gradient, activations, mix_out, gate_out, chan_out, gain_out = close_call(
        in_part.reshape(SEQ, T, D), feed_part.reshape(SEQ, T, D), mix_grad.reshape(4, 4, SEQ, 16, MW), extra,
        tokens, adj_middle, middle, gains[0], gain_two,
    )
    feed_out = swap_call(feed_sum.reshape(SEQ, 16, FW))
    mixer_gradient = (
        mix_out.reshape(SEQ, 16, 3, WP)[..., :WL].transpose(1, 2, 0, 3).reshape(16, 3 * W).astype(f32)
    )
    feed_gradient = feed_out.reshape(SEQ, 16, 3, FL).transpose(1, 2, 0, 3).reshape(16, 3 * FF).astype(f32)
    gate_gradient = gate_out.reshape(-1)[: 40 * BW].reshape(40, BW)
    channel_gradient = chan_out.reshape(-1)[:160].reshape(20, 8)
    gain_gradient = lax.dynamic_slice(gain_out, (0, sq * 16), (2, 16)).T
    return (activations, input_gradient, mixer_gradient, gain_gradient, gate_gradient, channel_gradient, feed_gradient)


def solution(mesh):
    one = P(("dp", "seq"))
    two = P(("dp", "seq"), None)
    placed = (two, one, two, two, two, two, two, two)
    return jax.shard_map(shards, mesh=mesh, in_specs=placed, out_specs=(two,) * 7, check_vma=False)
```

```python
import functools

import jax
import jax.numpy as jnp
from jax import lax
from jax.experimental import pallas as pl
from jax.experimental.pallas import tpu as pltpu
from jax.sharding import PartitionSpec as P

D = 2048
W = 2560
FF = 6144
CONV = 4
BW = 160
SEQ = 8
DP = 16
T = 128
G = 1024
WL = W // SEQ
WP = 384
MW = 3 * WP
FL = FF // SEQ
FW = 3 * FL
HALF = T // 2

epsilon = 1e-06
rate_scale = 8.0
f32 = jnp.float32
bf16 = jnp.bfloat16
MESH = pl.DeviceIdType.MESH
ANY = pl.ANY
VMEM = pltpu.VMEM
DMA = pltpu.SemaphoreType.DMA


class Place:
    def __init__(self):
        self.dp = lax.axis_index("dp")
        self.sq = lax.axis_index("seq")
        self.x, self.y = self.dp // 4, self.dp % 4
        self.z, self.c = self.sq // 2, self.sq % 2

    def chip(self, k):
        return (self.z + k) % 4

    def slot(self, k, c):
        return 2 * self.chip(k) + c

    def z_peer(self, k):
        return (self.dp, 2 * self.chip(k) + self.c)

    def sibling(self):
        return (self.dp, 2 * self.z + 1 - self.c)

    def x_dp(self, k):
        return (self.x + k) % 4 * 4 + self.y

    def y_dp(self, k):
        return self.x * 4 + (self.y + k) % 4

    def dp_peer(self, dp):
        return (dp, self.sq)

    def seq_peer(self, k):
        return (self.dp, (self.sq + k) % SEQ)


def remote(src, dst, send, recv, device):
    return pltpu.make_async_remote_copy(
        src_ref=src, dst_ref=dst, send_sem=send, recv_sem=recv, device_id=device, device_id_type=MESH
    )


def greet(peers):
    barrier = pltpu.get_barrier_semaphore()
    for device in peers:
        pl.semaphore_signal(barrier, inc=1, device_id=device, device_id_type=MESH)
    return barrier, len(peers)


def z_peers(me):
    return [me.z_peer(1), me.z_peer(3), me.sibling()]


def dp_peers(me):
    return [me.dp_peer((me.dp + k) % DP) for k in range(1, DP)]


def seq_peers(me):
    return [me.seq_peer(k) for k in range(1, SEQ)]


class Gather:
    @staticmethod
    def scratch(n):
        return [VMEM((G, n), bf16), DMA((10,)), DMA((10,)), DMA((SEQ,))]

    def __init__(self, me, own, out, full, send, recv, keep):
        self.me, self.own, self.out, self.full = me, own, out, full
        self.send, self.recv, self.keep = send, recv, keep
        self.sent, self.kept = [], []

    def block(self, k, c, half=None):
        base = self.me.slot(k, c) * T
        if half is None:
            return self.full.at[pl.ds(pl.multiple_of(base, T), T)]
        return self.full.at[pl.ds(pl.multiple_of(base + half * HALF, HALF), HALF)]

    def push(self, n, src, dst, device):
        copy = remote(src, dst, self.send.at[n], self.recv.at[n], device)
        copy.start()
        self.sent.append(copy)

    def arrived(self, n, dst):
        remote(dst, dst, self.send.at[n], self.recv.at[n], self.me.sibling()).wait_recv()

    def store(self, k, c):
        if self.out is None:
            return
        there = self.out.at[pl.ds(pl.multiple_of(self.me.slot(k, c) * T, T), T)]
        copy = pltpu.make_async_copy(self.block(k, c), there, self.keep.at[len(self.kept)])
        copy.start()
        self.kept.append(copy)

    def start(self):
        me = self.me
        right, left = me.z_peer(1), me.z_peer(3)
        mine = self.block(0, me.c)
        a, b = self.block(0, me.c, 0), self.block(0, me.c, 1)
        self.push(0, a, a, right)
        self.push(1, b, b, left)
        self.push(2, b, b, right)
        self.push(3, a, a, left)
        self.push(4, mine, mine, me.sibling())
        self.store(0, me.c)

    def forward(self):
        me = self.me
        right, left = me.z_peer(1), me.z_peer(3)
        a, b = self.block(3, me.c, 0), self.block(1, me.c, 1)
        self.arrived(0, a)
        self.push(5, a, a, right)
        self.arrived(1, b)
        self.push(6, b, b, left)

    def across(self):
        me = self.me
        self.arrived(2, self.block(3, me.c, 1))
        whole = self.block(3, me.c)
        self.push(7, whole, whole, me.sibling())
        self.store(3, me.c)
        self.arrived(3, self.block(1, me.c, 0))
        whole = self.block(1, me.c)
        self.push(8, whole, whole, me.sibling())
        self.store(1, me.c)
        self.arrived(5, self.block(2, me.c, 0))
        self.arrived(6, self.block(2, me.c, 1))
        whole = self.block(2, me.c)
        self.push(9, whole, whole, me.sibling())
        self.store(2, me.c)

    def finish(self):
        other = 1 - self.me.c
        for n, k in ((4, 0), (7, 3), (8, 1), (9, 2)):
            self.arrived(n, self.block(k, other))
            self.store(k, other)
        for copy in self.sent:
            copy.wait_send()
        for copy in self.kept:
            copy.wait()


def add_rows(out, at, terms, rows, step=32):
    def body(i, carry):
        here = pl.ds(pl.multiple_of(i * step, step), step)
        total = terms[0](here)
        for term in terms[1:]:
            total = total + term(here)
        there = pl.ds(pl.multiple_of(at + i * step, step), step)
        out[there] = total.astype(out.dtype)
        return carry

    lax.fori_loop(0, rows // step, body, 0)


def reads(ref, start=0):
    def term(here):
        return ref[pl.ds(pl.multiple_of(here.start + start, 16), here.size)].astype(f32)

    return term


class Scatter:
    sems = 10

    @staticmethod
    def scratch(n):
        return [
            VMEM((4, T, n), bf16),
            VMEM((4, T, n), bf16),
            VMEM((2, HALF, n), bf16),
            VMEM((2, HALF, n), bf16),
            VMEM((4, HALF, n), bf16),
            DMA((10,)),
            DMA((10,)),
        ]

    def __init__(self, me, part, other, pair, through, passed, final, send, recv):
        self.me, self.part = me, part
        self.other, self.pair, self.through, self.passed, self.final = other, pair, through, passed, final
        self.send, self.recv = send, recv
        self.sent = []

    def piece(self, k, c):
        return self.part.at[pl.ds(pl.multiple_of(self.me.slot(k, c) * T, T), T)]

    def push(self, n, src, dst, device):
        copy = remote(src, dst, self.send.at[n], self.recv.at[n], device)
        copy.start()
        self.sent.append(copy)

    def arrived(self, n, dst):
        remote(dst, dst, self.send.at[n], self.recv.at[n], self.me.sibling()).wait_recv()

    def start(self):
        me = self.me
        for k in (2, 1, 3, 0):
            self.push(k, self.piece(k, 1 - me.c), self.other.at[k], me.sibling())

    def join(self):
        me = self.me
        a, b = pl.ds(0, HALF), pl.ds(HALF, HALF)
        right, left = me.z_peer(1), me.z_peer(3)
        for k in (2, 1, 3, 0):
            self.arrived(k, self.other.at[k])
            add_rows(
                self.pair.at[k], 0, [reads(self.piece(k, me.c)), reads(self.other.at[k])], T
            )
            if k == 2:
                self.push(4, self.pair.at[2, a], self.through.at[0], right)
                self.push(5, self.pair.at[2, b], self.through.at[1], left)
            if k == 1:
                self.push(6, self.pair.at[1, b], self.final.at[0], right)
            if k == 3:
                self.push(7, self.pair.at[3, a], self.final.at[1], left)

    def relay(self):
        me = self.me
        right, left = me.z_peer(1), me.z_peer(3)
        self.arrived(4, self.through.at[0])
        add_rows(self.passed.at[0], 0, [reads(self.through.at[0]), reads(self.pair.at[1])], HALF)
        self.push(8, self.passed.at[0], self.final.at[2], right)
        self.arrived(5, self.through.at[1])
        add_rows(self.passed.at[1], 0, [reads(self.through.at[1]), reads(self.pair.at[3], HALF)], HALF)
        self.push(9, self.passed.at[1], self.final.at[3], left)

    def finish(self, out, extra=None):
        for n, k in ((6, 0), (7, 1), (8, 2), (9, 3)):
            self.arrived(n, self.final.at[k])
        more = [] if extra is None else [reads(extra)]
        add_rows(
            out, 0, [reads(self.pair.at[0]), reads(self.final.at[1]), reads(self.final.at[2])] + more, HALF
        )
        more = [] if extra is None else [reads(extra, HALF)]
        add_rows(
            out,
            HALF,
            [reads(self.pair.at[0], HALF), reads(self.final.at[0]), reads(self.final.at[3])] + more,
            HALF,
        )
        for copy in self.sent:
            copy.wait_send()


def prologue_kernel(
    tok, cot, mix, feed, small, gates, chan,
    tok_all, cot_all, mix_out, feed_own, small_all, gain_all, gate_all, chan_all,
    gain_own, gate_own, chan_own, small_in, mix_all,
    tf, ts, tr, tk, cf, cs, cr, ck, ms, mr, fs, fr, ss, sr, p1s, p1r, p2s, p2r, gs, gr, es, er, hs, hr, ls,
):
    me = Place()
    quarter, at = me.dp // 8, me.dp % 8
    gate_to = (8 * quarter + me.sq, at)
    gate_self = me.sq == at
    chan_to = (8 * (me.dp % 2) + me.sq, me.dp // 2)
    chan_from = (2 * me.sq + me.dp // 8, me.dp % 8)
    chan_self = jnp.logical_and(chan_to[0] == me.dp, chan_to[1] == me.sq)
    barrier, count = greet(seq_peers(me) + dp_peers(me))

    @pl.when(jnp.logical_not(gate_self))
    def _():
        pl.semaphore_signal(barrier, inc=1, device_id=gate_to, device_id_type=MESH)

    @pl.when(jnp.logical_not(chan_self))
    def _():
        pl.semaphore_signal(barrier, inc=1, device_id=chan_from, device_id_type=MESH)

    local = [
        pltpu.make_async_copy(tok, tf.at[pl.ds(pl.multiple_of(me.sq * T, T), T)], ls.at[0]),
        pltpu.make_async_copy(cot, cf.at[pl.ds(pl.multiple_of(me.sq * T, T), T)], ls.at[1]),
        pltpu.make_async_copy(mix.at[me.sq], mix_all.at[me.dp, me.sq], ls.at[2]),
        pltpu.make_async_copy(feed.at[me.sq], feed_own.at[me.sq], ls.at[3]),
        pltpu.make_async_copy(small, small_in.at[me.sq], ls.at[4]),
    ]
    for copy in local:
        copy.start()

    pl.semaphore_wait(barrier, count + jnp.where(gate_self, 0, 1) + jnp.where(chan_self, 0, 1))

    sent = []
    order = (4, 3, 5, 2, 6, 1, 7)
    for k in order:
        device = me.seq_peer(k)
        to = (me.sq + k) % SEQ
        sent.append(remote(mix.at[to], mix_all.at[me.dp, me.sq], ms.at[k], mr.at[k], device))
        sent[-1].start()
        sent.append(remote(small, small_in.at[me.sq], ss.at[k], sr.at[k], device))
        sent[-1].start()
    gate_copy = remote(gates, gate_own, hs.at[0], hr.at[0], gate_to)
    chan_copy = remote(chan, chan_own, hs.at[1], hr.at[1], chan_to)
    gate_local = pltpu.make_async_copy(gates, gate_own, ls.at[5])
    chan_local = pltpu.make_async_copy(chan, chan_own, ls.at[6])

    @pl.when(jnp.logical_not(gate_self))
    def _():
        gate_copy.start()

    @pl.when(gate_self)
    def _():
        gate_local.start()

    @pl.when(jnp.logical_not(chan_self))
    def _():
        chan_copy.start()

    @pl.when(chan_self)
    def _():
        chan_local.start()

    local[0].wait()
    first = Gather(me, tok, tok_all, tf, ts, tr, tk)
    first.start()
    for k in order:
        to = (me.sq + k) % SEQ
        sent.append(remote(feed.at[to], feed_own.at[me.sq], fs.at[k], fr.at[k], me.seq_peer(k)))
        sent[-1].start()

    for copy in local[1:]:
        copy.wait()
    for k in range(1, SEQ):
        source = (me.sq - k + SEQ) % SEQ
        remote(mix.at[0], mix_all.at[me.dp, source], ms.at[k], mr.at[k], me.sibling()).wait_recv()

    lo, hi = pl.ds(0, 4), pl.ds(4, 4)
    for k in (2, 1, 3):
        block = mix_all.at[me.dp, lo]
        sent.append(remote(block, block, p1s.at[k], p1r.at[k], me.dp_peer(me.x_dp(k))))
        sent[-1].start()
        block = mix_all.at[me.dp, hi]
        sent.append(remote(block, block, p1s.at[4 + k], p1r.at[4 + k], me.dp_peer(me.y_dp(k))))
        sent[-1].start()

    for k in range(1, SEQ):
        source = (me.sq - k + SEQ) % SEQ
        remote(small, small_in.at[source], ss.at[k], sr.at[k], me.sibling()).wait_recv()
    gain = small_in[0, 0:16].astype(f32)
    for k in range(1, SEQ):
        gain = gain + small_in[k, 0:16].astype(f32)
    gain_own[...] = gain.astype(bf16)
    for k in range(SEQ):
        small_all[k] = small_in[k]

    @pl.when(jnp.logical_not(gate_self))
    def _():
        gate_copy.wait()

    @pl.when(gate_self)
    def _():
        gate_local.wait()

    @pl.when(jnp.logical_not(chan_self))
    def _():
        chan_copy.wait()

    @pl.when(chan_self)
    def _():
        chan_local.wait()

    own = [
        pltpu.make_async_copy(gain_own, gain_all.at[me.dp], ls.at[0]),
        pltpu.make_async_copy(gate_own, gate_all.at[me.dp], ls.at[1]),
        pltpu.make_async_copy(chan_own, chan_all.at[me.dp], ls.at[2]),
    ]
    for copy in own:
        copy.start()
    for k in range(1, DP):
        device = me.dp_peer((me.dp + k) % DP)
        for n, (src, dst) in enumerate(((gain_own, gain_all), (gate_own, gate_all), (chan_own, chan_all))):
            sent.append(remote(src, dst.at[me.dp], es.at[n, k], er.at[n, k], device))
            sent[-1].start()

    first.forward()
    second = Gather(me, cot, cot_all, cf, cs, cr, ck)
    second.start()

    for j in (0, 2, 1, 3):
        if j:
            source = me.x_dp(4 - j)
            remote(mix_all.at[source, lo], mix_all.at[source, lo], p1s.at[j], p1r.at[j], me.sibling()).wait_recv()
            source = me.y_dp(4 - j)
            remote(
                mix_all.at[source, hi], mix_all.at[source, hi], p1s.at[4 + j], p1r.at[4 + j], me.sibling()
            ).wait_recv()
        for k in (2, 1, 3):
            block = mix_all.at[me.x_dp((4 - j) % 4), lo]
            sent.append(remote(block, block, p2s.at[j, k], p2r.at[j, k], me.dp_peer(me.y_dp(k))))
            sent[-1].start()
            block = mix_all.at[me.y_dp((4 - j) % 4), hi]
            sent.append(remote(block, block, p2s.at[4 + j, k], p2r.at[4 + j, k], me.dp_peer(me.x_dp(k))))
            sent[-1].start()

    first.across()
    second.forward()
    first.finish()
    second.across()
    second.finish()
    for k in range(1, SEQ):
        source = (me.sq - k + SEQ) % SEQ
        remote(feed.at[0], feed_own.at[source], fs.at[k], fr.at[k], me.sibling()).wait_recv()
    for copy in own:
        copy.wait()
    for k in range(1, DP):
        source = (me.dp - k + DP) % DP
        for n, (src, dst) in enumerate(((gain_own, gain_all), (gate_own, gate_all), (chan_own, chan_all))):
            remote(src, dst.at[source], es.at[n, k], er.at[n, k], me.sibling()).wait_recv()
    for j in range(4):
        for k in (1, 2, 3):
            row = (me.x - j + 4) % 4 * 4 + (me.y - k + 4) % 4
            block = mix_all.at[row, lo]
            remote(block, block, p2s.at[j, k], p2r.at[j, k], me.sibling()).wait_recv()
            row = (me.x - k + 4) % 4 * 4 + (me.y - j + 4) % 4
            block = mix_all.at[row, hi]
            remote(block, block, p2s.at[4 + j, k], p2r.at[4 + j, k], me.sibling()).wait_recv()
    keep = pltpu.make_async_copy(mix_all, mix_out, ls.at[7])
    keep.start()
    for copy in sent:
        copy.wait_send()
    keep.wait()


def prologue(tokens, cot, mix, feed, small, gates, chan):
    sds = jax.ShapeDtypeStruct
    hbm, vmem = pl.BlockSpec(memory_space=ANY), pl.BlockSpec(memory_space=VMEM)
    return pl.pallas_call(
        prologue_kernel,
        out_shape=(
            sds((G, D), bf16), sds((G, D), bf16), sds((DP, SEQ, 16, MW), bf16),
            sds((SEQ, 16, FW), bf16), sds((SEQ, 32, 128), bf16), sds((DP, 16, 128), bf16),
            sds((DP, 16, 512), bf16), sds((DP, 16, 256), bf16),
        ),
        in_specs=[hbm, hbm, hbm, hbm, vmem, vmem, vmem],
        out_specs=[hbm, hbm, hbm, hbm, vmem, vmem, vmem, vmem],
        scratch_shapes=[
            VMEM((16, 128), bf16), VMEM((16, 512), bf16), VMEM((16, 256), bf16), VMEM((SEQ, 32, 128), bf16),
            VMEM((DP, SEQ, 16, MW), bf16), *Gather.scratch(D), *Gather.scratch(D),
            DMA((SEQ,)), DMA((SEQ,)), DMA((SEQ,)), DMA((SEQ,)), DMA((SEQ,)), DMA((SEQ,)),
            DMA((8,)), DMA((8,)), DMA((8, 4)), DMA((8, 4)),
            DMA((1,)), DMA((1,)), DMA((3, DP)), DMA((3, DP)), DMA((2,)), DMA((2,)), DMA((8,)),
        ],
        compiler_params=pltpu.CompilerParams(collective_id=1, has_side_effects=True, vmem_limit_bytes=62 << 20),
        cost_estimate=pl.CostEstimate(flops=1000, bytes_accessed=100 << 20, transcendentals=0),
        name="prologue",
    )(tokens, cot, mix, feed, small, gates, chan)


def norm_rows(value, gain):
    return value * lax.rsqrt(jnp.mean(value * value, axis=-1, keepdims=True) + epsilon) * gain


def middle_kernel(part, tok, gain, middle, norm_all, *rest):
    scatter, gathering = rest[:7], rest[7:]
    me = Place()
    mine = pl.multiple_of(me.sq * T, T)
    own = gathering[0]
    barrier, count = greet(z_peers(me))
    pl.semaphore_wait(barrier, count)
    total = Scatter(me, part, *scatter)
    total.start()
    total.join()
    total.relay()
    total.finish(middle, tok)

    def body(i, carry):
        here = pl.ds(pl.multiple_of(i * 16, 16), 16)
        there = pl.ds(pl.multiple_of(mine + i * 16, 16), 16)
        own[there] = norm_rows(middle[here], gain[...]).astype(bf16)
        return carry

    lax.fori_loop(0, T // 16, body, 0)
    gather = Gather(me, own, norm_all, *gathering)
    gather.start()
    gather.forward()
    gather.across()
    gather.finish()


def middle_call(part, tok, gain):
    sds = jax.ShapeDtypeStruct
    hbm, vmem = pl.BlockSpec(memory_space=ANY), pl.BlockSpec(memory_space=VMEM)
    return pl.pallas_call(
        middle_kernel,
        out_shape=(sds((T, D), f32), sds((G, D), bf16)),
        in_specs=[vmem, vmem, vmem],
        out_specs=[vmem, hbm],
        scratch_shapes=Scatter.scratch(D) + Gather.scratch(D),
        compiler_params=pltpu.CompilerParams(collective_id=2, has_side_effects=True, vmem_limit_bytes=62 << 20),
        cost_estimate=pl.CostEstimate(flops=1000, bytes_accessed=100 << 20, transcendentals=0),
        name="middle",
    )(part, tok, gain)


def norm_pull(value, gain, incoming):
    r = lax.rsqrt(jnp.mean(value * value, axis=-1, keepdims=True) + epsilon)
    scaled = incoming * gain
    inner = jnp.mean(value * scaled, axis=-1, keepdims=True)
    normed = value * r
    return r * (scaled - normed * (inner * r)), incoming * normed


def turn_kernel(part, middle, cot, gain, adj_middle, gain_grad, adj_all, adj, *rest):
    scatter, gathering = rest[:7], rest[7:]
    me = Place()
    mine = pl.multiple_of(me.sq * T, T)
    own = gathering[0]
    barrier, count = greet(z_peers(me))
    pl.semaphore_wait(barrier, count)
    total = Scatter(me, part, *scatter)
    total.start()
    total.join()
    total.relay()
    total.finish(adj)

    def body(i, carry):
        here = pl.ds(pl.multiple_of(i * 16, 16), 16)
        pulled, terms = norm_pull(middle[here], gain[...], adj[here])
        value = cot[here].astype(f32) + pulled
        adj_middle[here] = value
        own[pl.ds(pl.multiple_of(mine + i * 16, 16), 16)] = value.astype(bf16)
        return carry + jnp.sum(terms, axis=0, keepdims=True)

    gain_grad[...] = lax.fori_loop(0, T // 16, body, jnp.zeros((1, D), f32))
    gather = Gather(me, own, adj_all, *gathering)
    gather.start()
    gather.forward()
    gather.across()
    gather.finish()


def turn_call(part, middle, cot, gain):
    sds = jax.ShapeDtypeStruct
    hbm, vmem = pl.BlockSpec(memory_space=ANY), pl.BlockSpec(memory_space=VMEM)
    return pl.pallas_call(
        turn_kernel,
        out_shape=(sds((T, D), f32), sds((1, D), f32), sds((G, D), bf16)),
        in_specs=[vmem] * 4,
        out_specs=[vmem, vmem, hbm],
        scratch_shapes=[VMEM((T, D), f32)] + Scatter.scratch(D) + Gather.scratch(D),
        compiler_params=pltpu.CompilerParams(collective_id=3, has_side_effects=True, vmem_limit_bytes=62 << 20),
        cost_estimate=pl.CostEstimate(flops=1000, bytes_accessed=100 << 20, transcendentals=0),
        name="turn",
    )(part, middle, cot, gain)


def close_kernel(
    part, feed_part, normed_in, both_in, adj_in, mixed_in, eg, tok, adj_middle, middle, gain, gain_two,
    in_grad, act, mix_out, gate_out, chan_out, gain_out,
    normed, both, adj_out, mixed, mg, adj, r1, s1, r2, last, e_in, gate_sum, chan_sum, gp, gp_in, gain_sum, gain_in, *rest,
):
    one, two = rest[:7], rest[7:14]
    m1s, m1r, m2s, m2r, m3s, m3r, es, er, gs, gr, hs, hr, qs, qr, ls, ws = rest[14:]
    me = Place()
    loads = [
        pltpu.make_async_copy(src, dst, ws.at[n])
        for n, (src, dst) in enumerate(
            ((normed_in, normed), (both_in, both), (adj_in, adj_out), (mixed_in, mixed))
        )
    ]
    for copy in loads:
        copy.start()
    quarter, at = me.dp // 8, me.dp % 8
    gate_to = (8 * quarter + me.sq, at)
    gate_self = me.sq == at
    chan_from = (8 * (me.dp % 2) + me.sq, me.dp // 2)
    chan_to = (2 * me.sq + me.dp // 8, me.dp % 8)
    chan_self = jnp.logical_and(chan_from[0] == me.dp, chan_from[1] == me.sq)
    barrier, count = greet(seq_peers(me) + dp_peers(me))

    @pl.when(jnp.logical_not(gate_self))
    def _():
        pl.semaphore_signal(barrier, inc=1, device_id=gate_to, device_id_type=MESH)

    @pl.when(jnp.logical_not(chan_self))
    def _():
        pl.semaphore_signal(barrier, inc=1, device_id=chan_from, device_id_type=MESH)

    pl.semaphore_wait(barrier, count + jnp.where(gate_self, 0, 1) + jnp.where(chan_self, 0, 1))

    sent = []

    def push(src, dst, send, recv, device):
        sent.append(remote(src, dst, send, recv, device))
        sent[-1].start()

    def arrived(dst, send, recv):
        remote(dst, dst, send, recv, me.sibling()).wait_recv()

    lo, hi = pl.ds(0, 4), pl.ds(4, 4)
    inner = Scatter(me, part, *one)
    outer = Scatter(me, feed_part, *two)
    inner.start()
    for k in range(1, DP):
        to = (me.dp + k) % DP
        push(eg.at[to], e_in.at[k], es.at[k], er.at[k], me.dp_peer(to))
    inner.join()
    for copy in loads:
        copy.wait()

    def tile(i, carry):
        here = pl.ds(pl.multiple_of(i * 256, 256), 256)
        left = tn(normed[:, here], both[...]).astype(bf16)
        right = tn(adj_out[:, here], mixed[...]).astype(bf16)
        for h in range(2):
            for n in range(SEQ):
                rows = slice(h * T + n * 16, h * T + (n + 1) * 16)
                mg[i // 2, i % 2 * 2 + h, n, :, : 2 * WP] = left[rows]
                mg[i // 2, i % 2 * 2 + h, n, :, 2 * WP :] = right[rows]
        return carry

    lax.fori_loop(0, 8, tile, 0)
    for k in (2, 1, 3):
        push(mg.at[:, (me.y + k) % 4, lo], r1.at[0, k - 1], m1s.at[k], m1r.at[k], me.dp_peer(me.y_dp(k)))
        push(mg.at[(me.x + k) % 4, :, hi], r1.at[1, k - 1], m1s.at[4 + k], m1r.at[4 + k], me.dp_peer(me.x_dp(k)))
    outer.start()
    inner.relay()
    outer.join()
    inner.finish(adj)

    def pull(i, carry):
        here = pl.ds(pl.multiple_of(i * 16, 16), 16)
        pulled, terms = norm_pull(tok[here].astype(f32), gain[...], adj[here])
        in_grad[here] = adj_middle[here] + pulled
        return carry + jnp.sum(terms, axis=0, keepdims=True)

    gain_one = lax.fori_loop(0, T // 16, pull, jnp.zeros((1, D), f32))
    gp[...] = jnp.zeros(gp.shape, f32)
    for k in range(DP):
        gp[k, 0:1] = gain_one[:, k * 128 : (k + 1) * 128]
        gp[k, 1:2] = gain_two[:, k * 128 : (k + 1) * 128]
    for k in range(1, DP):
        to = (me.dp + k) % DP
        push(gp.at[to], gp_in.at[k], gs.at[k], gr.at[k], me.dp_peer(to))
    outer.relay()

    for k in range(1, DP):
        arrived(e_in.at[k], es.at[k], er.at[k])

    def small(n, carry):
        def step(k, total):
            return total + e_in[k, n].astype(f32)

        total = lax.fori_loop(1, DP, step, eg[me.dp, n].astype(f32))

        @pl.when(n < 4)
        def _():
            gate_sum[n] = total

        @pl.when(n == 4)
        def _():
            chan_sum[...] = total

        return carry

    lax.fori_loop(0, 5, small, 0)
    gate_copy = remote(gate_sum, gate_out, hs.at[0], hr.at[0], gate_to)
    chan_copy = remote(chan_sum, chan_out, hs.at[1], hr.at[1], chan_to)
    gate_local = pltpu.make_async_copy(gate_sum, gate_out, ls.at[0])
    chan_local = pltpu.make_async_copy(chan_sum, chan_out, ls.at[1])

    @pl.when(jnp.logical_not(gate_self))
    def _():
        gate_copy.start()

    @pl.when(gate_self)
    def _():
        gate_local.start()

    @pl.when(jnp.logical_not(chan_self))
    def _():
        chan_copy.start()

    @pl.when(chan_self)
    def _():
        chan_local.start()

    for k in (1, 3, 2):
        arrived(r1.at[0, k - 1], m1s.at[k], m1r.at[k])
        arrived(r1.at[1, k - 1], m1s.at[4 + k], m1r.at[4 + k])
    for j in (2, 1, 3, 0):

        def first(i, carry, j=j):
            xx, yy = (me.x + j) % 4, (me.y + j) % 4
            total = mg[xx, me.y, i].astype(f32)
            for k in range(3):
                total = total + r1[0, k, xx, i].astype(f32)
            s1[0, j, i] = total.astype(bf16)
            total = mg[me.x, yy, 4 + i].astype(f32)
            for k in range(3):
                total = total + r1[1, k, yy, i].astype(f32)
            s1[1, j, i] = total.astype(bf16)
            return carry

        lax.fori_loop(0, 4, first, 0)
        if j:
            push(s1.at[0, j], r2.at[0, j - 1], m2s.at[j], m2r.at[j], me.dp_peer(me.x_dp(j)))
            push(s1.at[1, j], r2.at[1, j - 1], m2s.at[4 + j], m2r.at[4 + j], me.dp_peer(me.y_dp(j)))

    for k in range(1, DP):
        arrived(gp_in.at[k], gs.at[k], gr.at[k])

    def gains(k, total):
        return total + gp_in[k]

    gain_sum[...] = lax.fori_loop(1, DP, gains, gp[me.dp])
    for k in range(1, SEQ):
        push(gain_sum, gain_in.at[k], qs.at[k], qr.at[k], me.seq_peer(k))

    outer.finish(adj, middle)

    def lower(i, carry):
        here = pl.ds(pl.multiple_of(i * 16, 16), 16)
        act[here] = adj[here].astype(bf16)
        return carry

    lax.fori_loop(0, T // 16, lower, 0)

    for j in (1, 3, 2):
        arrived(r2.at[0, j - 1], m2s.at[j], m2r.at[j])
        arrived(r2.at[1, j - 1], m2s.at[4 + j], m2r.at[4 + j])

    def second(i, carry):
        for h in range(2):
            total = s1[h, 0, i].astype(f32)
            for k in range(3):
                total = total + r2[h, k, i].astype(f32)
            last[4 * h + i] = total.astype(bf16)
        return carry

    lax.fori_loop(0, 4, second, 0)
    keep = pltpu.make_async_copy(last.at[me.sq], mix_out.at[me.sq], ls.at[2])
    keep.start()
    for k in (4, 3, 5, 2, 6, 1, 7):
        to = (me.sq + k) % SEQ
        push(last.at[to], mix_out.at[me.sq], m3s.at[k], m3r.at[k], me.seq_peer(k))
    for k in range(1, SEQ):
        arrived(gain_in.at[k], qs.at[k], qr.at[k])
    total = gain_sum[...]
    for k in range(1, SEQ):
        total = total + gain_in[k]
    gain_out[...] = total

    @pl.when(jnp.logical_not(gate_self))
    def _():
        gate_copy.wait()

    @pl.when(gate_self)
    def _():
        gate_local.wait()

    @pl.when(jnp.logical_not(chan_self))
    def _():
        chan_copy.wait()

    @pl.when(chan_self)
    def _():
        chan_local.wait()

    for k in range(1, SEQ):
        arrived(mix_out.at[(me.sq - k + SEQ) % SEQ], m3s.at[k], m3r.at[k])
    keep.wait()
    for copy in sent:
        copy.wait_send()


def close_call(part, feed_part, normed, both, adj_out, mixed, eg, tok, adj_middle, middle, gain, gain_two):
    sds = jax.ShapeDtypeStruct
    vmem = pl.BlockSpec(memory_space=VMEM)
    return pl.pallas_call(
        close_kernel,
        out_shape=(
            sds((T, D), f32), sds((T, D), bf16), sds((SEQ, 16, MW), bf16),
            sds((4, 16, 128), f32), sds((16, 128), f32), sds((8, 128), f32),
        ),
        in_specs=[vmem] * 2 + [pl.BlockSpec(memory_space=ANY)] * 4 + [vmem] * 6,
        out_specs=[vmem] * 6,
        scratch_shapes=[
            VMEM((G, D), bf16), VMEM((G, 2 * WP), bf16), VMEM((G, D), bf16), VMEM((G, WP), bf16),
            VMEM((4, 4, SEQ, 16, MW), bf16),
            VMEM((T, D), f32),
            VMEM((2, 3, 4, 4, 16, MW), bf16), VMEM((2, 4, 4, 16, MW), bf16), VMEM((2, 3, 4, 16, MW), bf16),
            VMEM((SEQ, 16, MW), bf16), VMEM((DP, 5, 16, 128), bf16), VMEM((4, 16, 128), f32),
            VMEM((16, 128), f32), VMEM((DP, 8, 128), f32), VMEM((DP, 8, 128), f32),
            VMEM((8, 128), f32), VMEM((SEQ, 8, 128), f32),
        ]
        + Scatter.scratch(D)
        + Scatter.scratch(D)
        + [
            DMA((8,)), DMA((8,)), DMA((8,)), DMA((8,)), DMA((8,)), DMA((8,)),
            DMA((DP,)), DMA((DP,)), DMA((DP,)), DMA((DP,)), DMA((2,)), DMA((2,)),
            DMA((SEQ,)), DMA((SEQ,)), DMA((3,)), DMA((4,)),
        ],
        compiler_params=pltpu.CompilerParams(collective_id=4, has_side_effects=True, vmem_limit_bytes=62 << 20),
        cost_estimate=pl.CostEstimate(flops=1000, bytes_accessed=100 << 20, transcendentals=0),
        name="close",
    )(part, feed_part, normed, both, adj_out, mixed, eg, tok, adj_middle, middle, gain, gain_two)


def swap_kernel(src, dst, ss, sr, ls):
    me = Place()
    barrier, count = greet(seq_peers(me))
    keep = pltpu.make_async_copy(src.at[me.sq], dst.at[me.sq], ls.at[0])
    keep.start()
    pl.semaphore_wait(barrier, count)
    sent = []
    for k in (4, 3, 5, 2, 6, 1, 7):
        to = (me.sq + k) % SEQ
        sent.append(remote(src.at[to], dst.at[me.sq], ss.at[k], sr.at[k], me.seq_peer(k)))
        sent[-1].start()
    for k in range(1, SEQ):
        source = (me.sq - k + SEQ) % SEQ
        remote(dst.at[source], dst.at[source], ss.at[k], sr.at[k], me.sibling()).wait_recv()
    keep.wait()
    for copy in sent:
        copy.wait_send()


def swap_call(src):
    hbm = pl.BlockSpec(memory_space=ANY)
    return pl.pallas_call(
        swap_kernel,
        out_shape=jax.ShapeDtypeStruct(src.shape, src.dtype),
        in_specs=[hbm],
        out_specs=hbm,
        scratch_shapes=[DMA((SEQ,)), DMA((SEQ,)), DMA((1,))],
        compiler_params=pltpu.CompilerParams(collective_id=5, has_side_effects=True, vmem_limit_bytes=62 << 20),
        cost_estimate=pl.CostEstimate(flops=1000, bytes_accessed=1 << 20, transcendentals=0),
        name="swap",
    )(src)


CHUNK = 256
STEPS = G // CHUNK
contract_last = (((1,), (1,)), ((), ()))
contract_first = (((0,), (0,)), ((), ()))
gelu_c = 0.7978845608028654
gelu_k = 0.044715


def gelu_parts(v):
    square = v * v
    t = jnp.tanh(gelu_c * (v + gelu_k * square * v))
    half = 0.5 * (1.0 + t)
    slope = half + 0.5 * v * (1.0 - t * t) * (gelu_c * (1.0 + 3.0 * gelu_k * square))
    return v * half, slope


def minus_expm1(z):
    series = -z * (1.0 + z * (1 / 2 + z * (1 / 6 + z * (1 / 24 + z * (1 / 120 + z * (1 / 720))))))
    return jnp.where(z > -0.25, series, 1.0 - jnp.exp(z))


def recur(conv, raw_a, raw_x, terms, start):
    recall = jax.nn.sigmoid(raw_a + terms[5:6])
    admit = jax.nn.sigmoid(raw_x + terms[6:7])
    lograte = terms[7:8] * recall
    decay = jnp.exp(lograte) * (1.0 - start)
    root = jnp.sqrt(minus_expm1(2.0 * lograte))
    scale = start + (1.0 - start) * root
    return recall, admit, lograte, decay, root, scale


def nt(left, right):
    return lax.dot_general(left, right, contract_last, preferred_element_type=f32)


def tn(left, right):
    return lax.dot_general(left, right, contract_first, preferred_element_type=f32)


def nn(left, right):
    return jnp.dot(left, right, preferred_element_type=f32)


def mix_kernel(
    tok, w, gates, terms_ref, gain, meta,
    normed, x_out, y_out, conv_out, ra_out, rx_out, prior_out, mixed, part,
    xpad, dec, drv, sts, carry,
):
    step = pl.program_id(0)

    @pl.when(step == 0)
    def _():
        xpad[0:8] = jnp.zeros((8, WP), f32)
        carry[...] = jnp.zeros((8, WP), f32)

    @pl.when(step > 0)
    def _():
        xpad[0:8] = xpad[CHUNK : CHUNK + 8]

    def body(i, c):
        here = pl.ds(pl.multiple_of(i * 16, 16), 16)
        normed[here] = norm_rows(tok[here].astype(f32), gain[...]).astype(bf16)
        return c

    lax.fori_loop(0, CHUNK // 16, body, 0)
    both = nn(normed[...], w[:, : 2 * WP])
    x_out[...] = both[:, :WP]
    xpad[8:] = both[:, :WP]
    y_out[...] = both[:, WP:]
    terms = terms_ref[...]
    start = meta[:, 0:1]
    conv = terms[4:5] + terms[0:1] * both[:, :WP]
    for k in range(1, CONV):
        conv = conv + terms[k : k + 1] * (meta[:, k : k + 1] * xpad[8 - k : 8 - k + CHUNK])
    conv_out[...] = conv
    lowered = conv.astype(bf16)
    raw_a = nn(lowered, gates[0])
    raw_x = nn(lowered, gates[1])
    ra_out[...] = raw_a
    rx_out[...] = raw_x
    recall, admit, lograte, decay, root, scale = recur(conv, raw_a, raw_x, terms, start)
    dec[...] = decay
    drv[...] = scale * admit * conv
    row = lax.broadcasted_iota(jnp.int32, (8, WP), 0)

    def scan(i, before):
        here = pl.ds(pl.multiple_of(i * 8, 8), 8)
        a, b = dec[here], drv[here]
        for s in (1, 2, 4):
            b = b + a * jnp.where(row >= s, pltpu.roll(b, s, 0), 0.0)
            a = a * jnp.where(row >= s, pltpu.roll(a, s, 0), 1.0)
        state = b + a * before
        sts[here] = state
        prior_out[here] = jnp.where(row >= 1, pltpu.roll(state, 1, 0), before)
        return jnp.broadcast_to(state[7:8], (8, WP))

    carry[...] = lax.fori_loop(0, CHUNK // 8, scan, carry[...], unroll=4)
    value, _ = gelu_parts(y_out[...])
    mixed[...] = (value * sts[...]).astype(bf16)
    part[...] = nt(mixed[...], w[:, 2 * WP :]).astype(bf16)


def rows_spec(width, back=False):
    if back:
        return pl.BlockSpec((CHUNK, width), lambda i: (STEPS - 1 - i, 0))
    return pl.BlockSpec((CHUNK, width), lambda i: (i, 0))


def whole(shape):
    return pl.BlockSpec(shape, lambda i: (0,) * len(shape))


def mix_call(tok, w, gates, terms, gain, meta):
    sds = jax.ShapeDtypeStruct
    wide = [sds((G, WP), f32)] * 6
    return pl.pallas_call(
        mix_kernel,
        grid=(STEPS,),
        out_shape=(sds((G, D), bf16), *wide, sds((G, WP), bf16), sds((G, D), bf16)),
        in_specs=[
            rows_spec(D), whole((D, MW)), whole((2, WP, WP)), whole((16, WP)), whole((1, D)), rows_spec(8),
        ],
        out_specs=[rows_spec(D)] + [rows_spec(WP)] * 6 + [rows_spec(WP), rows_spec(D)],
        scratch_shapes=[
            VMEM((CHUNK + 8, WP), f32), VMEM((CHUNK, WP), f32), VMEM((CHUNK, WP), f32),
            VMEM((CHUNK, WP), f32), VMEM((8, WP), f32),
        ],
        compiler_params=pltpu.CompilerParams(vmem_limit_bytes=62 << 20),
        cost_estimate=pl.CostEstimate(flops=2 * G * D * MW, bytes_accessed=30 << 20, transcendentals=0),
        name="mix",
    )(tok, w, gates, terms, gain, meta)


def unmix_kernel(
    adj_out, w, gates, terms_ref, meta, x_in, y_in, conv_in, ra_in, rx_in, prior_in,
    both, part, gate_grad, sums,
    dec, adj, acp, carry,
):
    step = pl.program_id(0)

    @pl.when(step == 0)
    def _():
        dec[CHUNK:] = jnp.zeros((8, WP), f32)
        acp[CHUNK:] = jnp.zeros((8, WP), f32)
        carry[...] = jnp.zeros((8, WP), f32)
        gate_grad[...] = jnp.zeros(gate_grad.shape, f32)
        sums[...] = jnp.zeros(sums.shape, f32)

    @pl.when(step > 0)
    def _():
        dec[CHUNK:] = dec[0:8]
        acp[CHUNK:] = acp[0:8]

    terms = terms_ref[...]
    start = meta[:, 0:1]
    conv, prior = conv_in[...], prior_in[...]
    recall, admit, lograte, decay, root, scale = recur(conv, ra_in[...], rx_in[...], terms, start)
    dec[0:CHUNK] = decay
    states = decay * prior + scale * admit * conv
    adj_mixed = nn(adj_out[...], w[:, 2 * WP :])
    value, slope = gelu_parts(y_in[...])
    adj[...] = adj_mixed * value
    both[:, WP:] = (adj_mixed * states * slope).astype(bf16)
    row = lax.broadcasted_iota(jnp.int32, (8, WP), 0)

    def scan(i, after):
        at = pl.multiple_of((CHUNK // 8 - 1 - i) * 8, 8)
        here = pl.ds(at, 8)
        later = dec[pl.ds(pl.multiple_of(at + 8, 8), 8)]
        a = jnp.where(row < 7, pltpu.roll(dec[here], 7, 0), later[0:1])
        b = adj[here]
        for s in (1, 2, 4):
            b = b + a * jnp.where(row < 8 - s, pltpu.roll(b, 8 - s, 0), 0.0)
            a = a * jnp.where(row < 8 - s, pltpu.roll(a, 8 - s, 0), 1.0)
        value = b + a * after
        adj[here] = value
        return jnp.broadcast_to(value[0:1], (8, WP))

    carry[...] = lax.fori_loop(0, CHUNK // 8, scan, carry[...], unroll=4)
    adjoint = adj[...]
    flow = adjoint * admit * conv
    adj_lograte = adjoint * prior * decay - (1.0 - start) * flow * (jnp.exp(2.0 * lograte) / root)
    adj_ra = adj_lograte * terms[7:8] * (recall * (1.0 - recall))
    adj_rx = flow * scale * (1.0 - admit)

    def total(v):
        return jnp.sum(v, axis=0, keepdims=True)

    sums[5:6] += total(adj_ra)
    sums[6:7] += total(adj_rx)
    sums[7:8] += total(adj_lograte * recall) * terms[8:9]
    low_a, low_x = adj_ra.astype(bf16), adj_rx.astype(bf16)
    lowered = conv.astype(bf16)
    adj_conv = adjoint * scale * admit + nt(low_a, gates[0]) + nt(low_x, gates[1])
    gate_grad[0] += tn(lowered, low_a)
    gate_grad[1] += tn(lowered, low_x)
    acp[0:CHUNK] = adj_conv
    x = x_in[...]
    adj_x = terms[0:1] * adj_conv
    sums[4:5] += total(adj_conv)
    sums[0:1] += total(adj_conv * x)
    for k in range(1, CONV):
        moved = meta[:, 3 + k : 4 + k] * acp[k : k + CHUNK]
        adj_x = adj_x + terms[k : k + 1] * moved
        sums[k : k + 1] += total(moved * x)
    both[:, :WP] = adj_x.astype(bf16)
    part[...] = nt(both[...], w[:, : 2 * WP]).astype(bf16)


def unmix_call(adj_out, w, gates, terms, meta, saved):
    sds = jax.ShapeDtypeStruct
    return pl.pallas_call(
        unmix_kernel,
        grid=(STEPS,),
        out_shape=(sds((G, 2 * WP), bf16), sds((G, D), bf16), sds((2, WP, WP), f32), sds((8, WP), f32)),
        in_specs=[
            rows_spec(D, True), whole((D, MW)), whole((2, WP, WP)), whole((16, WP)), rows_spec(8, True),
        ]
        + [rows_spec(WP, True)] * 6,
        out_specs=[rows_spec(2 * WP, True), rows_spec(D, True), whole((2, WP, WP)), whole((8, WP))],
        scratch_shapes=[
            VMEM((CHUNK + 8, WP), f32), VMEM((CHUNK, WP), f32), VMEM((CHUNK + 8, WP), f32), VMEM((8, WP), f32),
        ],
        compiler_params=pltpu.CompilerParams(vmem_limit_bytes=62 << 20),
        cost_estimate=pl.CostEstimate(flops=2 * G * D * MW, bytes_accessed=30 << 20, transcendentals=0),
        name="unmix",
    )(adj_out, w, gates, terms, meta, *saved)


def feed_kernel(n2, cot, w, part, back, hidden, adj_gu):
    gu = nn(n2[...], w[:, : 2 * FL])
    gate, up = gu[:, :FL], gu[:, FL:]
    adj_hidden = nn(cot[...], w[:, 2 * FL :])
    value, slope = gelu_parts(gate)
    hidden[...] = (value * up).astype(bf16)
    adj_gu[:, :FL] = (adj_hidden * up * slope).astype(bf16)
    adj_gu[:, FL:] = (adj_hidden * value).astype(bf16)
    part[...] = nt(hidden[...], w[:, 2 * FL :]).astype(bf16)
    back[...] = nt(adj_gu[...], w[:, : 2 * FL]).astype(bf16)


def feed_call(n2, cot, w):
    sds = jax.ShapeDtypeStruct
    return pl.pallas_call(
        feed_kernel,
        grid=(STEPS,),
        out_shape=(sds((G, D), bf16), sds((G, D), bf16), sds((G, FL), bf16), sds((G, 2 * FL), bf16)),
        in_specs=[rows_spec(D), rows_spec(D), whole((D, FW))],
        out_specs=[rows_spec(D), rows_spec(D), rows_spec(FL), rows_spec(2 * FL)],
        compiler_params=pltpu.CompilerParams(vmem_limit_bytes=62 << 20),
        cost_estimate=pl.CostEstimate(flops=4 * G * D * FW, bytes_accessed=30 << 20, transcendentals=0),
        name="feed",
    )(n2, cot, w)


def grad_kernel(left, right, left_two, right_two, out):
    width = right.shape[1]
    out[:, :width] = tn(left[...], right[...]).astype(bf16)
    out[:, width:] = tn(left_two[...], right_two[...]).astype(bf16)


def grad_call(left, right, left_two, right_two, name):
    width = right.shape[1] + right_two.shape[1]
    block = 256
    return pl.pallas_call(
        grad_kernel,
        grid=(D // block,),
        out_shape=jax.ShapeDtypeStruct((D, width), bf16),
        in_specs=[
            pl.BlockSpec((G, block), lambda i: (0, i)), whole(right.shape),
            pl.BlockSpec((G, block), lambda i: (0, i)), whole(right_two.shape),
        ],
        out_specs=pl.BlockSpec((block, width), lambda i: (i, 0)),
        compiler_params=pltpu.CompilerParams(vmem_limit_bytes=62 << 20),
        cost_estimate=pl.CostEstimate(flops=2 * G * D * width, bytes_accessed=20 << 20, transcendentals=0),
        name=name,
    )(left, right, left_two, right_two)


def shards(tokens, segments, mixer_weights, norm_gains, gate_weights, channel_terms, feed_weights, cotangent):
    sq = lax.axis_index("seq")
    mix = jnp.pad(mixer_weights.reshape(16, 3, SEQ, WL), ((0, 0), (0, 0), (0, 0), (0, WP - WL)))
    mix = mix.transpose(2, 0, 1, 3).reshape(SEQ, 16, MW)
    feed = feed_weights.reshape(16, 3, SEQ, FL).transpose(2, 0, 1, 3).reshape(SEQ, 16, FW)
    gain_rows = jnp.pad(norm_gains.T, ((0, 0), (0, 112)))
    placed = jnp.where(
        lax.broadcasted_iota(jnp.int32, (SEQ, 1, 1), 0) == sq, gain_rows[None], jnp.zeros((), bf16)
    ).reshape(16, 128)
    small = jnp.concatenate([placed, jnp.pad(segments.astype(bf16)[None], ((0, 15), (0, 0)))], 0)
    gate_block = jnp.pad(gate_weights.reshape(-1), (0, 16 * 512 - 40 * BW)).reshape(16, 512)
    chan_block = jnp.pad(channel_terms.reshape(-1), (0, 16 * 256 - 160)).reshape(16, 256)
    tok_all, cot_all, mix_all, feed_own, small_all, gain_all, gate_all, chan_all = prologue(
        tokens, cotangent, mix, feed, small, gate_block, chan_block
    )
    feed_w = lax.all_gather(feed_own.reshape(T, FW), "dp", axis=0, tiled=True)
    gains = gain_all[:, :, :16].reshape(DP, SEQ, 2, 16).transpose(2, 0, 1, 3).reshape(2, 1, D).astype(f32)
    gate_pair = gate_all.reshape(DP, -1)[:, : 40 * BW].reshape(2, 2, BW, BW)
    gates = jnp.pad(gate_pair[:, 0], ((0, 0), (0, WP - BW), (0, WP - BW))) + jnp.pad(
        gate_pair[:, 1], ((0, 0), (BW, WP - 2 * BW), (BW, WP - 2 * BW))
    )
    channel = chan_all.reshape(DP, -1)[:, :160].reshape(WL, 8).T.astype(f32)
    channel = jnp.pad(channel, ((0, 0), (0, WP - WL)))
    lam = channel[7:8]
    terms = jnp.concatenate(
        [channel[:7], -rate_scale * jax.nn.softplus(-lam), rate_scale * jax.nn.sigmoid(-lam), jnp.zeros((7, WP), f32)], 0
    )
    labels = small_all[:, 16].reshape(G).astype(f32)
    behind = [jnp.concatenate([jnp.full((k,), -1.0, f32), labels[: G - k]]) == labels for k in range(1, CONV)]
    ahead = [jnp.concatenate([behind[k - 1][k:], jnp.zeros((k,), bool)]) for k in range(1, CONV)]
    meta = jnp.stack([jnp.logical_not(behind[0])] + behind + ahead + [behind[0]], 1).astype(f32)
    w = mix_all.reshape(D, MW)
    tok_group, cot_group = tok_all, cot_all

    normed, *saved, mixed, part = mix_call(tok_group, w, gates, terms, gains[0], meta)
    middle, norm_two = middle_call(part, tokens, gains[1])
    feed_part, back_part, hidden, adj_gu = feed_call(norm_two, cot_group, feed_w)
    feed_grad = grad_call(norm_two, adj_gu, cot_group, hidden, "feedgrad")
    feed_sum = lax.psum_scatter(feed_grad, "dp", scatter_dimension=0, tiled=True)
    adj_middle, gain_two, adj_all = turn_call(back_part, middle, cotangent, gains[1])
    both, in_part, gate_grad, sums = unmix_call(adj_all, w, gates, terms, meta, saved)

    gate_piece = jnp.stack([gate_grad[:, :BW, :BW], gate_grad[:, BW : 2 * BW, BW : 2 * BW]], 1)
    gate_piece = jnp.pad(gate_piece.reshape(DP, 40 * BW), ((0, 0), (0, 16 * 512 - 40 * BW))).reshape(DP, 4, 16, 128)
    chan_piece = jnp.pad(sums[:, :WL].T.reshape(DP, 160), ((0, 0), (0, 16 * 128 - 160))).reshape(DP, 1, 16, 128)
    extra = jnp.concatenate([gate_piece, chan_piece], 1).astype(bf16)
    input_gradient, activations, mix_out, gate_out, chan_out, gain_out = close_call(
        in_part, feed_part, normed, both, adj_all, mixed, extra, tokens, adj_middle, middle, gains[0], gain_two,
    )
    feed_out = swap_call(feed_sum.reshape(SEQ, 16, FW))
    mixer_gradient = (
        mix_out.reshape(SEQ, 16, 3, WP)[..., :WL].transpose(1, 2, 0, 3).reshape(16, 3 * W).astype(f32)
    )
    feed_gradient = feed_out.reshape(SEQ, 16, 3, FL).transpose(1, 2, 0, 3).reshape(16, 3 * FF).astype(f32)
    gate_gradient = gate_out.reshape(-1)[: 40 * BW].reshape(40, BW)
    channel_gradient = chan_out.reshape(-1)[:160].reshape(20, 8)
    gain_gradient = lax.dynamic_slice(gain_out, (0, sq * 16), (2, 16)).T
    return (activations, input_gradient, mixer_gradient, gain_gradient, gate_gradient, channel_gradient, feed_gradient)


def solution(mesh):
    one = P(("dp", "seq"))
    two = P(("dp", "seq"), None)
    placed = (two, one, two, two, two, two, two, two)
    return jax.shard_map(shards, mesh=mesh, in_specs=placed, out_specs=(two,) * 7, check_vma=False)
```

```python
import functools

import jax
import jax.numpy as jnp
from jax import lax
from jax.experimental import pallas as pl
from jax.experimental.pallas import tpu as pltpu
from jax.sharding import PartitionSpec as P

D = 2048
W = 2560
FF = 6144
CONV = 4
BW = 160
SEQ = 8
DP = 16
T = 128
G = 1024
WL = W // SEQ
WP = 384
MW = 3 * WP
FL = FF // SEQ
FW = 3 * FL
HALF = T // 2
MINOR = 192

epsilon = 1e-06
rate_scale = 8.0
f32 = jnp.float32
bf16 = jnp.bfloat16
MESH = pl.DeviceIdType.MESH
ANY = pl.ANY
VMEM = pltpu.VMEM
DMA = pltpu.SemaphoreType.DMA


class Place:
    def __init__(self):
        self.dp = lax.axis_index("dp")
        self.sq = lax.axis_index("seq")
        self.x, self.y = self.dp // 4, self.dp % 4
        self.z, self.c = self.sq // 2, self.sq % 2

    def chip(self, k):
        return (self.z + k) % 4

    def slot(self, k, c):
        return 2 * self.chip(k) + c

    def z_peer(self, k):
        return (self.dp, 2 * self.chip(k) + self.c)

    def sibling(self):
        return (self.dp, 2 * self.z + 1 - self.c)

    def x_dp(self, k):
        return (self.x + k) % 4 * 4 + self.y

    def y_dp(self, k):
        return self.x * 4 + (self.y + k) % 4

    def dp_peer(self, dp):
        return (dp, self.sq)

    def seq_peer(self, k):
        return (self.dp, (self.sq + k) % SEQ)


def remote(src, dst, send, recv, device):
    return pltpu.make_async_remote_copy(
        src_ref=src, dst_ref=dst, send_sem=send, recv_sem=recv, device_id=device, device_id_type=MESH
    )


def greet(peers):
    barrier = pltpu.get_barrier_semaphore()
    for device in peers:
        pl.semaphore_signal(barrier, inc=1, device_id=device, device_id_type=MESH)
    return barrier, len(peers)


def z_peers(me):
    return [me.z_peer(1), me.z_peer(3), me.sibling()]


def ring_peers(me):
    return [me.dp_peer(me.x_dp(1)), me.dp_peer(me.x_dp(3)), me.dp_peer(me.y_dp(1)), me.dp_peer(me.y_dp(3))]


def dp_peers(me):
    return [me.dp_peer((me.dp + k) % DP) for k in range(1, DP)]


def seq_peers(me):
    return [me.seq_peer(k) for k in range(1, SEQ)]


class Gather:
    @staticmethod
    def scratch(n):
        return [VMEM((G, n), bf16), DMA((10,)), DMA((10,)), DMA((SEQ,))]

    def __init__(self, me, own, out, full, send, recv, keep):
        self.me, self.own, self.out, self.full = me, own, out, full
        self.send, self.recv, self.keep = send, recv, keep
        self.sent, self.kept = [], []

    def block(self, k, c, half=None):
        base = self.me.slot(k, c) * T
        if half is None:
            return self.full.at[pl.ds(pl.multiple_of(base, T), T)]
        return self.full.at[pl.ds(pl.multiple_of(base + half * HALF, HALF), HALF)]

    def push(self, n, src, dst, device):
        copy = remote(src, dst, self.send.at[n], self.recv.at[n], device)
        copy.start()
        self.sent.append(copy)

    def arrived(self, n, dst):
        remote(dst, dst, self.send.at[n], self.recv.at[n], self.me.sibling()).wait_recv()

    def store(self, k, c):
        if self.out is None:
            return
        there = self.out.at[pl.ds(pl.multiple_of(self.me.slot(k, c) * T, T), T)]
        copy = pltpu.make_async_copy(self.block(k, c), there, self.keep.at[len(self.kept)])
        copy.start()
        self.kept.append(copy)

    def start(self):
        me = self.me
        right, left = me.z_peer(1), me.z_peer(3)
        mine = self.block(0, me.c)
        a, b = self.block(0, me.c, 0), self.block(0, me.c, 1)
        self.push(0, a, a, right)
        self.push(1, b, b, left)
        self.push(2, b, b, right)
        self.push(3, a, a, left)
        self.push(4, mine, mine, me.sibling())
        self.store(0, me.c)

    def forward(self):
        me = self.me
        right, left = me.z_peer(1), me.z_peer(3)
        a, b = self.block(3, me.c, 0), self.block(1, me.c, 1)
        self.arrived(0, a)
        self.push(5, a, a, right)
        self.arrived(1, b)
        self.push(6, b, b, left)

    def hand_over(self, n, k):
        whole = self.block(k, self.me.c)
        self.push(n, whole, whole, self.me.sibling())
        self.store(k, self.me.c)

    def across_left(self):
        self.arrived(2, self.block(3, self.me.c, 1))
        self.hand_over(7, 3)

    def across_right(self):
        self.arrived(3, self.block(1, self.me.c, 0))
        self.hand_over(8, 1)

    def across_far(self):
        self.arrived(5, self.block(2, self.me.c, 0))
        self.arrived(6, self.block(2, self.me.c, 1))
        self.hand_over(9, 2)

    def across(self):
        self.across_left()
        self.across_right()
        self.across_far()

    def taken(self, n, k):
        self.arrived(n, self.block(k, 1 - self.me.c))
        self.store(k, 1 - self.me.c)

    def own_pair(self):
        self.taken(4, 0)

    def left_pair(self):
        self.taken(7, 3)

    def right_pair(self):
        self.taken(8, 1)

    def far_pair(self):
        self.taken(9, 2)

    def drain(self):
        for copy in self.sent:
            copy.wait_send()
        for copy in self.kept:
            copy.wait()

    def finish(self):
        self.own_pair()
        self.left_pair()
        self.right_pair()
        self.far_pair()
        self.drain()


class Spread:
    sems = 40

    def __init__(self, me, full, rows, send, recv):
        self.me, self.full, self.rows, self.send, self.recv = me, full, rows, send, recv

    def at(self, h, i, j):
        me = self.me
        dx, dy = (i, j) if h == 0 else (j, i)
        return (me.x + dx + 4) % 4 * 4 + (me.y + dy + 4) % 4

    def block(self, h, i, j, q=None):
        half = self.rows // 2
        base = self.at(h, i, j) * self.rows + h * half
        if q is None:
            return self.full.at[pl.ds(pl.multiple_of(base, 16), half)]
        return self.full.at[pl.ds(pl.multiple_of(base + q * (half // 2), 16), half // 2)]

    def push(self, h, n, block, i, j):
        n = 20 * h + n
        remote(block, block, self.send.at[n], self.recv.at[n], self.me.dp_peer(self.at(h, i, j))).start()

    def arrived(self, h, n, block):
        n = 20 * h + n
        remote(block, block, self.send.at[n], self.recv.at[n], self.me.sibling()).wait_recv()

    def second(self, t, i):
        for h in range(2):
            block = self.block(h, i, 0)
            self.push(h, 4 + 4 * t, block, 0, 1)
            self.push(h, 5 + 4 * t, block, 0, -1)

    def start(self):
        for h in range(2):
            block = self.block(h, 0, 0)
            self.push(h, 0, block, 1, 0)
            self.push(h, 1, block, -1, 0)
        self.second(0, 0)

    def turn(self):
        for h in range(2):
            self.arrived(h, 0, self.block(h, -1, 0))
            self.push(h, 2, self.block(h, -1, 0, 0), 1, 0)
            self.arrived(h, 1, self.block(h, 1, 0))
            self.push(h, 3, self.block(h, 1, 0, 1), -1, 0)
        self.second(1, -1)
        self.second(2, 1)

    def far(self):
        for h in range(2):
            self.arrived(h, 2, self.block(h, 2, 0, 0))
            self.arrived(h, 3, self.block(h, 2, 0, 1))
        self.second(3, 2)

    def hand_on(self, t):
        i = (0, -1, 1, 2)[t]
        for h in range(2):
            self.arrived(h, 4 + 4 * t, self.block(h, i, -1))
            self.push(h, 6 + 4 * t, self.block(h, i, -1, 0), 0, 1)
            self.arrived(h, 5 + 4 * t, self.block(h, i, 1))
            self.push(h, 7 + 4 * t, self.block(h, i, 1, 1), 0, -1)

    def finish(self):
        for t, i in enumerate((0, -1, 1, 2)):
            for h in range(2):
                self.arrived(h, 6 + 4 * t, self.block(h, i, 2, 0))
                self.arrived(h, 7 + 4 * t, self.block(h, i, 2, 1))

    def drain(self):
        for h in range(2):
            for n in range(20):
                handed = n in (2, 3) or (n >= 4 and n % 4 >= 2)
                block = self.block(h, 0, 0, 0 if handed else None)
                n = 20 * h + n
                remote(block, block, self.send.at[n], self.recv.at[n], self.me.sibling()).wait_send()


def add_rows(out, at, terms, rows, step=32):
    def body(i, carry):
        here = pl.ds(pl.multiple_of(i * step, step), step)
        total = terms[0](here)
        for term in terms[1:]:
            total = total + term(here)
        there = pl.ds(pl.multiple_of(at + i * step, step), step)
        out[there] = total.astype(out.dtype)
        return carry

    lax.fori_loop(0, rows // step, body, 0)


def reads(ref, start=0):
    def term(here):
        return ref[pl.ds(pl.multiple_of(here.start + start, 16), here.size)].astype(f32)

    return term


class Scatter:
    sems = 10

    @staticmethod
    def scratch(n):
        return [
            VMEM((4, T, n), bf16),
            VMEM((4, T, n), bf16),
            VMEM((2, HALF, n), bf16),
            VMEM((2, HALF, n), bf16),
            VMEM((4, HALF, n), bf16),
            DMA((10,)),
            DMA((10,)),
        ]

    def __init__(self, me, part, other, pair, through, passed, final, send, recv):
        self.me, self.part = me, part
        self.other, self.pair, self.through, self.passed, self.final = other, pair, through, passed, final
        self.send, self.recv = send, recv
        self.sent = []

    def piece(self, k, c):
        return self.part.at[pl.ds(pl.multiple_of(self.me.slot(k, c) * T, T), T)]

    def push(self, n, src, dst, device):
        copy = remote(src, dst, self.send.at[n], self.recv.at[n], device)
        copy.start()
        self.sent.append(copy)

    def arrived(self, n, dst):
        remote(dst, dst, self.send.at[n], self.recv.at[n], self.me.sibling()).wait_recv()

    def start(self):
        me = self.me
        for k in (2, 1, 3, 0):
            self.push(k, self.piece(k, 1 - me.c), self.other.at[k], me.sibling())

    def join(self):
        me = self.me
        a, b = pl.ds(0, HALF), pl.ds(HALF, HALF)
        right, left = me.z_peer(1), me.z_peer(3)
        for k in (2, 1, 3, 0):
            self.arrived(k, self.other.at[k])
            add_rows(
                self.pair.at[k], 0, [reads(self.piece(k, me.c)), reads(self.other.at[k])], T
            )
            if k == 2:
                self.push(4, self.pair.at[2, a], self.through.at[0], right)
                self.push(5, self.pair.at[2, b], self.through.at[1], left)
            if k == 1:
                self.push(6, self.pair.at[1, b], self.final.at[0], right)
            if k == 3:
                self.push(7, self.pair.at[3, a], self.final.at[1], left)

    def relay(self):
        me = self.me
        right, left = me.z_peer(1), me.z_peer(3)
        self.arrived(4, self.through.at[0])
        add_rows(self.passed.at[0], 0, [reads(self.through.at[0]), reads(self.pair.at[1])], HALF)
        self.push(8, self.passed.at[0], self.final.at[2], right)
        self.arrived(5, self.through.at[1])
        add_rows(self.passed.at[1], 0, [reads(self.through.at[1]), reads(self.pair.at[3], HALF)], HALF)
        self.push(9, self.passed.at[1], self.final.at[3], left)

    def finish(self, out, extra=None):
        for n, k in ((6, 0), (7, 1), (8, 2), (9, 3)):
            self.arrived(n, self.final.at[k])
        more = [] if extra is None else [reads(extra)]
        add_rows(
            out, 0, [reads(self.pair.at[0]), reads(self.final.at[1]), reads(self.final.at[2])] + more, HALF
        )
        more = [] if extra is None else [reads(extra, HALF)]
        add_rows(
            out,
            HALF,
            [reads(self.pair.at[0], HALF), reads(self.final.at[0]), reads(self.final.at[3])] + more,
            HALF,
        )
        for copy in self.sent:
            copy.wait_send()


def norm_rows(value, gain):
    return value * lax.rsqrt(jnp.mean(value * value, axis=-1, keepdims=True) + epsilon) * gain


def norm_pull(value, gain, incoming):
    r = lax.rsqrt(jnp.mean(value * value, axis=-1, keepdims=True) + epsilon)
    scaled = incoming * gain
    inner = jnp.mean(value * scaled, axis=-1, keepdims=True)
    normed = value * r
    return r * (scaled - normed * (inner * r)), incoming * normed


def turn_kernel(part, middle, cot, gain, adj_middle, gain_grad, adj_all, adj, *rest):
    scatter, gathering = rest[:7], rest[7:]
    me = Place()
    mine = pl.multiple_of(me.sq * T, T)
    own = gathering[0]
    barrier, count = greet(z_peers(me))
    pl.semaphore_wait(barrier, count)
    total = Scatter(me, part, *scatter)
    total.start()
    total.join()
    total.relay()
    total.finish(adj)

    def body(i, carry):
        here = pl.ds(pl.multiple_of(i * 16, 16), 16)
        pulled, terms = norm_pull(middle[here], gain[...], adj[here])
        value = cot[here].astype(f32) + pulled
        adj_middle[here] = value
        own[pl.ds(pl.multiple_of(mine + i * 16, 16), 16)] = value.astype(bf16)
        return carry + jnp.sum(terms, axis=0, keepdims=True)

    gain_grad[...] = lax.fori_loop(0, T // 16, body, jnp.zeros((1, D), f32))
    gather = Gather(me, own, adj_all, *gathering)
    gather.start()
    gather.forward()
    gather.across()
    gather.finish()


def turn_call(part, middle, cot, gain):
    sds = jax.ShapeDtypeStruct
    hbm, vmem = pl.BlockSpec(memory_space=ANY), pl.BlockSpec(memory_space=VMEM)
    return pl.pallas_call(
        turn_kernel,
        out_shape=(sds((T, D), f32), sds((1, D), f32), sds((G, D), bf16)),
        in_specs=[vmem] * 4,
        out_specs=[vmem, vmem, hbm],
        scratch_shapes=[VMEM((T, D), f32)] + Scatter.scratch(D) + Gather.scratch(D),
        compiler_params=pltpu.CompilerParams(collective_id=3, has_side_effects=True, vmem_limit_bytes=62 << 20),
        cost_estimate=pl.CostEstimate(flops=1000, bytes_accessed=100 << 20, transcendentals=0),
        name="turn",
    )(part, middle, cot, gain)


def close_kernel(
    part, feed_part, normed_in, both_in, adj_in, mixed_in, eg, sums, tok, adj_middle, middle, gain, gain_two,
    in_grad, act, mix_out, gate_out, chan_out, gain_out,
    normed, both, adj_out, mixed, mg, adj, r1, s1, r2, last, e_in, sums_in, gate_sum, chan_sum, gp, gp_in, gain_sum, gain_in, *rest,
):
    one, two = rest[:7], rest[7:14]
    m1s, m1r, m2s, m2r, m3s, m3r, es, er, us, ur, gs, gr, hs, hr, qs, qr, ls, ws = rest[14:]
    me = Place()
    loads = [
        pltpu.make_async_copy(src, dst, ws.at[n])
        for n, (src, dst) in enumerate(
            ((normed_in, normed), (both_in, both), (adj_in, adj_out), (mixed_in, mixed))
        )
    ]
    for copy in loads:
        copy.start()
    quarter, at = me.dp // 8, me.dp % 8
    gate_to = (8 * quarter + me.sq, at)
    gate_self = me.sq == at
    chan_from = (8 * (me.dp % 2) + me.sq, me.dp // 2)
    chan_to = (2 * me.sq + me.dp // 8, me.dp % 8)
    chan_self = jnp.logical_and(chan_from[0] == me.dp, chan_from[1] == me.sq)
    barrier, count = greet(seq_peers(me) + dp_peers(me))

    @pl.when(jnp.logical_not(gate_self))
    def _():
        pl.semaphore_signal(barrier, inc=1, device_id=gate_to, device_id_type=MESH)

    @pl.when(jnp.logical_not(chan_self))
    def _():
        pl.semaphore_signal(barrier, inc=1, device_id=chan_from, device_id_type=MESH)

    pl.semaphore_wait(barrier, count + jnp.where(gate_self, 0, 1) + jnp.where(chan_self, 0, 1))

    sent = []

    def push(src, dst, send, recv, device):
        sent.append(remote(src, dst, send, recv, device))
        sent[-1].start()

    def arrived(dst, send, recv):
        remote(dst, dst, send, recv, me.sibling()).wait_recv()

    lo, hi = pl.ds(0, 4), pl.ds(4, 4)
    inner = Scatter(me, part, *one)
    outer = Scatter(me, feed_part, *two)
    inner.start()
    for k in range(1, DP):
        to = (me.dp + k) % DP
        push(eg.at[to], e_in.at[k], es.at[k], er.at[k], me.dp_peer(to))
        push(sums, sums_in.at[k], us.at[k], ur.at[k], me.dp_peer(to))
    inner.join()
    for copy in loads:
        copy.wait()

    def tile(i, carry):
        here = pl.ds(pl.multiple_of(i * 256, 256), 256)
        left = tn(normed[:, here], both[...]).astype(bf16)
        right = tn(adj_out[:, here], mixed[...]).astype(bf16)
        for h in range(2):
            for n in range(SEQ):
                rows = slice(h * T + n * 16, h * T + (n + 1) * 16)
                mg[i // 2, i % 2 * 2 + h, n, :, : 2 * WP] = left[rows]
                mg[i // 2, i % 2 * 2 + h, n, :, 2 * WP :] = right[rows]
        return carry

    lax.fori_loop(0, 8, tile, 0)
    for k in (2, 1, 3):
        push(mg.at[:, (me.y + k) % 4, lo], r1.at[0, k - 1], m1s.at[k], m1r.at[k], me.dp_peer(me.y_dp(k)))
        push(mg.at[(me.x + k) % 4, :, hi], r1.at[1, k - 1], m1s.at[4 + k], m1r.at[4 + k], me.dp_peer(me.x_dp(k)))
    outer.start()
    inner.relay()
    outer.join()
    inner.finish(adj)

    def pull(i, carry):
        here = pl.ds(pl.multiple_of(i * 16, 16), 16)
        pulled, terms = norm_pull(tok[here].astype(f32), gain[...], adj[here])
        in_grad[here] = adj_middle[here] + pulled
        return carry + jnp.sum(terms, axis=0, keepdims=True)

    gain_one = lax.fori_loop(0, T // 16, pull, jnp.zeros((1, D), f32))
    gp[...] = jnp.zeros(gp.shape, f32)
    for k in range(DP):
        gp[k, 0:1] = gain_one[:, k * 128 : (k + 1) * 128]
        gp[k, 1:2] = gain_two[:, k * 128 : (k + 1) * 128]
    for k in range(1, DP):
        to = (me.dp + k) % DP
        push(gp.at[to], gp_in.at[k], gs.at[k], gr.at[k], me.dp_peer(to))
    outer.relay()

    for k in range(1, DP):
        arrived(e_in.at[k], es.at[k], er.at[k])
        arrived(sums_in.at[k], us.at[k], ur.at[k])

    def add_gates(i, carry):
        here = pl.ds(pl.multiple_of(i * 16, 16), 16)

        def step(k, total):
            return total + e_in[k, here].astype(f32)

        gate_sum[here] = lax.fori_loop(1, DP, step, eg[me.dp, here].astype(f32))
        return carry

    lax.fori_loop(0, 3, add_gates, 0)

    def add_sums(k, total):
        return total + sums_in[k]

    chan_sum[...] = lax.fori_loop(1, DP, add_sums, sums[...])
    gate_copy = remote(gate_sum, gate_out, hs.at[0], hr.at[0], gate_to)
    chan_copy = remote(chan_sum, chan_out, hs.at[1], hr.at[1], chan_to)
    gate_local = pltpu.make_async_copy(gate_sum, gate_out, ls.at[0])
    chan_local = pltpu.make_async_copy(chan_sum, chan_out, ls.at[1])

    @pl.when(jnp.logical_not(gate_self))
    def _():
        gate_copy.start()

    @pl.when(gate_self)
    def _():
        gate_local.start()

    @pl.when(jnp.logical_not(chan_self))
    def _():
        chan_copy.start()

    @pl.when(chan_self)
    def _():
        chan_local.start()

    for k in (1, 3, 2):
        arrived(r1.at[0, k - 1], m1s.at[k], m1r.at[k])
        arrived(r1.at[1, k - 1], m1s.at[4 + k], m1r.at[4 + k])
    for j in (2, 1, 3, 0):

        def first(i, carry, j=j):
            xx, yy = (me.x + j) % 4, (me.y + j) % 4
            total = mg[xx, me.y, i].astype(f32)
            for k in range(3):
                total = total + r1[0, k, xx, i].astype(f32)
            s1[0, j, i] = total.astype(bf16)
            total = mg[me.x, yy, 4 + i].astype(f32)
            for k in range(3):
                total = total + r1[1, k, yy, i].astype(f32)
            s1[1, j, i] = total.astype(bf16)
            return carry

        lax.fori_loop(0, 4, first, 0)
        if j:
            push(s1.at[0, j], r2.at[0, j - 1], m2s.at[j], m2r.at[j], me.dp_peer(me.x_dp(j)))
            push(s1.at[1, j], r2.at[1, j - 1], m2s.at[4 + j], m2r.at[4 + j], me.dp_peer(me.y_dp(j)))

    for k in range(1, DP):
        arrived(gp_in.at[k], gs.at[k], gr.at[k])

    def gains(k, total):
        return total + gp_in[k]

    gain_sum[...] = lax.fori_loop(1, DP, gains, gp[me.dp])
    for k in range(1, SEQ):
        push(gain_sum, gain_in.at[k], qs.at[k], qr.at[k], me.seq_peer(k))

    outer.finish(adj, middle)

    def lower(i, carry):
        here = pl.ds(pl.multiple_of(i * 16, 16), 16)
        act[here] = adj[here].astype(bf16)
        return carry

    lax.fori_loop(0, T // 16, lower, 0)

    for j in (1, 3, 2):
        arrived(r2.at[0, j - 1], m2s.at[j], m2r.at[j])
        arrived(r2.at[1, j - 1], m2s.at[4 + j], m2r.at[4 + j])

    def second(i, carry):
        for h in range(2):
            total = s1[h, 0, i].astype(f32)
            for k in range(3):
                total = total + r2[h, k, i].astype(f32)
            last[4 * h + i] = total.astype(bf16)
        return carry

    lax.fori_loop(0, 4, second, 0)
    keep = pltpu.make_async_copy(last.at[me.sq], mix_out.at[me.sq], ls.at[2])
    keep.start()
    for k in (4, 3, 5, 2, 6, 1, 7):
        to = (me.sq + k) % SEQ
        push(last.at[to], mix_out.at[me.sq], m3s.at[k], m3r.at[k], me.seq_peer(k))
    for k in range(1, SEQ):
        arrived(gain_in.at[k], qs.at[k], qr.at[k])
    total = gain_sum[...]
    for k in range(1, SEQ):
        total = total + gain_in[k]
    gain_out[...] = total

    @pl.when(jnp.logical_not(gate_self))
    def _():
        gate_copy.wait()

    @pl.when(gate_self)
    def _():
        gate_local.wait()

    @pl.when(jnp.logical_not(chan_self))
    def _():
        chan_copy.wait()

    @pl.when(chan_self)
    def _():
        chan_local.wait()

    for k in range(1, SEQ):
        arrived(mix_out.at[(me.sq - k + SEQ) % SEQ], m3s.at[k], m3r.at[k])
    keep.wait()
    for copy in sent:
        copy.wait_send()


def close_call(part, feed_part, normed, both, adj_out, mixed, eg, sums, tok, adj_middle, middle, gain, gain_two):
    sds = jax.ShapeDtypeStruct
    vmem = pl.BlockSpec(memory_space=VMEM)
    return pl.pallas_call(
        close_kernel,
        out_shape=(
            sds((T, D), f32), sds((T, D), bf16), sds((SEQ, 16, MW), bf16),
            sds((48, WP), f32), sds((8, WP), f32), sds((8, 128), f32),
        ),
        in_specs=[vmem] * 2 + [pl.BlockSpec(memory_space=ANY)] * 4 + [vmem] * 7,
        out_specs=[vmem] * 6,
        scratch_shapes=[
            VMEM((G, D), bf16), VMEM((G, 2 * WP), bf16), VMEM((G, D), bf16), VMEM((G, WP), bf16),
            VMEM((4, 4, SEQ, 16, MW), bf16),
            VMEM((T, D), f32),
            VMEM((2, 3, 4, 4, 16, MW), bf16), VMEM((2, 4, 4, 16, MW), bf16), VMEM((2, 3, 4, 16, MW), bf16),
            VMEM((SEQ, 16, MW), bf16), VMEM((DP, 48, WP), bf16), VMEM((DP, 8, WP), f32), VMEM((48, WP), f32),
            VMEM((8, WP), f32), VMEM((DP, 8, 128), f32), VMEM((DP, 8, 128), f32),
            VMEM((8, 128), f32), VMEM((SEQ, 8, 128), f32),
        ]
        + Scatter.scratch(D)
        + Scatter.scratch(D)
        + [
            DMA((8,)), DMA((8,)), DMA((8,)), DMA((8,)), DMA((8,)), DMA((8,)),
            DMA((DP,)), DMA((DP,)), DMA((DP,)), DMA((DP,)), DMA((DP,)), DMA((DP,)), DMA((2,)), DMA((2,)),
            DMA((SEQ,)), DMA((SEQ,)), DMA((3,)), DMA((4,)),
        ],
        compiler_params=pltpu.CompilerParams(collective_id=4, has_side_effects=True, vmem_limit_bytes=62 << 20),
        cost_estimate=pl.CostEstimate(flops=1000, bytes_accessed=100 << 20, transcendentals=0),
        name="close",
    )(part, feed_part, normed, both, adj_out, mixed, eg, sums, tok, adj_middle, middle, gain, gain_two)


def swap_kernel(src, dst, ss, sr, ls):
    me = Place()
    barrier, count = greet(seq_peers(me))
    keep = pltpu.make_async_copy(src.at[me.sq], dst.at[me.sq], ls.at[0])
    keep.start()
    pl.semaphore_wait(barrier, count)
    sent = []
    for k in (4, 3, 5, 2, 6, 1, 7):
        to = (me.sq + k) % SEQ
        sent.append(remote(src.at[to], dst.at[me.sq], ss.at[k], sr.at[k], me.seq_peer(k)))
        sent[-1].start()
    for k in range(1, SEQ):
        source = (me.sq - k + SEQ) % SEQ
        remote(dst.at[source], dst.at[source], ss.at[k], sr.at[k], me.sibling()).wait_recv()
    keep.wait()
    for copy in sent:
        copy.wait_send()


def swap_call(src, number, name):
    hbm = pl.BlockSpec(memory_space=ANY)
    return pl.pallas_call(
        swap_kernel,
        out_shape=jax.ShapeDtypeStruct(src.shape, src.dtype),
        in_specs=[hbm],
        out_specs=hbm,
        scratch_shapes=[DMA((SEQ,)), DMA((SEQ,)), DMA((1,))],
        compiler_params=pltpu.CompilerParams(collective_id=number, has_side_effects=True, vmem_limit_bytes=62 << 20),
        cost_estimate=pl.CostEstimate(flops=1000, bytes_accessed=1 << 20, transcendentals=0),
        name=name,
    )(src)


CHUNK = 256
STEPS = G // CHUNK
contract_last = (((1,), (1,)), ((), ()))
contract_first = (((0,), (0,)), ((), ()))
gelu_c = 0.7978845608028654
gelu_k = 0.044715


def gelu_parts(v):
    square = v * v
    t = jnp.tanh(gelu_c * (v + gelu_k * square * v))
    half = 0.5 * (1.0 + t)
    slope = half + 0.5 * v * (1.0 - t * t) * (gelu_c * (1.0 + 3.0 * gelu_k * square))
    return v * half, slope


def minus_expm1(z):
    series = -z * (1.0 + z * (1 / 2 + z * (1 / 6 + z * (1 / 24 + z * (1 / 120 + z * (1 / 720))))))
    return jnp.where(z > -0.25, series, 1.0 - jnp.exp(z))


def recur(conv, raw_a, raw_x, terms, start):
    recall = jax.nn.sigmoid(raw_a + terms[5:6])
    admit = jax.nn.sigmoid(raw_x + terms[6:7])
    lograte = terms[7:8] * recall
    decay = jnp.exp(lograte) * (1.0 - start)
    root = jnp.sqrt(minus_expm1(2.0 * lograte))
    scale = start + (1.0 - start) * root
    return recall, admit, lograte, decay, root, scale


def nt(left, right):
    return lax.dot_general(left, right, contract_last, preferred_element_type=f32)


def tn(left, right):
    return lax.dot_general(left, right, contract_first, preferred_element_type=f32)


def nn(left, right):
    return jnp.dot(left, right, preferred_element_type=f32)


def rows_spec(width, back=False):
    if back:
        return pl.BlockSpec((CHUNK, width), lambda i: (STEPS - 1 - i, 0))
    return pl.BlockSpec((CHUNK, width), lambda i: (i, 0))


def whole(shape):
    return pl.BlockSpec(shape, lambda i: (0,) * len(shape))


def rows_of(base, size):
    return pl.ds(pl.multiple_of(base, 16), size)


def lanes_of(base, size):
    return pl.ds(pl.multiple_of(base, 128), size)


def windows(lab, base):
    return lab[pl.ds(pl.multiple_of(base, 8), CHUNK + 16)]


def same(window, k):
    here = window[8 : 8 + CHUNK, 0:1]
    there = window[8 - k : 8 - k + CHUNK, 0:1]
    return (here == there).astype(f32)


def forward_kernel(
    tok, cot, mix, feed, small, gates, chan,
    cot_out, mix_out, normed_out, x_out, y_out, conv_out, prior_out, mixed_out,
    hidden_out, gu_out, back_out, ff_out, n2_out, gate_out, term_out, gain_out, lab_out, middle,
    mixw, feedw, part, xs, ys, convs, priors, mixeds, hiddens, gus,
    small_in, minor, gate_f,
    xpad, dec, drv, sts, carry, *rest,
):
    tg, cg, ng, sc = rest[:4], rest[4:8], rest[8:12], rest[12:19]
    ms, mr, fs, fr, ss, sr, ps, pr, qs, qr, es, er, hs, hr, ls, os = rest[19:]
    me = Place()
    quarter, at = me.dp // 8, me.dp % 8
    gate_to = (8 * quarter + me.sq, at)
    gate_self = me.sq == at
    chan_to = (8 * (me.dp % 2) + me.sq, me.dp // 2)
    chan_from = (2 * me.sq + me.dp // 8, me.dp % 8)
    chan_self = jnp.logical_and(chan_to[0] == me.dp, chan_to[1] == me.sq)
    barrier, count = greet(seq_peers(me) + ring_peers(me))

    @pl.when(jnp.logical_not(gate_self))
    def _():
        pl.semaphore_signal(barrier, inc=1, device_id=gate_to, device_id_type=MESH)

    @pl.when(jnp.logical_not(chan_self))
    def _():
        pl.semaphore_signal(barrier, inc=1, device_id=chan_from, device_id_type=MESH)

    tokg, cotg, n2g = tg[0], cg[0], ng[0]
    own_rows = rows_of(me.dp * T + me.sq * 16, 16)

    def feed_columns(p, j):
        return lanes_of(p * FF + j * FL, FL)

    local = [
        pltpu.make_async_copy(tok, tokg.at[rows_of(me.sq * T, T)], ls.at[0]),
        pltpu.make_async_copy(cot, cotg.at[rows_of(me.sq * T, T)], ls.at[1]),
        pltpu.make_async_copy(mix.at[me.sq], mixw.at[own_rows], ls.at[2]),
        pltpu.make_async_copy(small, small_in.at[me.sq], ls.at[3]),
    ] + [
        pltpu.make_async_copy(feed.at[:, feed_columns(p, me.sq)], feedw.at[own_rows, pl.ds(p * FL, FL)], ls.at[4 + p])
        for p in range(3)
    ]
    for copy in local:
        copy.start()

    pl.semaphore_wait(barrier, count + jnp.where(gate_self, 0, 1) + jnp.where(chan_self, 0, 1))

    sent = []

    def push(src, dst, send, recv, device):
        sent.append(remote(src, dst, send, recv, device))
        sent[-1].start()

    def arrived(dst, send, recv):
        remote(dst, dst, send, recv, me.sibling()).wait_recv()

    order = (4, 3, 5, 2, 6, 1, 7)
    for k in order:
        to = (me.sq + k) % SEQ
        push(mix.at[to], mixw.at[own_rows], ms.at[k], mr.at[k], me.seq_peer(k))
        push(small, small_in.at[me.sq], ss.at[k], sr.at[k], me.seq_peer(k))

    def minor_rows(dp, start, size):
        return minor.at[rows_of(dp * MINOR + start, size)]

    gate_copy = remote(gates, minor_rows(gate_to[0], 16, 96), hs.at[0], hr.at[0], gate_to)
    chan_copy = remote(chan, minor_rows(chan_to[0], 112, 48), hs.at[1], hr.at[1], chan_to)
    gate_local = pltpu.make_async_copy(gates, minor_rows(me.dp, 16, 96), ls.at[7])
    chan_local = pltpu.make_async_copy(chan, minor_rows(me.dp, 112, 48), ls.at[8])
    gate_here = remote(gates, minor_rows(me.dp, 16, 96), hs.at[0], hr.at[0], gate_to)
    chan_here = remote(chan, minor_rows(me.dp, 112, 48), hs.at[1], hr.at[1], chan_to)

    @pl.when(jnp.logical_not(gate_self))
    def _():
        gate_copy.start()

    @pl.when(gate_self)
    def _():
        gate_local.start()

    @pl.when(jnp.logical_not(chan_self))
    def _():
        chan_copy.start()

    @pl.when(chan_self)
    def _():
        chan_local.start()

    local[0].wait()
    tokens = Gather(me, None, None, *tg)
    tokens.start()
    for k in order:
        to = (me.sq + k) % SEQ
        for p in range(3):
            push(feed.at[:, feed_columns(p, to)], feedw.at[own_rows, pl.ds(p * FL, FL)],
                 fs.at[p, k], fr.at[p, k], me.seq_peer(k))
    for copy in local[1:]:
        copy.wait()

    def seq_rows(k):
        return rows_of(me.dp * T + (me.sq - k + SEQ) % SEQ * 16, 16)

    for k in range(1, SEQ):
        arrived(mixw.at[seq_rows(k)], ms.at[k], mr.at[k])

    mixes = Spread(me, mixw, T, ps, pr)
    feeds = Spread(me, feedw, T, qs, qr)
    minors = Spread(me, minor, MINOR, es, er)
    mixes.start()

    for k in range(1, SEQ):
        arrived(small_in.at[(me.sq - k + SEQ) % SEQ], ss.at[k], sr.at[k])
    gain = small_in[0, 0:16].astype(f32)
    for k in range(1, SEQ):
        gain = gain + small_in[k, 0:16].astype(f32)
    minor[rows_of(me.dp * MINOR, 16)] = gain.astype(bf16)
    minor[rows_of(me.dp * MINOR + 160, 32)] = jnp.zeros((32, 128), bf16)

    @pl.when(jnp.logical_not(gate_self))
    def _():
        gate_copy.wait_send()
        gate_here.wait_recv()

    @pl.when(gate_self)
    def _():
        gate_local.wait()

    @pl.when(jnp.logical_not(chan_self))
    def _():
        chan_copy.wait_send()
        chan_here.wait_recv()

    @pl.when(chan_self)
    def _():
        chan_local.wait()

    minors.start()
    tokens.forward()
    mixes.turn()
    minors.turn()
    cots = Gather(me, None, cot_out, *cg)
    cots.start()
    mixes.far()
    minors.far()

    lab_out[0:8] = jnp.full((8, 128), -1.0, f32)
    lab_out[G + 8 :] = jnp.full((8, 128), -2.0, f32)
    for k in range(SEQ):
        row = small_in[k, 16:32].astype(f32)[0:1]
        lab_out[8 + k * T : 8 + (k + 1) * T] = jnp.broadcast_to(row, (128, 128)).T

    tokens.across()
    for t in range(3):
        mixes.hand_on(t)
        minors.hand_on(t)
    minors.hand_on(3)
    mixes.hand_on(3)
    for k in range(1, SEQ):
        for p in range(3):
            arrived(feedw.at[seq_rows(k), pl.ds(p * FL, FL)], fs.at[p, k], fr.at[p, k])
    feeds.start()
    tokens.finish()
    minors.finish()
    terms = minor[112:160].astype(f32)
    for k in range(1, DP):
        terms = terms + minor[k * MINOR + 112 : k * MINOR + 160].astype(f32)
    for n in range(3):
        group = terms[16 * n : 16 * n + 16]
        lanes = slice(128 * n, 128 * n + 128)
        lane = lax.broadcasted_iota(jnp.int32, (1, 128), 1) + 128 * n
        term_out[:, lanes] = group
        term_out[7:8, lanes] = jnp.where(lane >= WL, -1.0, group[7:8] + group[9:10])
        term_out[8:9, lanes] = group[8:9] + group[10:11]
    gate_f[...] = jnp.zeros(gate_f.shape, f32)
    for k in range(DP):
        gain_out[:, k * 128 : (k + 1) * 128] = minor[k * MINOR : k * MINOR + 16].astype(f32)[0:8]
        base = k // 8 * WP + k % 8 * 40
        for n in range(2):
            lanes = k % 8 // 4 * 128 + n * 128
            start = k * MINOR + 16 + 48 * n
            gate_f[base : base + 40, lanes : lanes + 128] = minor[start : start + 48].astype(f32)[0:40]
    gate_out[0] = gate_f[:WP].astype(bf16)
    gate_out[1] = gate_f[WP:].astype(bf16)

    def normalise(i, c):
        here = pl.ds(pl.multiple_of(i * 16, 16), 16)
        tokg[here] = norm_rows(tokg[here].astype(f32), gain_out[0:1]).astype(bf16)
        return c

    lax.fori_loop(0, G // 16, normalise, 0)
    writes = [pltpu.make_async_copy(tokg, normed_out, os.at[0])]
    writes[0].start()
    cots.forward()
    cots.across()
    mixes.finish()
    writes.append(pltpu.make_async_copy(mixw, mix_out, os.at[1]))
    writes[1].start()

    xpad[0:8] = jnp.zeros((8, WP), f32)
    carry[...] = jnp.zeros((8, WP), f32)
    row = lax.broadcasted_iota(jnp.int32, (8, WP), 0)

    def mix_chunk(step, c):
        @pl.when(step == 1)
        def _():
            feeds.turn()

        @pl.when(step == 2)
        def _():
            feeds.far()

        @pl.when(step == 3)
        def _():
            feeds.hand_on(0)

        base = step * CHUNK
        rows = rows_of(base, CHUNK)
        both = nn(tokg[rows], mixw[:, : 2 * WP])
        x, y = both[:, :WP], both[:, WP:]
        xs[rows] = x
        ys[rows] = y
        xpad[8:] = x
        terms = term_out[...]
        window = windows(lab_out, base)
        start = 1.0 - same(window, 1)
        conv = terms[4:5] + terms[0:1] * x
        for k in range(1, CONV):
            conv = conv + terms[k : k + 1] * (same(window, k) * xpad[8 - k : 8 - k + CHUNK])
        xpad[0:8] = x[CHUNK - 8 :]
        convs[rows] = conv
        lowered = conv.astype(bf16)
        raw_a, raw_x = nn(lowered, gate_out[0]), nn(lowered, gate_out[1])
        recall, admit, lograte, decay, root, scale = recur(conv, raw_a, raw_x, terms, start)
        dec[...] = decay
        drv[...] = scale * admit * conv

        def scan(i, before):
            here = pl.ds(pl.multiple_of(i * 8, 8), 8)
            a, b = dec[here], drv[here]
            for s in (1, 2, 4):
                b = b + a * jnp.where(row >= s, pltpu.roll(b, s, 0), 0.0)
                a = a * jnp.where(row >= s, pltpu.roll(a, s, 0), 1.0)
            state = b + a * before
            sts[here] = state
            priors[pl.ds(pl.multiple_of(base + i * 8, 8), 8)] = jnp.where(row >= 1, pltpu.roll(state, 1, 0), before)
            return jnp.broadcast_to(state[7:8], (8, WP))

        carry[...] = lax.fori_loop(0, CHUNK // 8, scan, carry[...], unroll=4)
        value, _ = gelu_parts(ys[rows])
        mixed = (value * sts[...]).astype(bf16)
        mixeds[rows] = mixed
        part[rows] = nt(mixed, mixw[:, 2 * WP :]).astype(bf16)
        return c

    lax.fori_loop(0, STEPS, mix_chunk, 0)

    total = Scatter(me, part, *sc)
    total.start()
    for n, (src, dst) in enumerate(((xs, x_out), (ys, y_out), (convs, conv_out), (priors, prior_out), (mixeds, mixed_out))):
        writes.append(pltpu.make_async_copy(src, dst, os.at[2 + n]))
        writes[-1].start()
    total.join()
    feeds.hand_on(1)
    feeds.hand_on(2)
    total.relay()
    feeds.hand_on(3)
    total.finish(middle, tok)

    def second_norm(i, c):
        here = pl.ds(pl.multiple_of(i * 16, 16), 16)
        n2g[rows_of(me.sq * T + i * 16, 16)] = norm_rows(middle[here], gain_out[1:2]).astype(bf16)
        return c

    lax.fori_loop(0, T // 16, second_norm, 0)
    seconds = Gather(me, None, n2_out, *ng)
    seconds.start()
    cots.finish()
    writes[0].wait()
    feeds.finish()

    def feed_chunk(k, n):
        rows = rows_of(me.chip(k) * CHUNK, CHUNK)
        gu = nn(n2g[rows], feedw[:, : 2 * FL])
        gate, up = gu[:, :FL], gu[:, FL:]
        adj_hidden = nn(cotg[rows], feedw[:, 2 * FL :])
        value, slope = gelu_parts(gate)
        hidden = (value * up).astype(bf16)
        hiddens[rows] = hidden
        gus[rows, :FL] = (adj_hidden * up * slope).astype(bf16)
        gus[rows, FL:] = (adj_hidden * value).astype(bf16)
        tokg[rows] = nt(hidden, feedw[:, 2 * FL :]).astype(bf16)
        part[rows] = nt(gus[rows], feedw[:, : 2 * FL]).astype(bf16)

    def feed_store(k, n):
        rows = rows_of(me.chip(k) * CHUNK, CHUNK)
        for m, (src, dst) in enumerate(((hiddens, hidden_out), (gus, gu_out), (tokg, ff_out), (part, back_out))):
            writes.append(pltpu.make_async_copy(src.at[rows], dst.at[rows], os.at[7 + 4 * n + m]))
            writes[-1].start()

    seconds.own_pair()
    feed_chunk(0, 0)
    feed_store(0, 0)
    seconds.forward()
    seconds.across_left()
    seconds.across_right()
    seconds.left_pair()
    feed_chunk(3, 1)
    feed_store(3, 1)
    seconds.across_far()
    seconds.right_pair()
    feed_chunk(1, 2)
    feed_store(1, 2)
    seconds.far_pair()
    feed_chunk(2, 3)
    feed_store(2, 3)
    seconds.drain()
    for copy in writes[1:]:
        copy.wait()
    for copy in sent:
        copy.wait_send()
    mixes.drain()
    minors.drain()
    feeds.drain()


def forward_call(tok, cot, mix, feed, small, gates, chan):
    sds = jax.ShapeDtypeStruct
    hbm, vmem = pl.BlockSpec(memory_space=ANY), pl.BlockSpec(memory_space=VMEM)
    return pl.pallas_call(
        forward_kernel,
        out_shape=(
            sds((G, D), bf16), sds((D, MW), bf16), sds((G, D), bf16),
            sds((G, WP), f32), sds((G, WP), f32), sds((G, WP), f32), sds((G, WP), f32), sds((G, WP), bf16),
            sds((G, FL), bf16), sds((G, 2 * FL), bf16), sds((G, D), bf16), sds((G, D), bf16), sds((G, D), bf16),
            sds((2, WP, WP), bf16), sds((16, WP), f32), sds((8, D), f32), sds((G + 16, 128), f32), sds((T, D), f32),
        ),
        in_specs=[vmem, hbm, hbm, hbm, vmem, vmem, vmem],
        out_specs=[hbm] * 13 + [vmem] * 5,
        scratch_shapes=[
            VMEM((D, MW), bf16), VMEM((D, FW), bf16), VMEM((G, D), bf16),
            VMEM((G, WP), f32), VMEM((G, WP), f32), VMEM((G, WP), f32), VMEM((G, WP), f32), VMEM((G, WP), bf16),
            VMEM((G, FL), bf16), VMEM((G, 2 * FL), bf16),
            VMEM((SEQ, 32, 128), bf16), VMEM((DP * MINOR, 128), bf16), VMEM((2 * WP, WP), f32),
            VMEM((CHUNK + 8, WP), f32), VMEM((CHUNK, WP), f32), VMEM((CHUNK, WP), f32), VMEM((CHUNK, WP), f32),
            VMEM((8, WP), f32),
            *Gather.scratch(D), *Gather.scratch(D), *Gather.scratch(D), *Scatter.scratch(D),
            DMA((SEQ,)), DMA((SEQ,)), DMA((3, SEQ)), DMA((3, SEQ)), DMA((SEQ,)), DMA((SEQ,)),
            DMA((40,)), DMA((40,)), DMA((40,)), DMA((40,)), DMA((40,)), DMA((40,)),
            DMA((2,)), DMA((2,)), DMA((9,)), DMA((23,)),
        ],
        compiler_params=pltpu.CompilerParams(collective_id=1, has_side_effects=True, vmem_limit_bytes=63 << 20),
        cost_estimate=pl.CostEstimate(flops=30 * G * D * WP, bytes_accessed=100 << 20, transcendentals=0),
        name="forward",
    )(tok, cot, mix, feed, small, gates, chan)


def unmix_kernel(
    adj_out, w, gates, terms_ref, lab, x_in, y_in, conv_in, prior_in,
    both, part, gate_out, sums,
    dec, adj, acp, carry, gate_grad,
):
    step = pl.program_id(0)
    window = windows(lab, (STEPS - 1 - step) * CHUNK)

    @pl.when(step == 0)
    def _():
        dec[CHUNK:] = jnp.zeros((8, WP), f32)
        acp[CHUNK:] = jnp.zeros((8, WP), f32)
        carry[...] = jnp.zeros((8, WP), f32)
        gate_grad[...] = jnp.zeros(gate_grad.shape, f32)
        sums[...] = jnp.zeros(sums.shape, f32)

    @pl.when(step > 0)
    def _():
        dec[CHUNK:] = dec[0:8]
        acp[CHUNK:] = acp[0:8]

    terms = terms_ref[...]
    start = 1.0 - same(window, 1)
    conv, prior = conv_in[...], prior_in[...]
    lowered = conv.astype(bf16)
    raw_a, raw_x = nn(lowered, gates[0]), nn(lowered, gates[1])
    recall, admit, lograte, decay, root, scale = recur(conv, raw_a, raw_x, terms, start)
    dec[0:CHUNK] = decay
    states = decay * prior + scale * admit * conv
    adj_mixed = nn(adj_out[...], w[:, 2 * WP :])
    value, slope = gelu_parts(y_in[...])
    adj[...] = adj_mixed * value
    both[:, WP:] = (adj_mixed * states * slope).astype(bf16)
    row = lax.broadcasted_iota(jnp.int32, (8, WP), 0)

    def scan(i, after):
        at = pl.multiple_of((CHUNK // 8 - 1 - i) * 8, 8)
        here = pl.ds(at, 8)
        later = dec[pl.ds(pl.multiple_of(at + 8, 8), 8)]
        a = jnp.where(row < 7, pltpu.roll(dec[here], 7, 0), later[0:1])
        b = adj[here]
        for s in (1, 2, 4):
            b = b + a * jnp.where(row < 8 - s, pltpu.roll(b, 8 - s, 0), 0.0)
            a = a * jnp.where(row < 8 - s, pltpu.roll(a, 8 - s, 0), 1.0)
        value = b + a * after
        adj[here] = value
        return jnp.broadcast_to(value[0:1], (8, WP))

    carry[...] = lax.fori_loop(0, CHUNK // 8, scan, carry[...], unroll=4)
    adjoint = adj[...]
    flow = adjoint * admit * conv
    adj_lograte = adjoint * prior * decay - (1.0 - start) * flow * (jnp.exp(2.0 * lograte) / root)
    adj_ra = adj_lograte * terms[7:8] * (recall * (1.0 - recall))
    adj_rx = flow * scale * (1.0 - admit)

    def total(v):
        return jnp.sum(v, axis=0, keepdims=True)

    sums[5:6] += total(adj_ra)
    sums[6:7] += total(adj_rx)
    sums[7:8] += total(adj_lograte * recall) * terms[8:9]
    low_a, low_x = adj_ra.astype(bf16), adj_rx.astype(bf16)
    adj_conv = adjoint * scale * admit + nt(low_a, gates[0]) + nt(low_x, gates[1])
    gate_grad[0] += tn(lowered, low_a)
    gate_grad[1] += tn(lowered, low_x)
    acp[0:CHUNK] = adj_conv
    x = x_in[...]
    adj_x = terms[0:1] * adj_conv
    sums[4:5] += total(adj_conv)
    sums[0:1] += total(adj_conv * x)
    for k in range(1, CONV):
        moved = same(window, -k) * acp[k : k + CHUNK]
        adj_x = adj_x + terms[k : k + 1] * moved
        sums[k : k + 1] += total(moved * x)
    both[:, :WP] = adj_x.astype(bf16)
    part[...] = nt(both[...], w[:, : 2 * WP]).astype(bf16)

    @pl.when(step == STEPS - 1)
    def _():
        for k in range(DP):
            rows = gate_grad[k // 8, k % 8 * 40 : k % 8 * 40 + 40]
            gate_out[k] = jnp.concatenate([rows, jnp.zeros((8, WP), f32)], 0).astype(bf16)


def unmix_call(adj_out, w, gates, terms, lab, saved):
    sds = jax.ShapeDtypeStruct
    return pl.pallas_call(
        unmix_kernel,
        grid=(STEPS,),
        out_shape=(sds((G, 2 * WP), bf16), sds((G, D), bf16), sds((DP, 48, WP), bf16), sds((8, WP), f32)),
        in_specs=[
            rows_spec(D, True), whole((D, MW)), whole((2, WP, WP)), whole((16, WP)),
            whole((G + 16, 128)),
        ]
        + [rows_spec(WP, True)] * 4,
        out_specs=[rows_spec(2 * WP, True), rows_spec(D, True), whole((DP, 48, WP)), whole((8, WP))],
        scratch_shapes=[
            VMEM((CHUNK + 8, WP), f32), VMEM((CHUNK, WP), f32), VMEM((CHUNK + 8, WP), f32), VMEM((8, WP), f32),
            VMEM((2, WP, WP), f32),
        ],
        compiler_params=pltpu.CompilerParams(vmem_limit_bytes=62 << 20),
        cost_estimate=pl.CostEstimate(flops=2 * G * D * MW, bytes_accessed=30 << 20, transcendentals=0),
        name="unmix",
    )(adj_out, w, gates, terms, lab, *saved)


def grad_kernel(left, right, left_two, right_two, out):
    width = right.shape[1]
    out[:, :width] = tn(left[...], right[...]).astype(bf16)
    out[:, width:] = tn(left_two[...], right_two[...]).astype(bf16)


def grad_call(left, right, left_two, right_two, name):
    width = right.shape[1] + right_two.shape[1]
    block = 256
    return pl.pallas_call(
        grad_kernel,
        grid=(D // block,),
        out_shape=jax.ShapeDtypeStruct((D, width), bf16),
        in_specs=[
            pl.BlockSpec((G, block), lambda i: (0, i)), whole(right.shape),
            pl.BlockSpec((G, block), lambda i: (0, i)), whole(right_two.shape),
        ],
        out_specs=pl.BlockSpec((block, width), lambda i: (i, 0)),
        compiler_params=pltpu.CompilerParams(vmem_limit_bytes=62 << 20),
        cost_estimate=pl.CostEstimate(flops=2 * G * D * width, bytes_accessed=20 << 20, transcendentals=0),
        name=name,
    )(left, right, left_two, right_two)


def shards(tokens, segments, mixer_weights, norm_gains, gate_weights, channel_terms, feed_weights, cotangent):
    dp, sq = lax.axis_index("dp"), lax.axis_index("seq")
    mix = jnp.pad(mixer_weights.reshape(16, 3, SEQ, WL), ((0, 0), (0, 0), (0, 0), (0, WP - WL)))
    mix = mix.transpose(2, 0, 1, 3).reshape(SEQ, 16, MW)
    lane = lax.broadcasted_iota(jnp.int32, (2, 128), 1)
    gain_rows = jnp.where(lane // 16 == sq, jnp.tile(norm_gains.T, (1, SEQ)), jnp.zeros((), bf16))
    small = jnp.concatenate(
        [jnp.pad(gain_rows, ((0, 14), (0, 0))), jnp.pad(segments.astype(bf16)[None], ((0, 15), (0, 0)))], 0
    )
    gate_block = jnp.where(
        sq < 4,
        jnp.pad(gate_weights, ((0, 8), (0, 256 - BW))),
        jnp.pad(gate_weights, ((0, 8), (BW - 128, 2 * 128 - 2 * BW + 128))),
    )
    gate_block = jnp.concatenate([gate_block[:, :128], gate_block[:, 128:]], 0)
    channel = channel_terms.T.astype(f32)
    lam = channel[7:8]
    derived = jnp.concatenate([-rate_scale * jax.nn.softplus(-lam), rate_scale * jax.nn.sigmoid(-lam)], 0)
    coarse = lax.optimization_barrier(derived.astype(bf16)).astype(f32)
    columns = jnp.concatenate([channel[:7], coarse, derived - coarse], 0)
    piece = 8 * (dp % 2) + sq
    chan_block = lax.dynamic_update_slice(jnp.zeros((16, WP), f32), columns, (0, piece * 20)).astype(bf16)
    chan_block = jnp.concatenate([chan_block[:, n * 128 : n * 128 + 128] for n in range(3)], 0)
    (
        cot_all, w, normed, *saved, mixed, hidden, adj_gu, back_part, feed_part, norm_two,
        gates, terms, gains, lab, middle,
    ) = forward_call(tokens, cotangent, mix, feed_weights, small, gate_block, chan_block)
    feed_grad = grad_call(norm_two, adj_gu, cot_all, hidden, "feedgrad")
    feed_sum = lax.psum_scatter(feed_grad, "dp", scatter_dimension=0, tiled=True)
    adj_middle, gain_two, adj_all = turn_call(back_part, middle, cotangent, gains[1:2])
    both, in_part, gate_grad, sums = unmix_call(adj_all, w, gates, terms, lab, saved)
    input_gradient, activations, mix_out, gate_out, chan_out, gain_out = close_call(
        in_part, feed_part, normed, both, adj_all, mixed, gate_grad, sums, tokens,
        adj_middle, middle, gains[0:1], gain_two,
    )
    feed_out = swap_call(feed_sum.reshape(SEQ, 16, FW), 5, "swap")
    mixer_gradient = (
        mix_out.reshape(SEQ, 16, 3, WP)[..., :WL].transpose(1, 2, 0, 3).reshape(16, 3 * W).astype(f32)
    )
    feed_gradient = feed_out.reshape(SEQ, 16, 3, FL).transpose(1, 2, 0, 3).reshape(16, 3 * FF).astype(f32)
    gate_gradient = jnp.where(sq < 4, gate_out[:40, :BW], gate_out[:40, BW : 2 * BW])
    channel_gradient = lax.dynamic_slice(chan_out, (0, piece * 20), (8, 20)).T
    gain_gradient = lax.dynamic_slice(gain_out, (0, sq * 16), (2, 16)).T
    return (activations, input_gradient, mixer_gradient, gain_gradient, gate_gradient, channel_gradient, feed_gradient)


def solution(mesh):
    one = P(("dp", "seq"))
    two = P(("dp", "seq"), None)
    placed = (two, one, two, two, two, two, two, two)
    return jax.shard_map(shards, mesh=mesh, in_specs=placed, out_specs=(two,) * 7, check_vma=False)
```

```python
import functools

import jax
import jax.numpy as jnp
from jax import lax
from jax.experimental import pallas as pl
from jax.experimental.pallas import tpu as pltpu
from jax.sharding import PartitionSpec as P

D = 2048
W = 2560
FF = 6144
CONV = 4
BW = 160
SEQ = 8
DP = 16
T = 128
G = 1024
WL = W // SEQ
WP = 384
MW = 3 * WP
FL = FF // SEQ
FW = 3 * FL
HALF = T // 2
MINOR = 192

epsilon = 1e-06
rate_scale = 8.0
f32 = jnp.float32
bf16 = jnp.bfloat16
MESH = pl.DeviceIdType.MESH
ANY = pl.ANY
VMEM = pltpu.VMEM
DMA = pltpu.SemaphoreType.DMA


class Place:
    def __init__(self):
        self.dp = lax.axis_index("dp")
        self.sq = lax.axis_index("seq")
        self.x, self.y = self.dp // 4, self.dp % 4
        self.z, self.c = self.sq // 2, self.sq % 2

    def chip(self, k):
        return (self.z + k) % 4

    def slot(self, k, c):
        return 2 * self.chip(k) + c

    def z_peer(self, k):
        return (self.dp, 2 * self.chip(k) + self.c)

    def sibling(self):
        return (self.dp, 2 * self.z + 1 - self.c)

    def x_dp(self, k):
        return (self.x + k) % 4 * 4 + self.y

    def y_dp(self, k):
        return self.x * 4 + (self.y + k) % 4

    def dp_peer(self, dp):
        return (dp, self.sq)

    def seq_peer(self, k):
        return (self.dp, (self.sq + k) % SEQ)


def remote(src, dst, send, recv, device):
    return pltpu.make_async_remote_copy(
        src_ref=src, dst_ref=dst, send_sem=send, recv_sem=recv, device_id=device, device_id_type=MESH
    )


def greet(peers):
    barrier = pltpu.get_barrier_semaphore()
    for device in peers:
        pl.semaphore_signal(barrier, inc=1, device_id=device, device_id_type=MESH)
    return barrier, len(peers)


def z_peers(me):
    return [me.z_peer(1), me.z_peer(3), me.sibling()]


def ring_peers(me):
    return [me.dp_peer(me.x_dp(1)), me.dp_peer(me.x_dp(3)), me.dp_peer(me.y_dp(1)), me.dp_peer(me.y_dp(3))]


def dp_peers(me):
    return [me.dp_peer((me.dp + k) % DP) for k in range(1, DP)]


def seq_peers(me):
    return [me.seq_peer(k) for k in range(1, SEQ)]


class Gather:
    @staticmethod
    def scratch(n):
        return [VMEM((G, n), bf16), DMA((10,)), DMA((10,)), DMA((SEQ,))]

    def __init__(self, me, own, out, full, send, recv, keep):
        self.me, self.own, self.out, self.full = me, own, out, full
        self.send, self.recv, self.keep = send, recv, keep
        self.sent, self.kept = [], []

    def block(self, k, c, half=None):
        base = self.me.slot(k, c) * T
        if half is None:
            return self.full.at[pl.ds(pl.multiple_of(base, T), T)]
        return self.full.at[pl.ds(pl.multiple_of(base + half * HALF, HALF), HALF)]

    def push(self, n, src, dst, device):
        copy = remote(src, dst, self.send.at[n], self.recv.at[n], device)
        copy.start()
        self.sent.append(copy)

    def arrived(self, n, dst):
        remote(dst, dst, self.send.at[n], self.recv.at[n], self.me.sibling()).wait_recv()

    def store(self, k, c):
        if self.out is None:
            return
        there = self.out.at[pl.ds(pl.multiple_of(self.me.slot(k, c) * T, T), T)]
        copy = pltpu.make_async_copy(self.block(k, c), there, self.keep.at[len(self.kept)])
        copy.start()
        self.kept.append(copy)

    def start(self):
        me = self.me
        right, left = me.z_peer(1), me.z_peer(3)
        mine = self.block(0, me.c)
        a, b = self.block(0, me.c, 0), self.block(0, me.c, 1)
        self.push(0, a, a, right)
        self.push(1, b, b, left)
        self.push(2, b, b, right)
        self.push(3, a, a, left)
        self.push(4, mine, mine, me.sibling())
        self.store(0, me.c)

    def forward(self):
        me = self.me
        right, left = me.z_peer(1), me.z_peer(3)
        a, b = self.block(3, me.c, 0), self.block(1, me.c, 1)
        self.arrived(0, a)
        self.push(5, a, a, right)
        self.arrived(1, b)
        self.push(6, b, b, left)

    def hand_over(self, n, k):
        whole = self.block(k, self.me.c)
        self.push(n, whole, whole, self.me.sibling())
        self.store(k, self.me.c)

    def across_left(self):
        self.arrived(2, self.block(3, self.me.c, 1))
        self.hand_over(7, 3)

    def across_right(self):
        self.arrived(3, self.block(1, self.me.c, 0))
        self.hand_over(8, 1)

    def across_far(self):
        self.arrived(5, self.block(2, self.me.c, 0))
        self.arrived(6, self.block(2, self.me.c, 1))
        self.hand_over(9, 2)

    def across(self):
        self.across_left()
        self.across_right()
        self.across_far()

    def taken(self, n, k):
        self.arrived(n, self.block(k, 1 - self.me.c))
        self.store(k, 1 - self.me.c)

    def own_pair(self):
        self.taken(4, 0)

    def left_pair(self):
        self.taken(7, 3)

    def right_pair(self):
        self.taken(8, 1)

    def far_pair(self):
        self.taken(9, 2)

    def drain(self):
        for copy in self.sent:
            copy.wait_send()
        for copy in self.kept:
            copy.wait()

    def finish(self):
        self.own_pair()
        self.left_pair()
        self.right_pair()
        self.far_pair()
        self.drain()


class Spread:
    sems = 40

    def __init__(self, me, full, rows, send, recv):
        self.me, self.full, self.rows, self.send, self.recv = me, full, rows, send, recv

    def at(self, h, i, j):
        me = self.me
        dx, dy = (i, j) if h == 0 else (j, i)
        return (me.x + dx + 4) % 4 * 4 + (me.y + dy + 4) % 4

    def block(self, h, i, j, q=None):
        half = self.rows // 2
        base = self.at(h, i, j) * self.rows + h * half
        if q is None:
            return self.full.at[pl.ds(pl.multiple_of(base, 16), half)]
        return self.full.at[pl.ds(pl.multiple_of(base + q * (half // 2), 16), half // 2)]

    def push(self, h, n, block, i, j):
        n = 20 * h + n
        remote(block, block, self.send.at[n], self.recv.at[n], self.me.dp_peer(self.at(h, i, j))).start()

    def arrived(self, h, n, block):
        n = 20 * h + n
        remote(block, block, self.send.at[n], self.recv.at[n], self.me.sibling()).wait_recv()

    def second(self, t, i):
        for h in range(2):
            block = self.block(h, i, 0)
            self.push(h, 4 + 4 * t, block, 0, 1)
            self.push(h, 5 + 4 * t, block, 0, -1)

    def start(self):
        for h in range(2):
            block = self.block(h, 0, 0)
            self.push(h, 0, block, 1, 0)
            self.push(h, 1, block, -1, 0)
        self.second(0, 0)

    def turn(self):
        for h in range(2):
            self.arrived(h, 0, self.block(h, -1, 0))
            self.push(h, 2, self.block(h, -1, 0, 0), 1, 0)
            self.arrived(h, 1, self.block(h, 1, 0))
            self.push(h, 3, self.block(h, 1, 0, 1), -1, 0)
        self.second(1, -1)
        self.second(2, 1)

    def far(self):
        for h in range(2):
            self.arrived(h, 2, self.block(h, 2, 0, 0))
            self.arrived(h, 3, self.block(h, 2, 0, 1))
        self.second(3, 2)

    def hand_on(self, t):
        i = (0, -1, 1, 2)[t]
        for h in range(2):
            self.arrived(h, 4 + 4 * t, self.block(h, i, -1))
            self.push(h, 6 + 4 * t, self.block(h, i, -1, 0), 0, 1)
            self.arrived(h, 5 + 4 * t, self.block(h, i, 1))
            self.push(h, 7 + 4 * t, self.block(h, i, 1, 1), 0, -1)

    def finish(self):
        for t, i in enumerate((0, -1, 1, 2)):
            for h in range(2):
                self.arrived(h, 6 + 4 * t, self.block(h, i, 2, 0))
                self.arrived(h, 7 + 4 * t, self.block(h, i, 2, 1))

    def drain(self):
        for h in range(2):
            for n in range(20):
                handed = n in (2, 3) or (n >= 4 and n % 4 >= 2)
                block = self.block(h, 0, 0, 0 if handed else None)
                n = 20 * h + n
                remote(block, block, self.send.at[n], self.recv.at[n], self.me.sibling()).wait_send()


def add_rows(out, at, terms, rows, step=32):
    def body(i, carry):
        here = pl.ds(pl.multiple_of(i * step, step), step)
        total = terms[0](here)
        for term in terms[1:]:
            total = total + term(here)
        there = pl.ds(pl.multiple_of(at + i * step, step), step)
        out[there] = total.astype(out.dtype)
        return carry

    lax.fori_loop(0, rows // step, body, 0)


def reads(ref, start=0):
    def term(here):
        return ref[pl.ds(pl.multiple_of(here.start + start, 16), here.size)].astype(f32)

    return term


class Scatter:
    sems = 10

    @staticmethod
    def scratch(n):
        return [
            VMEM((4, T, n), bf16),
            VMEM((2, HALF, n), bf16),
            VMEM((2, HALF, n), bf16),
            VMEM((4, HALF, n), bf16),
            DMA((10,)),
            DMA((10,)),
        ]

    def __init__(self, me, part, other, through, passed, final, send, recv):
        self.me, self.part = me, part
        self.other, self.through, self.passed, self.final = other, through, passed, final
        self.send, self.recv = send, recv

    def piece(self, k, c):
        return self.part.at[pl.ds(pl.multiple_of(self.me.slot(k, c) * T, T), T)]

    def pair(self, k, q):
        base = self.me.slot(k, self.me.c) * T + q * HALF
        return self.part.at[pl.ds(pl.multiple_of(base, HALF), HALF)]

    def push(self, n, src, dst, device):
        remote(src, dst, self.send.at[n], self.recv.at[n], device).start()

    def arrived(self, n, dst):
        remote(dst, dst, self.send.at[n], self.recv.at[n], self.me.sibling()).wait_recv()

    def start(self):
        me = self.me
        for k in (2, 1, 3, 0):
            self.push(k, self.piece(k, 1 - me.c), self.other.at[k], me.sibling())

    def join(self):
        me = self.me
        right, left = me.z_peer(1), me.z_peer(3)
        for k in (2, 1, 3, 0):
            self.arrived(k, self.other.at[k])
            add_rows(
                self.piece(k, me.c), 0, [reads(self.piece(k, me.c)), reads(self.other.at[k])], T
            )
            if k == 2:
                self.push(4, self.pair(2, 0), self.through.at[0], right)
                self.push(5, self.pair(2, 1), self.through.at[1], left)
            if k == 1:
                self.push(6, self.pair(1, 1), self.final.at[0], right)
            if k == 3:
                self.push(7, self.pair(3, 0), self.final.at[1], left)

    def relay(self):
        me = self.me
        right, left = me.z_peer(1), me.z_peer(3)
        self.arrived(4, self.through.at[0])
        add_rows(self.passed.at[0], 0, [reads(self.through.at[0]), reads(self.pair(1, 0))], HALF)
        self.push(8, self.passed.at[0], self.final.at[2], right)
        self.arrived(5, self.through.at[1])
        add_rows(self.passed.at[1], 0, [reads(self.through.at[1]), reads(self.pair(3, 1))], HALF)
        self.push(9, self.passed.at[1], self.final.at[3], left)

    def finish(self, out, extra=None):
        me = self.me
        for n, k in ((6, 0), (7, 1), (8, 2), (9, 3)):
            self.arrived(n, self.final.at[k])
        more = [] if extra is None else [reads(extra)]
        add_rows(
            out, 0, [reads(self.pair(0, 0)), reads(self.final.at[1]), reads(self.final.at[2])] + more, HALF
        )
        more = [] if extra is None else [reads(extra, HALF)]
        add_rows(
            out,
            HALF,
            [reads(self.pair(0, 1)), reads(self.final.at[0]), reads(self.final.at[3])] + more,
            HALF,
        )
        for n in range(10):
            size = self.other.at[n] if n < 4 else self.final.at[0]
            remote(size, size, self.send.at[n], self.recv.at[n], me.sibling()).wait_send()


class RingSum:
    @staticmethod
    def scratch(shape):
        return [
            VMEM((2, *shape), bf16), VMEM((2, *shape), bf16), VMEM((4, *shape), bf16), DMA((6,)), DMA((6,)),
        ]

    def __init__(self, me, right, left, piece, through, passed, final, send, recv):
        self.me, self.right, self.left, self.piece = me, right, left, piece
        self.through, self.passed, self.final, self.send, self.recv = through, passed, final, send, recv

    def push(self, n, src, dst, device):
        remote(src, dst, self.send.at[n], self.recv.at[n], device).start()

    def arrived(self, n, dst):
        remote(dst, dst, self.send.at[n], self.recv.at[n], self.me.sibling()).wait_recv()

    def start(self):
        self.push(0, self.piece(2, 0), self.through.at[0], self.right)
        self.push(1, self.piece(2, 1), self.through.at[1], self.left)
        self.push(2, self.piece(1, 1), self.final.at[0], self.right)
        self.push(3, self.piece(3, 0), self.final.at[1], self.left)

    def add(self, out, terms):
        count, rows = terms[0].shape[0], terms[0].shape[1]

        def body(i, carry):
            m, here = i // (rows // 16), pl.ds(pl.multiple_of(i % (rows // 16) * 16, 16), 16)
            total = terms[0][m, here].astype(f32)
            for term in terms[1:]:
                total = total + term[m, here].astype(f32)
            out[m, here] = total.astype(out.dtype)
            return carry

        lax.fori_loop(0, count * (rows // 16), body, 0)

    def relay(self):
        self.arrived(0, self.through.at[0])
        self.add(self.passed.at[0], [self.through.at[0], self.piece(1, 0)])
        self.push(4, self.passed.at[0], self.final.at[2], self.right)
        self.arrived(1, self.through.at[1])
        self.add(self.passed.at[1], [self.through.at[1], self.piece(3, 1)])
        self.push(5, self.passed.at[1], self.final.at[3], self.left)

    def finish(self, out):
        for n, k in ((2, 0), (3, 1), (4, 2), (5, 3)):
            self.arrived(n, self.final.at[k])
        self.add(out(0), [self.piece(0, 0), self.final.at[1], self.final.at[2]])
        self.add(out(1), [self.piece(0, 1), self.final.at[0], self.final.at[3]])
        for n in range(6):
            size = self.final.at[0]
            remote(size, size, self.send.at[n], self.recv.at[n], self.me.sibling()).wait_send()


def norm_rows(value, gain):
    return value * lax.rsqrt(jnp.mean(value * value, axis=-1, keepdims=True) + epsilon) * gain


def norm_pull(value, gain, incoming):
    r = lax.rsqrt(jnp.mean(value * value, axis=-1, keepdims=True) + epsilon)
    scaled = incoming * gain
    inner = jnp.mean(value * scaled, axis=-1, keepdims=True)
    normed = value * r
    return r * (scaled - normed * (inner * r)), incoming * normed


CHUNK = 256
STEPS = G // CHUNK
contract_last = (((1,), (1,)), ((), ()))
contract_first = (((0,), (0,)), ((), ()))
gelu_c = 0.7978845608028654
gelu_k = 0.044715


def gelu_parts(v):
    square = v * v
    t = jnp.tanh(gelu_c * (v + gelu_k * square * v))
    half = 0.5 * (1.0 + t)
    slope = half + 0.5 * v * (1.0 - t * t) * (gelu_c * (1.0 + 3.0 * gelu_k * square))
    return v * half, slope


def minus_expm1(z):
    series = -z * (1.0 + z * (1 / 2 + z * (1 / 6 + z * (1 / 24 + z * (1 / 120 + z * (1 / 720))))))
    return jnp.where(z > -0.25, series, 1.0 - jnp.exp(z))


def recur(conv, raw_a, raw_x, terms, start):
    recall = jax.nn.sigmoid(raw_a + terms[5:6])
    admit = jax.nn.sigmoid(raw_x + terms[6:7])
    lograte = terms[7:8] * recall
    decay = jnp.exp(lograte) * (1.0 - start)
    root = jnp.sqrt(minus_expm1(2.0 * lograte))
    scale = start + (1.0 - start) * root
    return recall, admit, lograte, decay, root, scale


def nt(left, right):
    return lax.dot_general(left, right, contract_last, preferred_element_type=f32)


def tn(left, right):
    return lax.dot_general(left, right, contract_first, preferred_element_type=f32)


def nn(left, right):
    return jnp.dot(left, right, preferred_element_type=f32)


def rows_of(base, size):
    return pl.ds(pl.multiple_of(base, 16), size)


def lanes_of(base, size):
    return pl.ds(pl.multiple_of(base, 128), size)


def windows(lab, base):
    return lab[pl.ds(pl.multiple_of(base, 8), CHUNK + 16)]


def same(window, k):
    here = window[8 : 8 + CHUNK, 0:1]
    there = window[8 - k : 8 - k + CHUNK, 0:1]
    return (here == there).astype(f32)


def forward_kernel(
    tok, cot, mix, feed, small, gates, chan,
    cot_out, mix_out, normed_out, x_out, y_out, conv_out, prior_out, mixed_out,
    hidden_out, gu_out, back_out, ff_out, n2_out, gate_out, term_out, gain_out, lab_out, middle,
    mixw, feedw, part, xs, ys, convs, priors, mixeds, hiddens, gus,
    small_in, minor, gate_f,
    xpad, dec, drv, sts, carry, *rest,
):
    tg, cg, ng, sc = rest[:4], rest[4:8], rest[8:12], rest[12:18]
    ms, mr, fs, fr, ss, sr, ps, pr, qs, qr, es, er, hs, hr, ls, os = rest[18:]
    me = Place()
    quarter, at = me.dp // 8, me.dp % 8
    gate_to = (8 * quarter + me.sq, at)
    gate_self = me.sq == at
    chan_to = (8 * (me.dp % 2) + me.sq, me.dp // 2)
    chan_from = (2 * me.sq + me.dp // 8, me.dp % 8)
    chan_self = jnp.logical_and(chan_to[0] == me.dp, chan_to[1] == me.sq)
    barrier, count = greet(seq_peers(me) + ring_peers(me))

    @pl.when(jnp.logical_not(gate_self))
    def _():
        pl.semaphore_signal(barrier, inc=1, device_id=gate_to, device_id_type=MESH)

    @pl.when(jnp.logical_not(chan_self))
    def _():
        pl.semaphore_signal(barrier, inc=1, device_id=chan_from, device_id_type=MESH)

    tokg, cotg, n2g = tg[0], cg[0], ng[0]
    own_rows = rows_of(me.dp * T + me.sq * 16, 16)

    def feed_columns(p, j):
        return lanes_of(p * FF + j * FL, FL)

    local = [
        pltpu.make_async_copy(tok, tokg.at[rows_of(me.sq * T, T)], ls.at[0]),
        pltpu.make_async_copy(cot, cotg.at[rows_of(me.sq * T, T)], ls.at[1]),
        pltpu.make_async_copy(mix.at[me.sq], mixw.at[own_rows], ls.at[2]),
        pltpu.make_async_copy(small, small_in.at[me.sq], ls.at[3]),
    ] + [
        pltpu.make_async_copy(feed.at[:, feed_columns(p, me.sq)], feedw.at[own_rows, pl.ds(p * FL, FL)], ls.at[4 + p])
        for p in range(3)
    ]
    for copy in local:
        copy.start()

    pl.semaphore_wait(barrier, count + jnp.where(gate_self, 0, 1) + jnp.where(chan_self, 0, 1))

    sent = []

    def push(src, dst, send, recv, device):
        sent.append(remote(src, dst, send, recv, device))
        sent[-1].start()

    def arrived(dst, send, recv):
        remote(dst, dst, send, recv, me.sibling()).wait_recv()

    order = (4, 3, 5, 2, 6, 1, 7)
    for k in order:
        to = (me.sq + k) % SEQ
        push(mix.at[to], mixw.at[own_rows], ms.at[k], mr.at[k], me.seq_peer(k))
        push(small, small_in.at[me.sq], ss.at[k], sr.at[k], me.seq_peer(k))

    def minor_rows(dp, start, size):
        return minor.at[rows_of(dp * MINOR + start, size)]

    gate_copy = remote(gates, minor_rows(gate_to[0], 16, 96), hs.at[0], hr.at[0], gate_to)
    chan_copy = remote(chan, minor_rows(chan_to[0], 112, 48), hs.at[1], hr.at[1], chan_to)
    gate_local = pltpu.make_async_copy(gates, minor_rows(me.dp, 16, 96), ls.at[7])
    chan_local = pltpu.make_async_copy(chan, minor_rows(me.dp, 112, 48), ls.at[8])
    gate_here = remote(gates, minor_rows(me.dp, 16, 96), hs.at[0], hr.at[0], gate_to)
    chan_here = remote(chan, minor_rows(me.dp, 112, 48), hs.at[1], hr.at[1], chan_to)

    @pl.when(jnp.logical_not(gate_self))
    def _():
        gate_copy.start()

    @pl.when(gate_self)
    def _():
        gate_local.start()

    @pl.when(jnp.logical_not(chan_self))
    def _():
        chan_copy.start()

    @pl.when(chan_self)
    def _():
        chan_local.start()

    local[0].wait()
    tokens = Gather(me, None, None, *tg)
    tokens.start()
    for k in order:
        to = (me.sq + k) % SEQ
        for p in range(3):
            push(feed.at[:, feed_columns(p, to)], feedw.at[own_rows, pl.ds(p * FL, FL)],
                 fs.at[p, k], fr.at[p, k], me.seq_peer(k))
    for copy in local[1:]:
        copy.wait()

    def seq_rows(k):
        return rows_of(me.dp * T + (me.sq - k + SEQ) % SEQ * 16, 16)

    for k in range(1, SEQ):
        arrived(mixw.at[seq_rows(k)], ms.at[k], mr.at[k])

    mixes = Spread(me, mixw, T, ps, pr)
    feeds = Spread(me, feedw, T, qs, qr)
    minors = Spread(me, minor, MINOR, es, er)
    mixes.start()

    for k in range(1, SEQ):
        arrived(small_in.at[(me.sq - k + SEQ) % SEQ], ss.at[k], sr.at[k])
    gain = small_in[0, 0:16].astype(f32)
    for k in range(1, SEQ):
        gain = gain + small_in[k, 0:16].astype(f32)
    minor[rows_of(me.dp * MINOR, 16)] = gain.astype(bf16)
    minor[rows_of(me.dp * MINOR + 160, 32)] = jnp.zeros((32, 128), bf16)

    @pl.when(jnp.logical_not(gate_self))
    def _():
        gate_copy.wait_send()
        gate_here.wait_recv()

    @pl.when(gate_self)
    def _():
        gate_local.wait()

    @pl.when(jnp.logical_not(chan_self))
    def _():
        chan_copy.wait_send()
        chan_here.wait_recv()

    @pl.when(chan_self)
    def _():
        chan_local.wait()

    minors.start()
    tokens.forward()
    mixes.turn()
    minors.turn()
    cots = Gather(me, None, cot_out, *cg)
    cots.start()
    mixes.far()
    minors.far()

    lab_out[0:8] = jnp.full((8, 128), -1.0, f32)
    lab_out[G + 8 :] = jnp.full((8, 128), -2.0, f32)
    for k in range(SEQ):
        row = small_in[k, 16:32].astype(f32)[0:1]
        lab_out[8 + k * T : 8 + (k + 1) * T] = jnp.broadcast_to(row, (128, 128)).T

    tokens.across()
    for t in range(3):
        mixes.hand_on(t)
        minors.hand_on(t)
    minors.hand_on(3)
    mixes.hand_on(3)
    for k in range(1, SEQ):
        for p in range(3):
            arrived(feedw.at[seq_rows(k), pl.ds(p * FL, FL)], fs.at[p, k], fr.at[p, k])
    feeds.start()
    tokens.finish()
    minors.finish()
    terms = minor[112:160].astype(f32)
    for k in range(1, DP):
        terms = terms + minor[k * MINOR + 112 : k * MINOR + 160].astype(f32)
    for n in range(3):
        group = terms[16 * n : 16 * n + 16]
        lanes = slice(128 * n, 128 * n + 128)
        lane = lax.broadcasted_iota(jnp.int32, (1, 128), 1) + 128 * n
        term_out[:, lanes] = group
        term_out[7:8, lanes] = jnp.where(lane >= WL, -1.0, group[7:8] + group[9:10])
        term_out[8:9, lanes] = group[8:9] + group[10:11]
    gate_f[...] = jnp.zeros(gate_f.shape, f32)
    for k in range(DP):
        gain_out[:, k * 128 : (k + 1) * 128] = minor[k * MINOR : k * MINOR + 16].astype(f32)[0:8]
        base = k // 8 * WP + k % 8 * 40
        for n in range(2):
            lanes = k % 8 // 4 * 128 + n * 128
            start = k * MINOR + 16 + 48 * n
            gate_f[base : base + 40, lanes : lanes + 128] = minor[start : start + 48].astype(f32)[0:40]
    gate_out[0] = gate_f[:WP].astype(bf16)
    gate_out[1] = gate_f[WP:].astype(bf16)

    def normalise(i, c):
        here = pl.ds(pl.multiple_of(i * 16, 16), 16)
        tokg[here] = norm_rows(tokg[here].astype(f32), gain_out[0:1]).astype(bf16)
        return c

    lax.fori_loop(0, G // 16, normalise, 0)
    writes = [pltpu.make_async_copy(tokg, normed_out, os.at[0])]
    writes[0].start()
    cots.forward()
    cots.across()
    mixes.finish()
    writes.append(pltpu.make_async_copy(mixw, mix_out, os.at[1]))
    writes[1].start()

    xpad[0:8] = jnp.zeros((8, WP), f32)
    carry[...] = jnp.zeros((8, WP), f32)
    row = lax.broadcasted_iota(jnp.int32, (8, WP), 0)

    def mix_chunk(step, c):
        @pl.when(step == 1)
        def _():
            feeds.turn()

        @pl.when(step == 2)
        def _():
            feeds.far()

        @pl.when(step == 3)
        def _():
            feeds.hand_on(0)

        base = step * CHUNK
        rows = rows_of(base, CHUNK)
        both = nn(tokg[rows], mixw[:, : 2 * WP])
        x, y = both[:, :WP], both[:, WP:]
        xs[rows] = x
        ys[rows] = y
        xpad[8:] = x
        terms = term_out[...]
        window = windows(lab_out, base)
        start = 1.0 - same(window, 1)
        conv = terms[4:5] + terms[0:1] * x
        for k in range(1, CONV):
            conv = conv + terms[k : k + 1] * (same(window, k) * xpad[8 - k : 8 - k + CHUNK])
        xpad[0:8] = x[CHUNK - 8 :]
        convs[rows] = conv
        lowered = conv.astype(bf16)
        raw_a, raw_x = nn(lowered, gate_out[0]), nn(lowered, gate_out[1])
        recall, admit, lograte, decay, root, scale = recur(conv, raw_a, raw_x, terms, start)
        dec[...] = decay
        drv[...] = scale * admit * conv

        def scan(i, before):
            here = pl.ds(pl.multiple_of(i * 8, 8), 8)
            a, b = dec[here], drv[here]
            for s in (1, 2, 4):
                b = b + a * jnp.where(row >= s, pltpu.roll(b, s, 0), 0.0)
                a = a * jnp.where(row >= s, pltpu.roll(a, s, 0), 1.0)
            state = b + a * before
            sts[here] = state
            priors[pl.ds(pl.multiple_of(base + i * 8, 8), 8)] = jnp.where(row >= 1, pltpu.roll(state, 1, 0), before)
            return jnp.broadcast_to(state[7:8], (8, WP))

        carry[...] = lax.fori_loop(0, CHUNK // 8, scan, carry[...], unroll=4)
        value, _ = gelu_parts(ys[rows])
        mixed = (value * sts[...]).astype(bf16)
        mixeds[rows] = mixed
        part[rows] = nt(mixed, mixw[:, 2 * WP :]).astype(bf16)
        return c

    lax.fori_loop(0, STEPS, mix_chunk, 0)

    total = Scatter(me, part, *sc)
    total.start()
    for n, (src, dst) in enumerate(((xs, x_out), (ys, y_out), (convs, conv_out), (priors, prior_out), (mixeds, mixed_out))):
        writes.append(pltpu.make_async_copy(src, dst, os.at[2 + n]))
        writes[-1].start()
    total.join()
    feeds.hand_on(1)
    feeds.hand_on(2)
    total.relay()
    feeds.hand_on(3)
    total.finish(middle, tok)

    def second_norm(i, c):
        here = pl.ds(pl.multiple_of(i * 16, 16), 16)
        n2g[rows_of(me.sq * T + i * 16, 16)] = norm_rows(middle[here], gain_out[1:2]).astype(bf16)
        return c

    lax.fori_loop(0, T // 16, second_norm, 0)
    seconds = Gather(me, None, n2_out, *ng)
    seconds.start()
    cots.finish()
    writes[0].wait()
    feeds.finish()

    def feed_chunk(k, n):
        rows = rows_of(me.chip(k) * CHUNK, CHUNK)
        gu = nn(n2g[rows], feedw[:, : 2 * FL])
        gate, up = gu[:, :FL], gu[:, FL:]
        adj_hidden = nn(cotg[rows], feedw[:, 2 * FL :])
        value, slope = gelu_parts(gate)
        hidden = (value * up).astype(bf16)
        hiddens[rows] = hidden
        gus[rows, :FL] = (adj_hidden * up * slope).astype(bf16)
        gus[rows, FL:] = (adj_hidden * value).astype(bf16)
        tokg[rows] = nt(hidden, feedw[:, 2 * FL :]).astype(bf16)
        part[rows] = nt(gus[rows], feedw[:, : 2 * FL]).astype(bf16)

    def feed_store(k, n):
        rows = rows_of(me.chip(k) * CHUNK, CHUNK)
        for m, (src, dst) in enumerate(((hiddens, hidden_out), (gus, gu_out), (tokg, ff_out), (part, back_out))):
            writes.append(pltpu.make_async_copy(src.at[rows], dst.at[rows], os.at[7 + 4 * n + m]))
            writes[-1].start()

    seconds.own_pair()
    feed_chunk(0, 0)
    feed_store(0, 0)
    seconds.forward()
    seconds.across_left()
    seconds.across_right()
    seconds.left_pair()
    feed_chunk(3, 1)
    feed_store(3, 1)
    seconds.across_far()
    seconds.right_pair()
    feed_chunk(1, 2)
    feed_store(1, 2)
    seconds.far_pair()
    feed_chunk(2, 3)
    feed_store(2, 3)
    seconds.drain()
    for copy in writes[1:]:
        copy.wait()
    for copy in sent:
        copy.wait_send()
    mixes.drain()
    minors.drain()
    feeds.drain()


def forward_call(tok, cot, mix, feed, small, gates, chan):
    sds = jax.ShapeDtypeStruct
    hbm, vmem = pl.BlockSpec(memory_space=ANY), pl.BlockSpec(memory_space=VMEM)
    return pl.pallas_call(
        forward_kernel,
        out_shape=(
            sds((G, D), bf16), sds((D, MW), bf16), sds((G, D), bf16),
            sds((G, WP), f32), sds((G, WP), f32), sds((G, WP), f32), sds((G, WP), f32), sds((G, WP), bf16),
            sds((G, FL), bf16), sds((G, 2 * FL), bf16), sds((G, D), bf16), sds((G, D), bf16), sds((G, D), bf16),
            sds((2, WP, WP), bf16), sds((16, WP), f32), sds((8, D), f32), sds((G + 16, 128), f32), sds((T, D), f32),
        ),
        in_specs=[vmem, hbm, hbm, hbm, vmem, vmem, vmem],
        out_specs=[hbm] * 13 + [vmem] * 5,
        scratch_shapes=[
            VMEM((D, MW), bf16), VMEM((D, FW), bf16), VMEM((G, D), bf16),
            VMEM((G, WP), f32), VMEM((G, WP), f32), VMEM((G, WP), f32), VMEM((G, WP), f32), VMEM((G, WP), bf16),
            VMEM((G, FL), bf16), VMEM((G, 2 * FL), bf16),
            VMEM((SEQ, 32, 128), bf16), VMEM((DP * MINOR, 128), bf16), VMEM((2 * WP, WP), f32),
            VMEM((CHUNK + 8, WP), f32), VMEM((CHUNK, WP), f32), VMEM((CHUNK, WP), f32), VMEM((CHUNK, WP), f32),
            VMEM((8, WP), f32),
            *Gather.scratch(D), *Gather.scratch(D), *Gather.scratch(D), *Scatter.scratch(D),
            DMA((SEQ,)), DMA((SEQ,)), DMA((3, SEQ)), DMA((3, SEQ)), DMA((SEQ,)), DMA((SEQ,)),
            DMA((40,)), DMA((40,)), DMA((40,)), DMA((40,)), DMA((40,)), DMA((40,)),
            DMA((2,)), DMA((2,)), DMA((9,)), DMA((23,)),
        ],
        compiler_params=pltpu.CompilerParams(collective_id=1, has_side_effects=True, vmem_limit_bytes=(63 << 20) + (900 << 10)),
        cost_estimate=pl.CostEstimate(flops=30 * G * D * WP, bytes_accessed=100 << 20, transcendentals=0),
        name="forward",
    )(tok, cot, mix, feed, small, gates, chan)


def turn_kernel(
    back_in, ff_in, n2_in, cot_in, hid_in, gu_in, x_in, y_in, conv_in, prior_in, w_in,
    middle, cot, gains, gates, terms_ref, lab,
    adj_all, s1_out, both_out, part_out, adj_middle, act, gain_grad, extra,
    part, ffp, mg, s1, both, dec, adjs, acp, carry, gate_grad, sums, *rest,
):
    one, two, gathering, ring_a, ring_b = rest[:6], rest[6:12], rest[12:16], rest[16:21], rest[21:26]
    ls, os = rest[26:]
    me = Place()
    first = [pltpu.make_async_copy(back_in, part, ls.at[0]), pltpu.make_async_copy(ff_in, ffp, ls.at[1])]
    first[0].start()
    barrier, count = greet(z_peers(me) + ring_peers(me))
    pl.semaphore_wait(barrier, count)
    xs, ys = (me.dp_peer(me.x_dp(1)), me.dp_peer(me.x_dp(3))), (me.dp_peer(me.y_dp(1)), me.dp_peer(me.y_dp(3)))
    upper = RingSum(
        me, *ys, lambda k, q: mg.at[:, (me.y + k) % 4, pl.ds(q * 32, 32)], *ring_a
    )
    lower = RingSum(
        me, *xs, lambda k, q: mg.at[(me.x + k) % 4, :, pl.ds(HALF + q * 32, 32)], *ring_b
    )
    mine = me.sq * T

    def grads(n2, cots, gu, hid):
        loads = [
            pltpu.make_async_copy(src, dst, ls.at[2 + n])
            for n, (src, dst) in enumerate(((n2_in, n2), (cot_in, cots), (gu_in, gu), (hid_in, hid)))
        ]
        first[0].wait()
        inner = Scatter(me, part, *one)
        inner.start()
        for copy in loads:
            copy.start()
        first[1].start()
        inner.join()
        for copy in loads:
            copy.wait()

        def tile(i, c):
            here = pl.ds(pl.multiple_of(i * 256, 256), 256)
            left = tn(n2[:, here], gu[...]).astype(bf16)
            right = tn(cots[:, here], hid[...]).astype(bf16)
            for h in range(2):
                mg[i // 2, i % 2 * 2 + h, :, : 2 * FL] = left[h * T : (h + 1) * T]
                mg[i // 2, i % 2 * 2 + h, :, 2 * FL :] = right[h * T : (h + 1) * T]

            @pl.when(i == 3)
            def _():
                inner.relay()

            return c

        lax.fori_loop(0, 8, tile, 0)
        upper.start()
        lower.start()
        inner.finish(adj_middle)

    pl.run_scoped(grads, VMEM((G, D), bf16), VMEM((G, D), bf16), VMEM((G, 2 * FL), bf16), VMEM((G, FL), bf16))

    def pull(i, c):
        here = pl.ds(pl.multiple_of(i * 16, 16), 16)
        pulled, terms = norm_pull(middle[here], gains[1:2], adj_middle[here])
        value = cot[here].astype(f32) + pulled
        adj_middle[here] = value
        gathering[0][rows_of(mine + i * 16, 16)] = value.astype(bf16)
        return c + jnp.sum(terms, axis=0, keepdims=True)

    gain_grad[...] = lax.fori_loop(0, T // 16, pull, jnp.zeros((1, D), f32))
    gather = Gather(me, None, adj_all, *gathering)
    gather.start()
    first[1].wait()
    outer = Scatter(me, ffp, *two)

    def unmix(x_all, y_all, conv_all, prior_all, w):
        loads = [
            pltpu.make_async_copy(src, dst, ls.at[2 + n])
            for n, (src, dst) in enumerate(
                ((x_in, x_all), (y_in, y_all), (conv_in, conv_all), (prior_in, prior_all), (w_in, w))
            )
        ]
        for copy in loads:
            copy.start()
        gather.forward()
        upper.relay()
        lower.relay()
        gather.across()
        dec[CHUNK:] = jnp.zeros((8, WP), f32)
        acp[CHUNK:] = jnp.zeros((8, WP), f32)
        carry[...] = jnp.zeros((8, WP), f32)
        gate_grad[...] = jnp.zeros(gate_grad.shape, f32)
        sums[...] = jnp.zeros(sums.shape, f32)
        for copy in loads:
            copy.wait()
        gather.finish()
        outer.start()
        row = lax.broadcasted_iota(jnp.int32, (8, WP), 0)

        def chunk(step, c):
            @pl.when(step == 1)
            def _():
                outer.join()

            @pl.when(step == 3)
            def _():
                outer.relay()

            base = (STEPS - 1 - step) * CHUNK
            rows = rows_of(base, CHUNK)
            window = windows(lab, base)
            terms = terms_ref[...]
            start = 1.0 - same(window, 1)
            conv, prior = conv_all[rows], prior_all[rows]
            lowered = conv.astype(bf16)
            raw_a, raw_x = nn(lowered, gates[0]), nn(lowered, gates[1])
            recall, admit, lograte, decay, root, scale = recur(conv, raw_a, raw_x, terms, start)
            dec[0:CHUNK] = decay
            states = decay * prior + scale * admit * conv
            adj_mixed = nn(gathering[0][rows], w[:, 2 * WP :])
            value, slope = gelu_parts(y_all[rows])
            adjs[...] = adj_mixed * value
            both[rows, WP:] = (adj_mixed * states * slope).astype(bf16)

            def scan(i, after):
                at = pl.multiple_of((CHUNK // 8 - 1 - i) * 8, 8)
                here = pl.ds(at, 8)
                later = dec[pl.ds(pl.multiple_of(at + 8, 8), 8)]
                a = jnp.where(row < 7, pltpu.roll(dec[here], 7, 0), later[0:1])
                b = adjs[here]
                for s in (1, 2, 4):
                    b = b + a * jnp.where(row < 8 - s, pltpu.roll(b, 8 - s, 0), 0.0)
                    a = a * jnp.where(row < 8 - s, pltpu.roll(a, 8 - s, 0), 1.0)
                value = b + a * after
                adjs[here] = value
                return jnp.broadcast_to(value[0:1], (8, WP))

            carry[...] = lax.fori_loop(0, CHUNK // 8, scan, carry[...], unroll=4)
            adjoint = adjs[...]
            flow = adjoint * admit * conv
            adj_lograte = adjoint * prior * decay - (1.0 - start) * flow * (jnp.exp(2.0 * lograte) / root)
            adj_ra = adj_lograte * terms[7:8] * (recall * (1.0 - recall))
            adj_rx = flow * scale * (1.0 - admit)

            def total(v):
                return jnp.sum(v, axis=0, keepdims=True)

            sums[5:6] += total(adj_ra)
            sums[6:7] += total(adj_rx)
            sums[7:8] += total(adj_lograte * recall) * terms[8:9]
            low_a, low_x = adj_ra.astype(bf16), adj_rx.astype(bf16)
            adj_conv = adjoint * scale * admit + nt(low_a, gates[0]) + nt(low_x, gates[1])
            gate_grad[0] += tn(lowered, low_a)
            gate_grad[1] += tn(lowered, low_x)
            acp[0:CHUNK] = adj_conv
            x = x_all[rows]
            adj_x = terms[0:1] * adj_conv
            sums[4:5] += total(adj_conv)
            sums[0:1] += total(adj_conv * x)
            for k in range(1, CONV):
                moved = same(window, -k) * acp[k : k + CHUNK]
                adj_x = adj_x + terms[k : k + 1] * moved
                sums[k : k + 1] += total(moved * x)
            dec[CHUNK:] = dec[0:8]
            acp[CHUNK:] = acp[0:8]
            both[rows, :WP] = adj_x.astype(bf16)
            part[rows] = nt(both[rows], w[:, : 2 * WP]).astype(bf16)
            return c

        lax.fori_loop(0, STEPS, chunk, 0)

    wide = VMEM((G, WP), f32)
    pl.run_scoped(unmix, wide, wide, wide, wide, VMEM((D, MW), bf16))
    writes = [pltpu.make_async_copy(part, part_out, os.at[0]), pltpu.make_async_copy(both, both_out, os.at[1])]
    for copy in writes:
        copy.start()
    for k in range(DP):
        rows = slice(k % 8 * 40, k % 8 * 40 + 40)
        for n in range(2):
            lanes = slice(k % 8 // 4 * 128 + n * 128, k % 8 // 4 * 128 + n * 128 + 128)
            piece = jnp.concatenate([gate_grad[k // 8, rows, lanes], jnp.zeros((8, 128), f32)], 0)
            extra[k, 48 * n : 48 * n + 48] = piece.astype(bf16)
            lanes = slice(channel_window(k) + n * 128, channel_window(k) + n * 128 + 128)
            piece = jnp.concatenate([sums[:, lanes], jnp.zeros((8, 128), f32)], 0)
            extra[k, 96 + 16 * n : 112 + 16 * n] = piece.astype(bf16)
    upper.finish(lambda q: s1.at[0, :, pl.ds(q * 32, 32)])
    lower.finish(lambda q: s1.at[1, :, pl.ds(q * 32, 32)])
    writes.append(pltpu.make_async_copy(s1, s1_out, os.at[2]))
    writes[2].start()
    outer.finish(act, middle)
    for copy in writes:
        copy.wait()


def channel_window(k):
    return min(k * 20 // 128, 1) * 128


def turn_call(back, ff, n2, cots, hid, gu, saved, w, middle, cot, gains, gates, terms, lab):
    sds = jax.ShapeDtypeStruct
    hbm, vmem = pl.BlockSpec(memory_space=ANY), pl.BlockSpec(memory_space=VMEM)
    return pl.pallas_call(
        turn_kernel,
        out_shape=(
            sds((G, D), bf16), sds((2, 4, HALF, FW), bf16), sds((G, 2 * WP), bf16), sds((G, D), bf16),
            sds((T, D), f32), sds((T, D), bf16), sds((1, D), f32), sds((DP, 128, 128), bf16),
        ),
        in_specs=[hbm] * 11 + [vmem] * 6,
        out_specs=[hbm] * 4 + [vmem] * 4,
        scratch_shapes=[
            VMEM((G, D), bf16), VMEM((G, D), bf16), VMEM((4, 4, T, FW), bf16),
            VMEM((2, 4, HALF, FW), bf16), VMEM((G, 2 * WP), bf16),
            VMEM((CHUNK + 8, WP), f32), VMEM((CHUNK, WP), f32), VMEM((CHUNK + 8, WP), f32), VMEM((8, WP), f32),
            VMEM((2, WP, WP), f32), VMEM((8, WP), f32),
            *Scatter.scratch(D), *Scatter.scratch(D), *Gather.scratch(D),
            *RingSum.scratch((4, 32, FW)), *RingSum.scratch((4, 32, FW)), DMA((8,)), DMA((3,)),
        ],
        compiler_params=pltpu.CompilerParams(collective_id=2, has_side_effects=True, vmem_limit_bytes=(63 << 20) + (900 << 10)),
        cost_estimate=pl.CostEstimate(flops=30 * G * D * WP, bytes_accessed=100 << 20, transcendentals=0),
        name="turn",
    )(back, ff, n2, cots, hid, gu, *saved, w, middle, cot, gains, gates, terms, lab)


def close_kernel(
    part_in, normed_in, both_in, adj_in, mixed_in, extra_in, s1_in, tok, adj_middle, gains, gain_two,
    in_grad, mix_out, feed_out, gate_out, chan_out, gain_out,
    part, normed, both, adj_out, mixed, mg, s1f, s1, lastf, last, adj, gp, gp_in, gain_sum, gain_in, *rest,
):
    one, fa, fb, ma, mb, na, nb = rest[:6], *(rest[6 + 5 * n : 11 + 5 * n] for n in range(6))
    m3s, m3r, f3s, f3r, gs, gr, hs, hr, qs, qr, ls, ws = rest[36:]
    me = Place()
    loads = [
        pltpu.make_async_copy(src, dst, ws.at[n])
        for n, (src, dst) in enumerate(
            ((part_in, part), (s1_in, s1f), (normed_in, normed), (both_in, both), (adj_in, adj_out),
             (mixed_in, mixed), (extra_in, mg.at[:, :, :, pl.ds(MW, 128)]))
        )
    ]
    for copy in loads:
        copy.start()
    quarter, at = me.dp // 8, me.dp % 8
    gate_to = (8 * quarter + me.sq, at)
    gate_self = me.sq == at
    chan_from = (8 * (me.dp % 2) + me.sq, me.dp // 2)
    chan_to = (2 * me.sq + me.dp // 8, me.dp % 8)
    chan_self = jnp.logical_and(chan_from[0] == me.dp, chan_from[1] == me.sq)
    barrier, count = greet(seq_peers(me) + dp_peers(me))

    @pl.when(jnp.logical_not(gate_self))
    def _():
        pl.semaphore_signal(barrier, inc=1, device_id=gate_to, device_id_type=MESH)

    @pl.when(jnp.logical_not(chan_self))
    def _():
        pl.semaphore_signal(barrier, inc=1, device_id=chan_from, device_id_type=MESH)

    pl.semaphore_wait(barrier, count + jnp.where(gate_self, 0, 1) + jnp.where(chan_self, 0, 1))

    sent = []

    def push(src, dst, send, recv, device):
        sent.append(remote(src, dst, send, recv, device))
        sent[-1].start()

    def arrived(dst, send, recv):
        remote(dst, dst, send, recv, me.sibling()).wait_recv()

    xs, ys = (me.dp_peer(me.x_dp(1)), me.dp_peer(me.x_dp(3))), (me.dp_peer(me.y_dp(1)), me.dp_peer(me.y_dp(3)))
    feed_up = RingSum(me, *xs, lambda k, q: s1f.at[0, pl.ds((me.x + k) % 4, 1), pl.ds(q * 32, 32)], *fa)
    feed_low = RingSum(me, *ys, lambda k, q: s1f.at[1, pl.ds((me.y + k) % 4, 1), pl.ds(q * 32, 32)], *fb)
    mix_up = RingSum(me, *ys, lambda k, q: mg.at[:, (me.y + k) % 4, pl.ds(q * 32, 32)], *ma)
    mix_low = RingSum(me, *xs, lambda k, q: mg.at[(me.x + k) % 4, :, pl.ds(HALF + q * 32, 32)], *mb)
    last_up = RingSum(me, *xs, lambda k, q: s1.at[0, pl.ds((me.x + k) % 4, 1), pl.ds(q * 32, 32)], *na)
    last_low = RingSum(me, *ys, lambda k, q: s1.at[1, pl.ds((me.y + k) % 4, 1), pl.ds(q * 32, 32)], *nb)

    inner = Scatter(me, part, *one)
    loads[0].wait()
    inner.start()
    loads[1].wait()
    feed_up.start()
    feed_low.start()
    inner.join()
    for copy in loads[2:]:
        copy.wait()

    def tile(i, carry):
        here = pl.ds(pl.multiple_of(i * 256, 256), 256)
        left = tn(normed[:, here], both[...]).astype(bf16)
        right = tn(adj_out[:, here], mixed[...]).astype(bf16)
        for h in range(2):
            mg[i // 2, i % 2 * 2 + h, :, : 2 * WP] = left[h * T : (h + 1) * T]
            mg[i // 2, i % 2 * 2 + h, :, 2 * WP : MW] = right[h * T : (h + 1) * T]

        @pl.when(i == 4)
        def _():
            inner.relay()
            feed_up.relay()
            feed_low.relay()

        return carry

    lax.fori_loop(0, 8, tile, 0)
    mix_up.start()
    mix_low.start()
    inner.finish(adj)

    def pull(i, carry):
        here = pl.ds(pl.multiple_of(i * 16, 16), 16)
        pulled, terms = norm_pull(tok[here].astype(f32), gains[0:1], adj[here])
        in_grad[here] = adj_middle[here] + pulled
        return carry + jnp.sum(terms, axis=0, keepdims=True)

    gain_one = lax.fori_loop(0, T // 16, pull, jnp.zeros((1, D), f32))
    gp[...] = jnp.zeros(gp.shape, f32)
    for k in range(DP):
        gp[k, 0:1] = gain_one[:, k * 128 : (k + 1) * 128]
        gp[k, 1:2] = gain_two[:, k * 128 : (k + 1) * 128]
    for k in range(1, DP):
        to = (me.dp + k) % DP
        push(gp.at[to], gp_in.at[k], gs.at[k], gr.at[k], me.dp_peer(to))

    feed_up.finish(lambda q: lastf.at[:, pl.ds(q * 32, 32)])
    feed_low.finish(lambda q: lastf.at[:, pl.ds(HALF + q * 32, 32)])

    def feed_columns(p, j):
        return lanes_of(p * FF + j * FL, FL)

    keeps = [
        pltpu.make_async_copy(
            lastf.at[0, rows_of(me.sq * 16, 16), pl.ds(p * FL, FL)], feed_out.at[:, feed_columns(p, me.sq)], ls.at[p]
        )
        for p in range(3)
    ]
    for copy in keeps:
        copy.start()
    order = (4, 3, 5, 2, 6, 1, 7)
    for k in order:
        to = (me.sq + k) % SEQ
        for p in range(3):
            push(lastf.at[0, rows_of(to * 16, 16), pl.ds(p * FL, FL)], feed_out.at[:, feed_columns(p, me.sq)],
                 f3s.at[p, k], f3r.at[p, k], me.seq_peer(k))

    mix_up.relay()
    mix_low.relay()

    for k in range(1, DP):
        arrived(gp_in.at[k], gs.at[k], gr.at[k])

    def sum_gains(k, total):
        return total + gp_in[k]

    gain_sum[...] = lax.fori_loop(1, DP, sum_gains, gp[me.dp])
    for k in range(1, SEQ):
        push(gain_sum, gain_in.at[k], qs.at[k], qr.at[k], me.seq_peer(k))

    mix_up.finish(lambda q: s1.at[0, :, pl.ds(q * 32, 32)])
    last_up.start()
    mix_low.finish(lambda q: s1.at[1, :, pl.ds(q * 32, 32)])
    last_low.start()
    for k in range(1, SEQ):
        arrived(gain_in.at[k], qs.at[k], qr.at[k])
    total = gain_sum[...]
    for k in range(1, SEQ):
        total = total + gain_in[k]
    gain_out[...] = total
    last_up.relay()
    last_low.relay()
    last_up.finish(lambda q: last.at[:, pl.ds(q * 32, 32)])
    last_low.finish(lambda q: last.at[:, pl.ds(HALF + q * 32, 32)])

    columns = pl.ds(0, MW)
    keeps.append(pltpu.make_async_copy(last.at[0, rows_of(me.sq * 16, 16), columns], mix_out.at[me.sq], ls.at[3]))
    keeps[-1].start()
    for k in order:
        to = (me.sq + k) % SEQ
        push(last.at[0, rows_of(to * 16, 16), columns], mix_out.at[me.sq], m3s.at[k], m3r.at[k], me.seq_peer(k))
    gate_sum, chan_sum = last.at[0, pl.ds(0, 96), pl.ds(MW, 128)], last.at[0, pl.ds(96, 32), pl.ds(MW, 128)]
    gate_copy = remote(gate_sum, gate_out, hs.at[0], hr.at[0], gate_to)
    chan_copy = remote(chan_sum, chan_out, hs.at[1], hr.at[1], chan_to)
    gate_local = pltpu.make_async_copy(gate_sum, gate_out, ls.at[4])
    chan_local = pltpu.make_async_copy(chan_sum, chan_out, ls.at[5])

    @pl.when(jnp.logical_not(gate_self))
    def _():
        gate_copy.start()

    @pl.when(gate_self)
    def _():
        gate_local.start()

    @pl.when(jnp.logical_not(chan_self))
    def _():
        chan_copy.start()

    @pl.when(chan_self)
    def _():
        chan_local.start()

    for k in range(1, SEQ):
        source = (me.sq - k + SEQ) % SEQ
        for p in range(3):
            arrived(feed_out.at[:, feed_columns(p, source)], f3s.at[p, k], f3r.at[p, k])
        arrived(mix_out.at[source], m3s.at[k], m3r.at[k])

    @pl.when(jnp.logical_not(gate_self))
    def _():
        gate_copy.wait()

    @pl.when(gate_self)
    def _():
        gate_local.wait()

    @pl.when(jnp.logical_not(chan_self))
    def _():
        chan_copy.wait()

    @pl.when(chan_self)
    def _():
        chan_local.wait()

    for copy in keeps:
        copy.wait()
    for copy in sent:
        copy.wait_send()


def close_call(part, normed, both, adj_out, mixed, extra, s1, tok, adj_middle, gains, gain_two):
    sds = jax.ShapeDtypeStruct
    hbm, vmem = pl.BlockSpec(memory_space=ANY), pl.BlockSpec(memory_space=VMEM)
    wide = MW + 128
    return pl.pallas_call(
        close_kernel,
        out_shape=(
            sds((T, D), f32), sds((SEQ, 16, MW), bf16), sds((16, 3 * FF), bf16),
            sds((96, 128), bf16), sds((32, 128), bf16), sds((8, 128), f32),
        ),
        in_specs=[hbm] * 7 + [vmem] * 4,
        out_specs=[vmem] * 6,
        scratch_shapes=[
            VMEM((G, D), bf16), VMEM((G, D), bf16), VMEM((G, 2 * WP), bf16), VMEM((G, D), bf16), VMEM((G, WP), bf16),
            VMEM((4, 4, T, wide), bf16), VMEM((2, 4, HALF, FW), bf16), VMEM((2, 4, HALF, wide), bf16),
            VMEM((1, T, FW), bf16), VMEM((1, T, wide), bf16), VMEM((T, D), f32),
            VMEM((DP, 8, 128), f32), VMEM((DP, 8, 128), f32), VMEM((8, 128), f32), VMEM((SEQ, 8, 128), f32),
            *Scatter.scratch(D),
            *RingSum.scratch((1, 32, FW)), *RingSum.scratch((1, 32, FW)),
            *RingSum.scratch((4, 32, wide)), *RingSum.scratch((4, 32, wide)),
            *RingSum.scratch((1, 32, wide)), *RingSum.scratch((1, 32, wide)),
            DMA((8,)), DMA((8,)), DMA((3, 8)), DMA((3, 8)), DMA((DP,)), DMA((DP,)), DMA((2,)), DMA((2,)),
            DMA((SEQ,)), DMA((SEQ,)), DMA((6,)), DMA((7,)),
        ],
        compiler_params=pltpu.CompilerParams(collective_id=4, has_side_effects=True, vmem_limit_bytes=62 << 20),
        cost_estimate=pl.CostEstimate(flops=5 * G * D * WP, bytes_accessed=100 << 20, transcendentals=0),
        name="close",
    )(part, normed, both, adj_out, mixed, extra, s1, tok, adj_middle, gains, gain_two)


def shards(tokens, segments, mixer_weights, norm_gains, gate_weights, channel_terms, feed_weights, cotangent):
    dp, sq = lax.axis_index("dp"), lax.axis_index("seq")
    mix = jnp.pad(mixer_weights.reshape(16, 3, SEQ, WL), ((0, 0), (0, 0), (0, 0), (0, WP - WL)))
    mix = mix.transpose(2, 0, 1, 3).reshape(SEQ, 16, MW)
    lane = lax.broadcasted_iota(jnp.int32, (2, 128), 1)
    gain_rows = jnp.where(lane // 16 == sq, jnp.tile(norm_gains.T, (1, SEQ)), jnp.zeros((), bf16))
    small = jnp.concatenate(
        [jnp.pad(gain_rows, ((0, 14), (0, 0))), jnp.pad(segments.astype(bf16)[None], ((0, 15), (0, 0)))], 0
    )
    gate_block = jnp.where(
        sq < 4,
        jnp.pad(gate_weights, ((0, 8), (0, 256 - BW))),
        jnp.pad(gate_weights, ((0, 8), (BW - 128, 2 * 128 - 2 * BW + 128))),
    )
    gate_block = jnp.concatenate([gate_block[:, :128], gate_block[:, 128:]], 0)
    channel = channel_terms.T.astype(f32)
    lam = channel[7:8]
    derived = jnp.concatenate([-rate_scale * jax.nn.softplus(-lam), rate_scale * jax.nn.sigmoid(-lam)], 0)
    coarse = lax.optimization_barrier(derived.astype(bf16)).astype(f32)
    columns = jnp.concatenate([channel[:7], coarse, derived - coarse], 0)
    piece = 8 * (dp % 2) + sq
    chan_block = lax.dynamic_update_slice(jnp.zeros((16, WP), f32), columns, (0, piece * 20)).astype(bf16)
    chan_block = jnp.concatenate([chan_block[:, n * 128 : n * 128 + 128] for n in range(3)], 0)
    (
        cot_all, w, normed, *saved, mixed, hidden, adj_gu, back_part, feed_part, norm_two,
        gates, terms, gains, lab, middle,
    ) = forward_call(tokens, cotangent, mix, feed_weights, small, gate_block, chan_block)
    adj_all, s1, both, in_part, adj_middle, activations, gain_two, extra = turn_call(
        back_part, feed_part, norm_two, cot_all, hidden, adj_gu, saved, w, middle, cotangent, gains, gates, terms, lab
    )
    input_gradient, mix_out, feed_out, gate_out, chan_out, gain_out = close_call(
        in_part, normed, both, adj_all, mixed, extra.reshape(4, 4, 128, 128), s1, tokens, adj_middle, gains, gain_two
    )
    mixer_gradient = (
        mix_out.reshape(SEQ, 16, 3, WP)[..., :WL].transpose(1, 2, 0, 3).reshape(16, 3 * W).astype(f32)
    )
    feed_gradient = feed_out.astype(f32)
    gate_out = jnp.concatenate([gate_out[:40], gate_out[48:88]], 1).astype(f32)
    gate_gradient = jnp.where(sq < 4, gate_out[:, :BW], gate_out[:, BW - 128 : 2 * BW - 128])
    chan_out = jnp.concatenate([chan_out[:8], chan_out[16:24]], 1).astype(f32)
    window = jnp.minimum(piece * 20 // 128, 1) * 128
    channel_gradient = lax.dynamic_slice(chan_out, (0, piece * 20 - window), (8, 20)).T
    gain_gradient = lax.dynamic_slice(gain_out, (0, sq * 16), (2, 16)).T
    return (activations, input_gradient, mixer_gradient, gain_gradient, gate_gradient, channel_gradient, feed_gradient)


def solution(mesh):
    one = P(("dp", "seq"))
    two = P(("dp", "seq"), None)
    placed = (two, one, two, two, two, two, two, two)
    return jax.shard_map(shards, mesh=mesh, in_specs=placed, out_specs=(two,) * 7, check_vma=False)
```

```python
import functools

import jax
import jax.numpy as jnp
from jax import lax
from jax.experimental import pallas as pl
from jax.experimental.pallas import tpu as pltpu
from jax.sharding import PartitionSpec as P

D = 2048
W = 2560
FF = 6144
CONV = 4
BW = 160
SEQ = 8
DP = 16
T = 128
G = 1024
WL = W // SEQ
WP = 384
MW = 3 * WP
FL = FF // SEQ
FW = 3 * FL
HALF = T // 2
MINOR = 192

epsilon = 1e-06
rate_scale = 8.0
f32 = jnp.float32
bf16 = jnp.bfloat16
MESH = pl.DeviceIdType.MESH
ANY = pl.ANY
VMEM = pltpu.VMEM
DMA = pltpu.SemaphoreType.DMA


class Place:
    def __init__(self):
        self.dp = lax.axis_index("dp")
        self.sq = lax.axis_index("seq")
        self.x, self.y = self.dp // 4, self.dp % 4
        self.z, self.c = self.sq // 2, self.sq % 2

    def chip(self, k):
        return (self.z + k) % 4

    def slot(self, k, c):
        return 2 * self.chip(k) + c

    def z_peer(self, k):
        return (self.dp, 2 * self.chip(k) + self.c)

    def sibling(self):
        return (self.dp, 2 * self.z + 1 - self.c)

    def x_dp(self, k):
        return (self.x + k) % 4 * 4 + self.y

    def y_dp(self, k):
        return self.x * 4 + (self.y + k) % 4

    def dp_peer(self, dp):
        return (dp, self.sq)

    def seq_peer(self, k):
        return (self.dp, (self.sq + k) % SEQ)


def remote(src, dst, send, recv, device):
    return pltpu.make_async_remote_copy(
        src_ref=src, dst_ref=dst, send_sem=send, recv_sem=recv, device_id=device, device_id_type=MESH
    )


def greet(peers):
    barrier = pltpu.get_barrier_semaphore()
    for device in peers:
        pl.semaphore_signal(barrier, inc=1, device_id=device, device_id_type=MESH)
    return barrier, len(peers)


def z_peers(me):
    return [me.z_peer(1), me.z_peer(3), me.sibling()]


def ring_peers(me):
    return [me.dp_peer(me.x_dp(1)), me.dp_peer(me.x_dp(3)), me.dp_peer(me.y_dp(1)), me.dp_peer(me.y_dp(3))]


def dp_peers(me):
    return [me.dp_peer((me.dp + k) % DP) for k in range(1, DP)]


def seq_peers(me):
    return [me.seq_peer(k) for k in range(1, SEQ)]


class Gather:
    @staticmethod
    def scratch(n):
        return [VMEM((G, n), bf16), DMA((10,)), DMA((10,)), DMA((SEQ,))]

    def __init__(self, me, own, out, full, send, recv, keep):
        self.me, self.own, self.out, self.full = me, own, out, full
        self.send, self.recv, self.keep = send, recv, keep

    def block(self, k, c, half=None):
        base = self.me.slot(k, c) * T
        if half is None:
            return self.full.at[pl.ds(pl.multiple_of(base, T), T)]
        return self.full.at[pl.ds(pl.multiple_of(base + half * HALF, HALF), HALF)]

    def push(self, n, src, dst, device):
        remote(src, dst, self.send.at[n], self.recv.at[n], device).start()

    def arrived(self, n, dst):
        remote(dst, dst, self.send.at[n], self.recv.at[n], self.me.sibling()).wait_recv()

    def kept(self, k, other):
        c = 1 - self.me.c if other else self.me.c
        there = self.out.at[pl.ds(pl.multiple_of(self.me.slot(k, c) * T, T), T)]
        return pltpu.make_async_copy(self.block(k, c), there, self.keep.at[2 * k + other])

    def store(self, k, other):
        if self.out is not None:
            self.kept(k, other).start()

    def start(self):
        me = self.me
        right, left = me.z_peer(1), me.z_peer(3)
        mine = self.block(0, me.c)
        a, b = self.block(0, me.c, 0), self.block(0, me.c, 1)
        self.push(0, a, a, right)
        self.push(1, b, b, left)
        self.push(2, b, b, right)
        self.push(3, a, a, left)
        self.push(4, mine, mine, me.sibling())
        self.store(0, 0)

    def forward(self):
        me = self.me
        right, left = me.z_peer(1), me.z_peer(3)
        a, b = self.block(3, me.c, 0), self.block(1, me.c, 1)
        self.arrived(0, a)
        self.push(5, a, a, right)
        self.arrived(1, b)
        self.push(6, b, b, left)

    def hand_over(self, n, k):
        whole = self.block(k, self.me.c)
        self.push(n, whole, whole, self.me.sibling())
        self.store(k, 0)

    def across_left(self):
        self.arrived(2, self.block(3, self.me.c, 1))
        self.hand_over(7, 3)

    def across_right(self):
        self.arrived(3, self.block(1, self.me.c, 0))
        self.hand_over(8, 1)

    def across_far(self):
        self.arrived(5, self.block(2, self.me.c, 0))
        self.arrived(6, self.block(2, self.me.c, 1))
        self.hand_over(9, 2)

    def across(self):
        self.across_left()
        self.across_right()
        self.across_far()

    def taken(self, n, k):
        self.arrived(n, self.block(k, 1 - self.me.c))
        self.store(k, 1)

    def own_pair(self):
        self.taken(4, 0)

    def left_pair(self):
        self.taken(7, 3)

    def right_pair(self):
        self.taken(8, 1)

    def far_pair(self):
        self.taken(9, 2)

    def drain(self):
        for n in range(10):
            part = n in (0, 1, 2, 3, 5, 6)
            size = self.block(0, self.me.c, 0) if part else self.block(0, self.me.c)
            remote(size, size, self.send.at[n], self.recv.at[n], self.me.sibling()).wait_send()
        if self.out is not None:
            for k in range(4):
                self.kept(k, 0).wait()
                self.kept(k, 1).wait()

    def finish(self):
        self.own_pair()
        self.left_pair()
        self.right_pair()
        self.far_pair()
        self.drain()


class Spread:
    sems = 40

    def __init__(self, me, full, rows, send, recv):
        self.me, self.full, self.rows, self.send, self.recv = me, full, rows, send, recv

    def at(self, h, i, j):
        me = self.me
        dx, dy = (i, j) if h == 0 else (j, i)
        return (me.x + dx + 4) % 4 * 4 + (me.y + dy + 4) % 4

    def block(self, h, i, j, q=None):
        half = self.rows // 2
        base = self.at(h, i, j) * self.rows + h * half
        if q is None:
            return self.full.at[pl.ds(pl.multiple_of(base, 16), half)]
        return self.full.at[pl.ds(pl.multiple_of(base + q * (half // 2), 16), half // 2)]

    def push(self, h, n, block, i, j):
        n = 20 * h + n
        remote(block, block, self.send.at[n], self.recv.at[n], self.me.dp_peer(self.at(h, i, j))).start()

    def arrived(self, h, n, block):
        n = 20 * h + n
        remote(block, block, self.send.at[n], self.recv.at[n], self.me.sibling()).wait_recv()

    def second(self, t, i):
        for h in range(2):
            block = self.block(h, i, 0)
            self.push(h, 4 + 4 * t, block, 0, 1)
            self.push(h, 5 + 4 * t, block, 0, -1)

    def start(self):
        for h in range(2):
            block = self.block(h, 0, 0)
            self.push(h, 0, block, 1, 0)
            self.push(h, 1, block, -1, 0)
        self.second(0, 0)

    def turn(self):
        for h in range(2):
            self.arrived(h, 0, self.block(h, -1, 0))
            self.push(h, 2, self.block(h, -1, 0, 0), 1, 0)
            self.arrived(h, 1, self.block(h, 1, 0))
            self.push(h, 3, self.block(h, 1, 0, 1), -1, 0)
        self.second(1, -1)
        self.second(2, 1)

    def far(self):
        for h in range(2):
            self.arrived(h, 2, self.block(h, 2, 0, 0))
            self.arrived(h, 3, self.block(h, 2, 0, 1))
        self.second(3, 2)

    def hand_on(self, t):
        i = (0, -1, 1, 2)[t]
        for h in range(2):
            self.arrived(h, 4 + 4 * t, self.block(h, i, -1))
            self.push(h, 6 + 4 * t, self.block(h, i, -1, 0), 0, 1)
            self.arrived(h, 5 + 4 * t, self.block(h, i, 1))
            self.push(h, 7 + 4 * t, self.block(h, i, 1, 1), 0, -1)

    def finish(self):
        for t, i in enumerate((0, -1, 1, 2)):
            for h in range(2):
                self.arrived(h, 6 + 4 * t, self.block(h, i, 2, 0))
                self.arrived(h, 7 + 4 * t, self.block(h, i, 2, 1))

    def drain(self):
        for h in range(2):
            for n in range(20):
                handed = n in (2, 3) or (n >= 4 and n % 4 >= 2)
                block = self.block(h, 0, 0, 0 if handed else None)
                n = 20 * h + n
                remote(block, block, self.send.at[n], self.recv.at[n], self.me.sibling()).wait_send()


def add_rows(out, at, terms, rows, step=32):
    def body(i, carry):
        here = pl.ds(pl.multiple_of(i * step, step), step)
        total = terms[0](here)
        for term in terms[1:]:
            total = total + term(here)
        there = pl.ds(pl.multiple_of(at + i * step, step), step)
        out[there] = total.astype(out.dtype)
        return carry

    lax.fori_loop(0, rows // step, body, 0)


def reads(ref, start=0):
    def term(here):
        return ref[pl.ds(pl.multiple_of(here.start + start, 16), here.size)].astype(f32)

    return term


class Scatter:
    sems = 10

    @staticmethod
    def scratch(n):
        return [
            VMEM((4, T, n), bf16),
            VMEM((2, HALF, n), bf16),
            VMEM((2, HALF, n), bf16),
            VMEM((4, HALF, n), bf16),
            DMA((10,)),
            DMA((10,)),
        ]

    def __init__(self, me, part, other, through, passed, final, send, recv):
        self.me, self.part = me, part
        self.other, self.through, self.passed, self.final = other, through, passed, final
        self.send, self.recv = send, recv

    def piece(self, k, c):
        return self.part.at[pl.ds(pl.multiple_of(self.me.slot(k, c) * T, T), T)]

    def pair(self, k, q):
        base = self.me.slot(k, self.me.c) * T + q * HALF
        return self.part.at[pl.ds(pl.multiple_of(base, HALF), HALF)]

    def push(self, n, src, dst, device):
        remote(src, dst, self.send.at[n], self.recv.at[n], device).start()

    def arrived(self, n, dst):
        remote(dst, dst, self.send.at[n], self.recv.at[n], self.me.sibling()).wait_recv()

    def start(self):
        me = self.me
        for k in (2, 1, 3, 0):
            self.push(k, self.piece(k, 1 - me.c), self.other.at[k], me.sibling())

    def join(self):
        me = self.me
        right, left = me.z_peer(1), me.z_peer(3)
        for k in (2, 1, 3, 0):
            self.arrived(k, self.other.at[k])
            add_rows(
                self.piece(k, me.c), 0, [reads(self.piece(k, me.c)), reads(self.other.at[k])], T
            )
            if k == 2:
                self.push(4, self.pair(2, 0), self.through.at[0], right)
                self.push(5, self.pair(2, 1), self.through.at[1], left)
            if k == 1:
                self.push(6, self.pair(1, 1), self.final.at[0], right)
            if k == 3:
                self.push(7, self.pair(3, 0), self.final.at[1], left)

    def relay(self):
        me = self.me
        right, left = me.z_peer(1), me.z_peer(3)
        self.arrived(4, self.through.at[0])
        add_rows(self.passed.at[0], 0, [reads(self.through.at[0]), reads(self.pair(1, 0))], HALF)
        self.push(8, self.passed.at[0], self.final.at[2], right)
        self.arrived(5, self.through.at[1])
        add_rows(self.passed.at[1], 0, [reads(self.through.at[1]), reads(self.pair(3, 1))], HALF)
        self.push(9, self.passed.at[1], self.final.at[3], left)

    def finish(self, out, extra=None):
        me = self.me
        for n, k in ((6, 0), (7, 1), (8, 2), (9, 3)):
            self.arrived(n, self.final.at[k])
        more = [] if extra is None else [reads(extra)]
        add_rows(
            out, 0, [reads(self.pair(0, 0)), reads(self.final.at[1]), reads(self.final.at[2])] + more, HALF
        )
        more = [] if extra is None else [reads(extra, HALF)]
        add_rows(
            out,
            HALF,
            [reads(self.pair(0, 1)), reads(self.final.at[0]), reads(self.final.at[3])] + more,
            HALF,
        )
        for n in range(10):
            size = self.other.at[n] if n < 4 else self.final.at[0]
            remote(size, size, self.send.at[n], self.recv.at[n], me.sibling()).wait_send()


class RingSum:
    @staticmethod
    def scratch(shape):
        return [
            VMEM((2, *shape), bf16), VMEM((2, *shape), bf16), VMEM((4, *shape), bf16), DMA((6,)), DMA((6,)),
        ]

    def __init__(self, me, right, left, piece, through, passed, final, send, recv):
        self.me, self.right, self.left, self.piece = me, right, left, piece
        self.through, self.passed, self.final, self.send, self.recv = through, passed, final, send, recv

    def push(self, n, src, dst, device):
        remote(src, dst, self.send.at[n], self.recv.at[n], device).start()

    def arrived(self, n, dst):
        remote(dst, dst, self.send.at[n], self.recv.at[n], self.me.sibling()).wait_recv()

    def start(self):
        self.push(0, self.piece(2, 0), self.through.at[0], self.right)
        self.push(1, self.piece(2, 1), self.through.at[1], self.left)
        self.push(2, self.piece(1, 1), self.final.at[0], self.right)
        self.push(3, self.piece(3, 0), self.final.at[1], self.left)

    def add(self, out, terms):
        count, rows = terms[0].shape[0], terms[0].shape[1]

        def body(i, carry):
            m, here = i // (rows // 16), pl.ds(pl.multiple_of(i % (rows // 16) * 16, 16), 16)
            total = terms[0][m, here].astype(f32)
            for term in terms[1:]:
                total = total + term[m, here].astype(f32)
            out[m, here] = total.astype(out.dtype)
            return carry

        lax.fori_loop(0, count * (rows // 16), body, 0)

    def relay(self):
        self.arrived(0, self.through.at[0])
        self.add(self.passed.at[0], [self.through.at[0], self.piece(1, 0)])
        self.push(4, self.passed.at[0], self.final.at[2], self.right)
        self.arrived(1, self.through.at[1])
        self.add(self.passed.at[1], [self.through.at[1], self.piece(3, 1)])
        self.push(5, self.passed.at[1], self.final.at[3], self.left)

    def finish(self, out):
        for n, k in ((2, 0), (3, 1), (4, 2), (5, 3)):
            self.arrived(n, self.final.at[k])
        self.add(out(0), [self.piece(0, 0), self.final.at[1], self.final.at[2]])
        self.add(out(1), [self.piece(0, 1), self.final.at[0], self.final.at[3]])
        for n in range(6):
            size = self.final.at[0]
            remote(size, size, self.send.at[n], self.recv.at[n], self.me.sibling()).wait_send()


def norm_rows(value, gain):
    return value * lax.rsqrt(jnp.mean(value * value, axis=-1, keepdims=True) + epsilon) * gain


def norm_pull(value, gain, incoming):
    r = lax.rsqrt(jnp.mean(value * value, axis=-1, keepdims=True) + epsilon)
    scaled = incoming * gain
    inner = jnp.mean(value * scaled, axis=-1, keepdims=True)
    normed = value * r
    return r * (scaled - normed * (inner * r)), incoming * normed


CHUNK = 256
STEPS = G // CHUNK
contract_last = (((1,), (1,)), ((), ()))
contract_first = (((0,), (0,)), ((), ()))
gelu_c = 0.7978845608028654
gelu_k = 0.044715


def gelu_parts(v):
    square = v * v
    t = jnp.tanh(gelu_c * (v + gelu_k * square * v))
    half = 0.5 * (1.0 + t)
    slope = half + 0.5 * v * (1.0 - t * t) * (gelu_c * (1.0 + 3.0 * gelu_k * square))
    return v * half, slope


def minus_expm1(z):
    series = -z * (1.0 + z * (1 / 2 + z * (1 / 6 + z * (1 / 24 + z * (1 / 120 + z * (1 / 720))))))
    return jnp.where(z > -0.25, series, 1.0 - jnp.exp(z))


def recur(conv, raw_a, raw_x, terms, start):
    recall = jax.nn.sigmoid(raw_a + terms[5:6])
    admit = jax.nn.sigmoid(raw_x + terms[6:7])
    lograte = terms[7:8] * recall
    decay = jnp.exp(lograte) * (1.0 - start)
    root = jnp.sqrt(minus_expm1(2.0 * lograte))
    scale = start + (1.0 - start) * root
    return recall, admit, lograte, decay, root, scale


def nt(left, right):
    return lax.dot_general(left, right, contract_last, preferred_element_type=f32)


def tn(left, right):
    return lax.dot_general(left, right, contract_first, preferred_element_type=f32)


def nn(left, right):
    return jnp.dot(left, right, preferred_element_type=f32)


def rows_of(base, size):
    return pl.ds(pl.multiple_of(base, 16), size)


def lanes_of(base, size):
    return pl.ds(pl.multiple_of(base, 128), size)


def windows(lab, base):
    return lab[pl.ds(pl.multiple_of(base, 8), CHUNK + 16)]


def same(window, k):
    here = window[8 : 8 + CHUNK, 0:1]
    there = window[8 - k : 8 - k + CHUNK, 0:1]
    return (here == there).astype(f32)


def log_one_plus(x):
    z = x / (2.0 + x)
    s = z * z
    return 2.0 * z * (1.0 + s * (1 / 3 + s * (1 / 5 + s * (1 / 7 + s * (1 / 9 + s * (1 / 11 + s * (1 / 13)))))))


def forward_kernel(
    tok, cot, mixer, feed, numbers, gain_in, gate_in, chan_in,
    cot_out, mix_out, normed_out, x_out, y_out, conv_out, prior_out, mixed_out,
    hidden_out, gu_out, back_out, ff_out, n2_out, gate_out, term_out, gain_out, lab_out, middle,
    mixw, feedw, part, xs, ys, convs, priors, mixeds, hiddens, gus,
    mix, small, gates, chan, small_in, minor, gate_f,
    xpad, dec, drv, sts, carry, *rest,
):
    tg, cg, ng, sc = rest[:4], rest[4:8], rest[8:12], rest[12:18]
    ms, mr, fs, fr, ss, sr, ps, pr, qs, qr, es, er, hs, hr, ls, os = rest[18:]
    me = Place()
    quarter, at = me.dp // 8, me.dp % 8
    gate_to = (8 * quarter + me.sq, at)
    gate_self = me.sq == at
    chan_to = (8 * (me.dp % 2) + me.sq, me.dp // 2)
    chan_from = (2 * me.sq + me.dp // 8, me.dp % 8)
    chan_self = jnp.logical_and(chan_to[0] == me.dp, chan_to[1] == me.sq)
    barrier, count = greet(seq_peers(me) + ring_peers(me))

    @pl.when(jnp.logical_not(gate_self))
    def _():
        pl.semaphore_signal(barrier, inc=1, device_id=gate_to, device_id_type=MESH)

    @pl.when(jnp.logical_not(chan_self))
    def _():
        pl.semaphore_signal(barrier, inc=1, device_id=chan_from, device_id_type=MESH)

    tokg, cotg, n2g = tg[0], cg[0], ng[0]
    own_rows = rows_of(me.dp * T + me.sq * 16, 16)

    def feed_columns(p, j):
        return lanes_of(p * FF + j * FL, FL)

    local = [
        pltpu.make_async_copy(tok, tokg.at[rows_of(me.sq * T, T)], ls.at[0]),
        pltpu.make_async_copy(cot, cotg.at[rows_of(me.sq * T, T)], ls.at[1]),
    ] + [
        pltpu.make_async_copy(feed.at[:, feed_columns(p, me.sq)], feedw.at[own_rows, pl.ds(p * FL, FL)], ls.at[4 + p])
        for p in range(3)
    ]
    for copy in local:
        copy.start()

    for j in range(SEQ):
        for p in range(3):
            value = mixer[:, p * W + j * WL : p * W + (j + 1) * WL]
            mix[j, :, p * WP : (p + 1) * WP] = jnp.concatenate([value, jnp.zeros((16, WP - WL), bf16)], 1)
    row = jnp.concatenate([gain_in[...].astype(f32), jnp.zeros((2, 112), f32)], 1)
    row = pltpu.roll(row, me.sq * 16, 1)
    small[0:16] = jnp.concatenate([row, jnp.zeros((14, 128), f32)], 0).astype(bf16)
    small[16:32] = jnp.concatenate([numbers[...].astype(f32), jnp.zeros((15, 128), f32)], 0).astype(bf16)
    value = gate_in[...].astype(f32)
    value = jnp.where(
        me.sq < 4,
        jnp.concatenate([value, jnp.zeros((40, 256 - BW), f32)], 1),
        jnp.concatenate([jnp.zeros((40, BW - 128), f32), value, jnp.zeros((40, 384 - 2 * BW), f32)], 1),
    )
    for n in range(2):
        half = jnp.concatenate([value[:, n * 128 : n * 128 + 128], jnp.zeros((8, 128), f32)], 0)
        gates[n * 48 : n * 48 + 48] = half.astype(bf16)
    value = jnp.concatenate([chan_in[...].astype(f32), jnp.zeros((8, WP - 20), f32)], 1)
    value = pltpu.roll(value, (8 * (me.dp % 2) + me.sq) * 20, 1)
    for n in range(3):
        part_rows = jnp.concatenate([value[:, n * 128 : n * 128 + 128], jnp.zeros((8, 128), f32)], 0)
        chan[n * 16 : n * 16 + 16] = part_rows.astype(bf16)
    mixw[own_rows] = mix[me.sq]
    small_in[me.sq] = small[...]

    pl.semaphore_wait(barrier, count + jnp.where(gate_self, 0, 1) + jnp.where(chan_self, 0, 1))

    sent = []

    def push(src, dst, send, recv, device):
        sent.append(remote(src, dst, send, recv, device))
        sent[-1].start()

    def arrived(dst, send, recv):
        remote(dst, dst, send, recv, me.sibling()).wait_recv()

    order = (4, 3, 5, 2, 6, 1, 7)
    for k in order:
        to = (me.sq + k) % SEQ
        push(mix.at[to], mixw.at[own_rows], ms.at[k], mr.at[k], me.seq_peer(k))
        push(small, small_in.at[me.sq], ss.at[k], sr.at[k], me.seq_peer(k))

    def minor_rows(dp, start, size):
        return minor.at[rows_of(dp * MINOR + start, size)]

    gate_copy = remote(gates, minor_rows(gate_to[0], 16, 96), hs.at[0], hr.at[0], gate_to)
    chan_copy = remote(chan, minor_rows(chan_to[0], 112, 48), hs.at[1], hr.at[1], chan_to)
    gate_local = pltpu.make_async_copy(gates, minor_rows(me.dp, 16, 96), ls.at[7])
    chan_local = pltpu.make_async_copy(chan, minor_rows(me.dp, 112, 48), ls.at[8])
    gate_here = remote(gates, minor_rows(me.dp, 16, 96), hs.at[0], hr.at[0], gate_to)
    chan_here = remote(chan, minor_rows(me.dp, 112, 48), hs.at[1], hr.at[1], chan_to)

    @pl.when(jnp.logical_not(gate_self))
    def _():
        gate_copy.start()

    @pl.when(gate_self)
    def _():
        gate_local.start()

    @pl.when(jnp.logical_not(chan_self))
    def _():
        chan_copy.start()

    @pl.when(chan_self)
    def _():
        chan_local.start()

    local[0].wait()
    tokens = Gather(me, None, None, *tg)
    tokens.start()
    for k in order:
        to = (me.sq + k) % SEQ
        for p in range(3):
            push(feed.at[:, feed_columns(p, to)], feedw.at[own_rows, pl.ds(p * FL, FL)],
                 fs.at[p, k], fr.at[p, k], me.seq_peer(k))
    for copy in local[1:]:
        copy.wait()

    def seq_rows(k):
        return rows_of(me.dp * T + (me.sq - k + SEQ) % SEQ * 16, 16)

    mixes = Spread(me, mixw, T, ps, pr)
    feeds = Spread(me, feedw, T, qs, qr)
    minors = Spread(me, minor, MINOR, es, er)

    for k in range(1, SEQ):
        arrived(small_in.at[(me.sq - k + SEQ) % SEQ], ss.at[k], sr.at[k])
    gain = small_in[0, 0:16].astype(f32)
    for k in range(1, SEQ):
        gain = gain + small_in[k, 0:16].astype(f32)
    minor[rows_of(me.dp * MINOR, 16)] = gain.astype(bf16)
    minor[rows_of(me.dp * MINOR + 160, 32)] = jnp.zeros((32, 128), bf16)

    @pl.when(jnp.logical_not(gate_self))
    def _():
        gate_copy.wait_send()
        gate_here.wait_recv()

    @pl.when(gate_self)
    def _():
        gate_local.wait()

    @pl.when(jnp.logical_not(chan_self))
    def _():
        chan_copy.wait_send()
        chan_here.wait_recv()

    @pl.when(chan_self)
    def _():
        chan_local.wait()

    minors.start()
    for k in range(1, SEQ):
        arrived(mixw.at[seq_rows(k)], ms.at[k], mr.at[k])
    mixes.start()
    tokens.forward()

    lab_out[0:8] = jnp.full((8, 128), -1.0, f32)
    lab_out[G + 8 :] = jnp.full((8, 128), -2.0, f32)
    for k in range(SEQ):
        row = small_in[k, 16:32].astype(f32)[0:1]
        lab_out[8 + k * T : 8 + (k + 1) * T] = jnp.broadcast_to(row, (128, 128)).T

    minors.turn()
    mixes.turn()
    cots = Gather(me, None, cot_out, *cg)
    cots.start()
    minors.far()
    mixes.far()
    tokens.across_left()
    tokens.across_right()
    for t in range(4):
        minors.hand_on(t)
    mixes.hand_on(0)
    tokens.across_far()
    minors.finish()
    for k in range(DP):
        gain_out[:, k * 128 : (k + 1) * 128] = minor[k * MINOR : k * MINOR + 16].astype(f32)[0:8]

    def normed_copy(k, other):
        c = 1 - me.c if other else me.c
        rows = rows_of(me.slot(k, c) * T, T)
        return pltpu.make_async_copy(part.at[rows], normed_out.at[rows], os.at[23 + 2 * k + other])

    def normalise(k, other):
        base = me.slot(k, 1 - me.c if other else me.c) * T

        def body(i, c):
            here = rows_of(base + i * 16, 16)
            part[here] = norm_rows(tokg[here].astype(f32), gain_out[0:1]).astype(bf16)
            return c

        lax.fori_loop(0, T // 16, body, 0)
        normed_copy(k, other).start()

    normalise(0, 0)
    tokens.own_pair()
    normalise(0, 1)
    mixes.hand_on(1)
    mixes.hand_on(2)
    normalise(3, 0)
    normalise(1, 0)
    tokens.left_pair()
    normalise(3, 1)
    tokens.right_pair()
    normalise(1, 1)
    mixes.hand_on(3)
    for k in range(1, SEQ):
        for p in range(3):
            arrived(feedw.at[seq_rows(k), pl.ds(p * FL, FL)], fs.at[p, k], fr.at[p, k])
    feeds.start()
    normalise(2, 0)
    tokens.far_pair()
    normalise(2, 1)
    tokens.drain()
    terms = minor[112:160].astype(f32)
    for k in range(1, DP):
        terms = terms + minor[k * MINOR + 112 : k * MINOR + 160].astype(f32)
    for n in range(3):
        group = terms[16 * n : 16 * n + 16]
        lanes = slice(128 * n, 128 * n + 128)
        term_out[:, lanes] = group
        lam = group[7:8]
        small_exp = jnp.exp(-jnp.abs(lam))
        term_out[7:8, lanes] = -rate_scale * (jnp.maximum(-lam, 0.0) + log_one_plus(small_exp))
        term_out[8:9, lanes] = rate_scale * jax.nn.sigmoid(-lam)
    gate_f[...] = jnp.zeros(gate_f.shape, f32)
    for k in range(DP):
        base = k // 8 * WP + k % 8 * 40
        for n in range(2):
            lanes = k % 8 // 4 * 128 + n * 128
            start = k * MINOR + 16 + 48 * n
            gate_f[base : base + 40, lanes : lanes + 128] = minor[start : start + 48].astype(f32)[0:40]
    gate_out[0] = gate_f[:WP].astype(bf16)
    gate_out[1] = gate_f[WP:].astype(bf16)
    for k in range(4):
        normed_copy(k, 0).wait()
        normed_copy(k, 1).wait()
    mixes.finish()
    writes = [pltpu.make_async_copy(mixw, mix_out, os.at[1])]
    writes[0].start()

    xpad[0:8] = jnp.zeros((8, WP), f32)
    carry[...] = jnp.zeros((8, WP), f32)
    row = lax.broadcasted_iota(jnp.int32, (8, WP), 0)

    def mix_chunk(step, c):
        @pl.when(step == 1)
        def _():
            cots.forward()
            feeds.turn()

        @pl.when(step == 2)
        def _():
            feeds.far()

        @pl.when(step == 3)
        def _():
            cots.across()
            feeds.hand_on(0)

        base = step * CHUNK
        rows = rows_of(base, CHUNK)
        both = nn(part[rows], mixw[:, : 2 * WP])
        x, y = both[:, :WP], both[:, WP:]
        xs[rows] = x
        ys[rows] = y
        xpad[8:] = x
        terms = term_out[...]
        window = windows(lab_out, base)
        start = 1.0 - same(window, 1)
        conv = terms[4:5] + terms[0:1] * x
        for k in range(1, CONV):
            conv = conv + terms[k : k + 1] * (same(window, k) * xpad[8 - k : 8 - k + CHUNK])
        xpad[0:8] = x[CHUNK - 8 :]
        convs[rows] = conv
        lowered = conv.astype(bf16)
        raw_a, raw_x = nn(lowered, gate_out[0]), nn(lowered, gate_out[1])
        recall, admit, lograte, decay, root, scale = recur(conv, raw_a, raw_x, terms, start)
        dec[...] = decay
        drv[...] = scale * admit * conv

        def scan(i, before):
            here = pl.ds(pl.multiple_of(i * 8, 8), 8)
            a, b = dec[here], drv[here]
            for s in (1, 2, 4):
                b = b + a * jnp.where(row >= s, pltpu.roll(b, s, 0), 0.0)
                a = a * jnp.where(row >= s, pltpu.roll(a, s, 0), 1.0)
            state = b + a * before
            sts[here] = state
            priors[pl.ds(pl.multiple_of(base + i * 8, 8), 8)] = jnp.where(row >= 1, pltpu.roll(state, 1, 0), before)
            return jnp.broadcast_to(state[7:8], (8, WP))

        carry[...] = lax.fori_loop(0, CHUNK // 8, scan, carry[...], unroll=4)
        value, _ = gelu_parts(ys[rows])
        mixed = (value * sts[...]).astype(bf16)
        mixeds[rows] = mixed
        part[rows] = nt(mixed, mixw[:, 2 * WP :]).astype(bf16)
        return c

    lax.fori_loop(0, STEPS, mix_chunk, 0)

    total = Scatter(me, part, *sc)
    total.start()
    for n, (src, dst) in enumerate(((xs, x_out), (ys, y_out), (convs, conv_out), (priors, prior_out), (mixeds, mixed_out))):
        writes.append(pltpu.make_async_copy(src, dst, os.at[2 + n]))
        writes[-1].start()
    total.join()
    feeds.hand_on(1)
    feeds.hand_on(2)
    total.relay()
    feeds.hand_on(3)
    total.finish(middle, tok)

    def second_norm(i, c):
        here = pl.ds(pl.multiple_of(i * 16, 16), 16)
        n2g[rows_of(me.sq * T + i * 16, 16)] = norm_rows(middle[here], gain_out[1:2]).astype(bf16)
        return c

    lax.fori_loop(0, T // 16, second_norm, 0)
    seconds = Gather(me, None, n2_out, *ng)
    seconds.start()
    cots.finish()
    feeds.finish()

    def feed_chunk(k, n):
        rows = rows_of(me.chip(k) * CHUNK, CHUNK)
        gu = nn(n2g[rows], feedw[:, : 2 * FL])
        gate, up = gu[:, :FL], gu[:, FL:]
        adj_hidden = nn(cotg[rows], feedw[:, 2 * FL :])
        value, slope = gelu_parts(gate)
        hidden = (value * up).astype(bf16)
        hiddens[rows] = hidden
        gus[rows, :FL] = (adj_hidden * up * slope).astype(bf16)
        gus[rows, FL:] = (adj_hidden * value).astype(bf16)
        tokg[rows] = nt(hidden, feedw[:, 2 * FL :]).astype(bf16)
        part[rows] = nt(gus[rows], feedw[:, : 2 * FL]).astype(bf16)

    def feed_store(k, n):
        rows = rows_of(me.chip(k) * CHUNK, CHUNK)
        for m, (src, dst) in enumerate(((hiddens, hidden_out), (gus, gu_out), (tokg, ff_out), (part, back_out))):
            writes.append(pltpu.make_async_copy(src.at[rows], dst.at[rows], os.at[7 + 4 * n + m]))
            writes[-1].start()

    seconds.own_pair()
    feed_chunk(0, 0)
    feed_store(0, 0)
    seconds.forward()
    seconds.across_left()
    seconds.across_right()
    seconds.left_pair()
    feed_chunk(3, 1)
    feed_store(3, 1)
    seconds.across_far()
    seconds.right_pair()
    feed_chunk(1, 2)
    feed_store(1, 2)
    seconds.far_pair()
    feed_chunk(2, 3)
    feed_store(2, 3)
    seconds.drain()
    for copy in writes:
        copy.wait()
    for copy in sent:
        copy.wait_send()
    mixes.drain()
    minors.drain()
    feeds.drain()


def forward_call(tok, cot, mixer, feed, numbers, gain, gates, chan):
    sds = jax.ShapeDtypeStruct
    hbm, vmem = pl.BlockSpec(memory_space=ANY), pl.BlockSpec(memory_space=VMEM)
    return pl.pallas_call(
        forward_kernel,
        out_shape=(
            sds((G, D), bf16), sds((D, MW), bf16), sds((G, D), bf16),
            sds((G, WP), f32), sds((G, WP), f32), sds((G, WP), f32), sds((G, WP), f32), sds((G, WP), bf16),
            sds((G, FL), bf16), sds((G, 2 * FL), bf16), sds((G, D), bf16), sds((G, D), bf16), sds((G, D), bf16),
            sds((2, WP, WP), bf16), sds((16, WP), f32), sds((8, D), f32), sds((G + 16, 128), f32), sds((T, D), f32),
        ),
        in_specs=[vmem, hbm, vmem, hbm, vmem, vmem, vmem, vmem],
        out_specs=[hbm] * 13 + [vmem] * 5,
        scratch_shapes=[
            VMEM((D, MW), bf16), VMEM((D, FW), bf16), VMEM((G, D), bf16),
            VMEM((G, WP), f32), VMEM((G, WP), f32), VMEM((G, WP), f32), VMEM((G, WP), f32), VMEM((G, WP), bf16),
            VMEM((G, FL), bf16), VMEM((G, 2 * FL), bf16),
            VMEM((SEQ, 16, MW), bf16), VMEM((32, 128), bf16), VMEM((96, 128), bf16), VMEM((48, 128), bf16),
            VMEM((SEQ, 32, 128), bf16), VMEM((DP * MINOR, 128), bf16), VMEM((2 * WP, WP), f32),
            VMEM((CHUNK + 8, WP), f32), VMEM((CHUNK, WP), f32), VMEM((CHUNK, WP), f32), VMEM((CHUNK, WP), f32),
            VMEM((8, WP), f32),
            *Gather.scratch(D), *Gather.scratch(D), *Gather.scratch(D), *Scatter.scratch(D),
            DMA((SEQ,)), DMA((SEQ,)), DMA((3, SEQ)), DMA((3, SEQ)), DMA((SEQ,)), DMA((SEQ,)),
            DMA((40,)), DMA((40,)), DMA((40,)), DMA((40,)), DMA((40,)), DMA((40,)),
            DMA((2,)), DMA((2,)), DMA((9,)), DMA((31,)),
        ],
        compiler_params=pltpu.CompilerParams(collective_id=1, has_side_effects=True, vmem_limit_bytes=(63 << 20) + (900 << 10)),
        cost_estimate=pl.CostEstimate(flops=30 * G * D * WP, bytes_accessed=100 << 20, transcendentals=0),
        name="forward",
    )(tok, cot, mixer, feed, numbers, gain, gates, chan)


def turn_kernel(
    back_in, ff_in, n2_in, cot_in, hid_in, gu_in, x_in, y_in, conv_in, prior_in, w_in,
    middle, cot, gains, gates, terms_ref, lab,
    adj_all, s1_out, both_out, part_out, adj_middle, act, gain_grad, extra,
    part, ffp, mg, s1, both, dec, adjs, acp, carry, gate_grad, sums, *rest,
):
    one, two, gathering, ring_a, ring_b = rest[:6], rest[6:12], rest[12:16], rest[16:21], rest[21:26]
    ls, os = rest[26:]
    me = Place()
    first = [pltpu.make_async_copy(back_in, part, ls.at[0]), pltpu.make_async_copy(ff_in, ffp, ls.at[1])]
    first[0].start()
    barrier, count = greet(z_peers(me) + ring_peers(me))
    pl.semaphore_wait(barrier, count)
    xs, ys = (me.dp_peer(me.x_dp(1)), me.dp_peer(me.x_dp(3))), (me.dp_peer(me.y_dp(1)), me.dp_peer(me.y_dp(3)))
    upper = RingSum(
        me, *ys, lambda k, q: mg.at[:, (me.y + k) % 4, pl.ds(q * 32, 32)], *ring_a
    )
    lower = RingSum(
        me, *xs, lambda k, q: mg.at[(me.x + k) % 4, :, pl.ds(HALF + q * 32, 32)], *ring_b
    )
    mine = me.sq * T

    def grads(n2, cots, gu, hid):
        loads = [
            pltpu.make_async_copy(src, dst, ls.at[2 + n])
            for n, (src, dst) in enumerate(((n2_in, n2), (cot_in, cots), (gu_in, gu), (hid_in, hid)))
        ]
        first[0].wait()
        inner = Scatter(me, part, *one)
        inner.start()
        for copy in loads:
            copy.start()
        first[1].start()
        inner.join()
        for copy in loads:
            copy.wait()

        def tile(i, c):
            here = pl.ds(pl.multiple_of(i * 256, 256), 256)
            left = tn(n2[:, here], gu[...]).astype(bf16)
            right = tn(cots[:, here], hid[...]).astype(bf16)
            for h in range(2):
                mg[i // 2, i % 2 * 2 + h, :, : 2 * FL] = left[h * T : (h + 1) * T]
                mg[i // 2, i % 2 * 2 + h, :, 2 * FL :] = right[h * T : (h + 1) * T]

            @pl.when(i == 3)
            def _():
                inner.relay()

            return c

        lax.fori_loop(0, 8, tile, 0)
        upper.start()
        lower.start()
        inner.finish(adj_middle)

    pl.run_scoped(grads, VMEM((G, D), bf16), VMEM((G, D), bf16), VMEM((G, 2 * FL), bf16), VMEM((G, FL), bf16))

    def pull(i, c):
        here = pl.ds(pl.multiple_of(i * 16, 16), 16)
        pulled, terms = norm_pull(middle[here], gains[1:2], adj_middle[here])
        value = cot[here].astype(f32) + pulled
        adj_middle[here] = value
        gathering[0][rows_of(mine + i * 16, 16)] = value.astype(bf16)
        return c + jnp.sum(terms, axis=0, keepdims=True)

    gain_grad[...] = lax.fori_loop(0, T // 16, pull, jnp.zeros((1, D), f32))
    gather = Gather(me, None, adj_all, *gathering)
    gather.start()
    first[1].wait()
    outer = Scatter(me, ffp, *two)

    def unmix(x_all, y_all, conv_all, prior_all, w):
        loads = [
            pltpu.make_async_copy(src, dst, ls.at[2 + n])
            for n, (src, dst) in enumerate(
                ((x_in, x_all), (y_in, y_all), (conv_in, conv_all), (prior_in, prior_all), (w_in, w))
            )
        ]
        for copy in loads:
            copy.start()
        gather.forward()
        upper.relay()
        lower.relay()
        gather.across()
        dec[CHUNK:] = jnp.zeros((8, WP), f32)
        acp[CHUNK:] = jnp.zeros((8, WP), f32)
        carry[...] = jnp.zeros((8, WP), f32)
        gate_grad[...] = jnp.zeros(gate_grad.shape, f32)
        sums[...] = jnp.zeros(sums.shape, f32)
        for copy in loads:
            copy.wait()
        gather.finish()
        outer.start()
        row = lax.broadcasted_iota(jnp.int32, (8, WP), 0)

        def chunk(step, c):
            @pl.when(step == 1)
            def _():
                outer.join()

            @pl.when(step == 3)
            def _():
                outer.relay()

            base = (STEPS - 1 - step) * CHUNK
            rows = rows_of(base, CHUNK)
            window = windows(lab, base)
            terms = terms_ref[...]
            start = 1.0 - same(window, 1)
            conv, prior = conv_all[rows], prior_all[rows]
            lowered = conv.astype(bf16)
            raw_a, raw_x = nn(lowered, gates[0]), nn(lowered, gates[1])
            recall, admit, lograte, decay, root, scale = recur(conv, raw_a, raw_x, terms, start)
            dec[0:CHUNK] = decay
            states = decay * prior + scale * admit * conv
            adj_mixed = nn(gathering[0][rows], w[:, 2 * WP :])
            value, slope = gelu_parts(y_all[rows])
            adjs[...] = adj_mixed * value
            both[rows, WP:] = (adj_mixed * states * slope).astype(bf16)

            def scan(i, after):
                at = pl.multiple_of((CHUNK // 8 - 1 - i) * 8, 8)
                here = pl.ds(at, 8)
                later = dec[pl.ds(pl.multiple_of(at + 8, 8), 8)]
                a = jnp.where(row < 7, pltpu.roll(dec[here], 7, 0), later[0:1])
                b = adjs[here]
                for s in (1, 2, 4):
                    b = b + a * jnp.where(row < 8 - s, pltpu.roll(b, 8 - s, 0), 0.0)
                    a = a * jnp.where(row < 8 - s, pltpu.roll(a, 8 - s, 0), 1.0)
                value = b + a * after
                adjs[here] = value
                return jnp.broadcast_to(value[0:1], (8, WP))

            carry[...] = lax.fori_loop(0, CHUNK // 8, scan, carry[...], unroll=4)
            adjoint = adjs[...]
            flow = adjoint * admit * conv
            adj_lograte = adjoint * prior * decay - (1.0 - start) * flow * (jnp.exp(2.0 * lograte) / root)
            adj_ra = adj_lograte * terms[7:8] * (recall * (1.0 - recall))
            adj_rx = flow * scale * (1.0 - admit)

            def total(v):
                return jnp.sum(v, axis=0, keepdims=True)

            sums[5:6] += total(adj_ra)
            sums[6:7] += total(adj_rx)
            sums[7:8] += total(adj_lograte * recall) * terms[8:9]
            low_a, low_x = adj_ra.astype(bf16), adj_rx.astype(bf16)
            adj_conv = adjoint * scale * admit + nt(low_a, gates[0]) + nt(low_x, gates[1])
            gate_grad[0] += tn(lowered, low_a)
            gate_grad[1] += tn(lowered, low_x)
            acp[0:CHUNK] = adj_conv
            x = x_all[rows]
            adj_x = terms[0:1] * adj_conv
            sums[4:5] += total(adj_conv)
            sums[0:1] += total(adj_conv * x)
            for k in range(1, CONV):
                moved = same(window, -k) * acp[k : k + CHUNK]
                adj_x = adj_x + terms[k : k + 1] * moved
                sums[k : k + 1] += total(moved * x)
            dec[CHUNK:] = dec[0:8]
            acp[CHUNK:] = acp[0:8]
            both[rows, :WP] = adj_x.astype(bf16)
            part[rows] = nt(both[rows], w[:, : 2 * WP]).astype(bf16)
            return c

        lax.fori_loop(0, STEPS, chunk, 0)

    wide = VMEM((G, WP), f32)
    pl.run_scoped(unmix, wide, wide, wide, wide, VMEM((D, MW), bf16))
    writes = [pltpu.make_async_copy(part, part_out, os.at[0]), pltpu.make_async_copy(both, both_out, os.at[1])]
    for copy in writes:
        copy.start()
    for k in range(DP):
        rows = slice(k % 8 * 40, k % 8 * 40 + 40)
        for n in range(2):
            lanes = slice(k % 8 // 4 * 128 + n * 128, k % 8 // 4 * 128 + n * 128 + 128)
            piece = jnp.concatenate([gate_grad[k // 8, rows, lanes], jnp.zeros((8, 128), f32)], 0)
            extra[k, 48 * n : 48 * n + 48] = piece.astype(bf16)
            lanes = slice(channel_window(k) + n * 128, channel_window(k) + n * 128 + 128)
            piece = jnp.concatenate([sums[:, lanes], jnp.zeros((8, 128), f32)], 0)
            extra[k, 96 + 16 * n : 112 + 16 * n] = piece.astype(bf16)
    upper.finish(lambda q: s1.at[0, :, pl.ds(q * 32, 32)])
    lower.finish(lambda q: s1.at[1, :, pl.ds(q * 32, 32)])
    writes.append(pltpu.make_async_copy(s1, s1_out, os.at[2]))
    writes[2].start()
    outer.finish(act, middle)
    for copy in writes:
        copy.wait()


def channel_window(k):
    return min(k * 20 // 128, 1) * 128


def turn_call(back, ff, n2, cots, hid, gu, saved, w, middle, cot, gains, gates, terms, lab):
    sds = jax.ShapeDtypeStruct
    hbm, vmem = pl.BlockSpec(memory_space=ANY), pl.BlockSpec(memory_space=VMEM)
    return pl.pallas_call(
        turn_kernel,
        out_shape=(
            sds((G, D), bf16), sds((2, 4, HALF, FW), bf16), sds((G, 2 * WP), bf16), sds((G, D), bf16),
            sds((T, D), f32), sds((T, D), bf16), sds((1, D), f32), sds((DP, 128, 128), bf16),
        ),
        in_specs=[hbm] * 11 + [vmem] * 6,
        out_specs=[hbm] * 4 + [vmem] * 4,
        scratch_shapes=[
            VMEM((G, D), bf16), VMEM((G, D), bf16), VMEM((4, 4, T, FW), bf16),
            VMEM((2, 4, HALF, FW), bf16), VMEM((G, 2 * WP), bf16),
            VMEM((CHUNK + 8, WP), f32), VMEM((CHUNK, WP), f32), VMEM((CHUNK + 8, WP), f32), VMEM((8, WP), f32),
            VMEM((2, WP, WP), f32), VMEM((8, WP), f32),
            *Scatter.scratch(D), *Scatter.scratch(D), *Gather.scratch(D),
            *RingSum.scratch((4, 32, FW)), *RingSum.scratch((4, 32, FW)), DMA((8,)), DMA((3,)),
        ],
        compiler_params=pltpu.CompilerParams(collective_id=2, has_side_effects=True, vmem_limit_bytes=(63 << 20) + (900 << 10)),
        cost_estimate=pl.CostEstimate(flops=30 * G * D * WP, bytes_accessed=100 << 20, transcendentals=0),
        name="turn",
    )(back, ff, n2, cots, hid, gu, *saved, w, middle, cot, gains, gates, terms, lab)


def close_kernel(
    part_in, normed_in, both_in, adj_in, mixed_in, extra_in, s1_in, tok, adj_middle, gains, gain_two,
    in_grad, mix_out, feed_out, gate_out, chan_out, gain_out,
    part, normed, both, adj_out, mixed, mg, s1f, s1, lastf, last, adj, gp, gp_in, gain_sum, gain_in, *rest,
):
    one, fa, fb, ma, mb, na, nb = rest[:6], *(rest[6 + 5 * n : 11 + 5 * n] for n in range(6))
    m3s, m3r, f3s, f3r, gs, gr, hs, hr, qs, qr, ls, ws = rest[36:]
    me = Place()
    loads = [
        pltpu.make_async_copy(src, dst, ws.at[n])
        for n, (src, dst) in enumerate(
            ((part_in, part), (s1_in, s1f), (normed_in, normed), (both_in, both), (adj_in, adj_out),
             (mixed_in, mixed), (extra_in, mg.at[:, :, :, pl.ds(MW, 128)]))
        )
    ]
    for copy in loads:
        copy.start()
    quarter, at = me.dp // 8, me.dp % 8
    gate_to = (8 * quarter + me.sq, at)
    gate_self = me.sq == at
    chan_from = (8 * (me.dp % 2) + me.sq, me.dp // 2)
    chan_to = (2 * me.sq + me.dp // 8, me.dp % 8)
    chan_self = jnp.logical_and(chan_from[0] == me.dp, chan_from[1] == me.sq)
    barrier, count = greet(seq_peers(me) + dp_peers(me))

    @pl.when(jnp.logical_not(gate_self))
    def _():
        pl.semaphore_signal(barrier, inc=1, device_id=gate_to, device_id_type=MESH)

    @pl.when(jnp.logical_not(chan_self))
    def _():
        pl.semaphore_signal(barrier, inc=1, device_id=chan_from, device_id_type=MESH)

    pl.semaphore_wait(barrier, count + jnp.where(gate_self, 0, 1) + jnp.where(chan_self, 0, 1))

    sent = []

    def push(src, dst, send, recv, device):
        sent.append(remote(src, dst, send, recv, device))
        sent[-1].start()

    def arrived(dst, send, recv):
        remote(dst, dst, send, recv, me.sibling()).wait_recv()

    xs, ys = (me.dp_peer(me.x_dp(1)), me.dp_peer(me.x_dp(3))), (me.dp_peer(me.y_dp(1)), me.dp_peer(me.y_dp(3)))
    feed_up = RingSum(me, *xs, lambda k, q: s1f.at[0, pl.ds((me.x + k) % 4, 1), pl.ds(q * 32, 32)], *fa)
    feed_low = RingSum(me, *ys, lambda k, q: s1f.at[1, pl.ds((me.y + k) % 4, 1), pl.ds(q * 32, 32)], *fb)
    mix_up = RingSum(me, *ys, lambda k, q: mg.at[:, (me.y + k) % 4, pl.ds(q * 32, 32)], *ma)
    mix_low = RingSum(me, *xs, lambda k, q: mg.at[(me.x + k) % 4, :, pl.ds(HALF + q * 32, 32)], *mb)
    last_up = RingSum(me, *xs, lambda k, q: s1.at[0, pl.ds((me.x + k) % 4, 1), pl.ds(q * 32, 32)], *na)
    last_low = RingSum(me, *ys, lambda k, q: s1.at[1, pl.ds((me.y + k) % 4, 1), pl.ds(q * 32, 32)], *nb)

    inner = Scatter(me, part, *one)
    loads[0].wait()
    inner.start()
    loads[1].wait()
    feed_up.start()
    feed_low.start()
    inner.join()
    for copy in loads[2:]:
        copy.wait()

    def tile(i, carry):
        here = pl.ds(pl.multiple_of(i * 256, 256), 256)
        left = tn(normed[:, here], both[...]).astype(bf16)
        right = tn(adj_out[:, here], mixed[...]).astype(bf16)
        for h in range(2):
            mg[i // 2, i % 2 * 2 + h, :, : 2 * WP] = left[h * T : (h + 1) * T]
            mg[i // 2, i % 2 * 2 + h, :, 2 * WP : MW] = right[h * T : (h + 1) * T]

        @pl.when(i == 4)
        def _():
            inner.relay()
            feed_up.relay()
            feed_low.relay()

        return carry

    lax.fori_loop(0, 8, tile, 0)
    mix_up.start()
    mix_low.start()
    inner.finish(adj)

    def pull(i, carry):
        here = pl.ds(pl.multiple_of(i * 16, 16), 16)
        pulled, terms = norm_pull(tok[here].astype(f32), gains[0:1], adj[here])
        in_grad[here] = adj_middle[here] + pulled
        return carry + jnp.sum(terms, axis=0, keepdims=True)

    gain_one = lax.fori_loop(0, T // 16, pull, jnp.zeros((1, D), f32))
    gp[...] = jnp.zeros(gp.shape, f32)
    for k in range(DP):
        gp[k, 0:1] = gain_one[:, k * 128 : (k + 1) * 128]
        gp[k, 1:2] = gain_two[:, k * 128 : (k + 1) * 128]
    for k in range(1, DP):
        to = (me.dp + k) % DP
        push(gp.at[to], gp_in.at[k], gs.at[k], gr.at[k], me.dp_peer(to))

    feed_up.finish(lambda q: lastf.at[:, pl.ds(q * 32, 32)])
    feed_low.finish(lambda q: lastf.at[:, pl.ds(HALF + q * 32, 32)])

    def feed_columns(p, j):
        return lanes_of(p * FF + j * FL, FL)

    keeps = [
        pltpu.make_async_copy(
            lastf.at[0, rows_of(me.sq * 16, 16), pl.ds(p * FL, FL)], feed_out.at[:, feed_columns(p, me.sq)], ls.at[p]
        )
        for p in range(3)
    ]
    for copy in keeps:
        copy.start()
    order = (4, 3, 5, 2, 6, 1, 7)
    for k in order:
        to = (me.sq + k) % SEQ
        for p in range(3):
            push(lastf.at[0, rows_of(to * 16, 16), pl.ds(p * FL, FL)], feed_out.at[:, feed_columns(p, me.sq)],
                 f3s.at[p, k], f3r.at[p, k], me.seq_peer(k))

    mix_up.relay()
    mix_low.relay()

    for k in range(1, DP):
        arrived(gp_in.at[k], gs.at[k], gr.at[k])

    def sum_gains(k, total):
        return total + gp_in[k]

    gain_sum[...] = lax.fori_loop(1, DP, sum_gains, gp[me.dp])
    for k in range(1, SEQ):
        push(gain_sum, gain_in.at[k], qs.at[k], qr.at[k], me.seq_peer(k))

    mix_up.finish(lambda q: s1.at[0, :, pl.ds(q * 32, 32)])
    last_up.start()
    mix_low.finish(lambda q: s1.at[1, :, pl.ds(q * 32, 32)])
    last_low.start()
    for k in range(1, SEQ):
        arrived(gain_in.at[k], qs.at[k], qr.at[k])
    total = gain_sum[...]
    for k in range(1, SEQ):
        total = total + gain_in[k]
    gain_out[...] = total
    last_up.relay()
    last_low.relay()
    last_up.finish(lambda q: last.at[:, pl.ds(q * 32, 32)])
    last_low.finish(lambda q: last.at[:, pl.ds(HALF + q * 32, 32)])

    columns = pl.ds(0, MW)
    keeps.append(pltpu.make_async_copy(last.at[0, rows_of(me.sq * 16, 16), columns], mix_out.at[me.sq], ls.at[3]))
    keeps[-1].start()
    for k in order:
        to = (me.sq + k) % SEQ
        push(last.at[0, rows_of(to * 16, 16), columns], mix_out.at[me.sq], m3s.at[k], m3r.at[k], me.seq_peer(k))
    gate_sum, chan_sum = last.at[0, pl.ds(0, 96), pl.ds(MW, 128)], last.at[0, pl.ds(96, 32), pl.ds(MW, 128)]
    gate_copy = remote(gate_sum, gate_out, hs.at[0], hr.at[0], gate_to)
    chan_copy = remote(chan_sum, chan_out, hs.at[1], hr.at[1], chan_to)
    gate_local = pltpu.make_async_copy(gate_sum, gate_out, ls.at[4])
    chan_local = pltpu.make_async_copy(chan_sum, chan_out, ls.at[5])

    @pl.when(jnp.logical_not(gate_self))
    def _():
        gate_copy.start()

    @pl.when(gate_self)
    def _():
        gate_local.start()

    @pl.when(jnp.logical_not(chan_self))
    def _():
        chan_copy.start()

    @pl.when(chan_self)
    def _():
        chan_local.start()

    for k in range(1, SEQ):
        source = (me.sq - k + SEQ) % SEQ
        for p in range(3):
            arrived(feed_out.at[:, feed_columns(p, source)], f3s.at[p, k], f3r.at[p, k])
        arrived(mix_out.at[source], m3s.at[k], m3r.at[k])

    @pl.when(jnp.logical_not(gate_self))
    def _():
        gate_copy.wait()

    @pl.when(gate_self)
    def _():
        gate_local.wait()

    @pl.when(jnp.logical_not(chan_self))
    def _():
        chan_copy.wait()

    @pl.when(chan_self)
    def _():
        chan_local.wait()

    for copy in keeps:
        copy.wait()
    for copy in sent:
        copy.wait_send()


def close_call(part, normed, both, adj_out, mixed, extra, s1, tok, adj_middle, gains, gain_two):
    sds = jax.ShapeDtypeStruct
    hbm, vmem = pl.BlockSpec(memory_space=ANY), pl.BlockSpec(memory_space=VMEM)
    wide = MW + 128
    return pl.pallas_call(
        close_kernel,
        out_shape=(
            sds((T, D), f32), sds((SEQ, 16, MW), bf16), sds((16, 3 * FF), bf16),
            sds((96, 128), bf16), sds((32, 128), bf16), sds((8, 128), f32),
        ),
        in_specs=[hbm] * 7 + [vmem] * 4,
        out_specs=[vmem] * 6,
        scratch_shapes=[
            VMEM((G, D), bf16), VMEM((G, D), bf16), VMEM((G, 2 * WP), bf16), VMEM((G, D), bf16), VMEM((G, WP), bf16),
            VMEM((4, 4, T, wide), bf16), VMEM((2, 4, HALF, FW), bf16), VMEM((2, 4, HALF, wide), bf16),
            VMEM((1, T, FW), bf16), VMEM((1, T, wide), bf16), VMEM((T, D), f32),
            VMEM((DP, 8, 128), f32), VMEM((DP, 8, 128), f32), VMEM((8, 128), f32), VMEM((SEQ, 8, 128), f32),
            *Scatter.scratch(D),
            *RingSum.scratch((1, 32, FW)), *RingSum.scratch((1, 32, FW)),
            *RingSum.scratch((4, 32, wide)), *RingSum.scratch((4, 32, wide)),
            *RingSum.scratch((1, 32, wide)), *RingSum.scratch((1, 32, wide)),
            DMA((8,)), DMA((8,)), DMA((3, 8)), DMA((3, 8)), DMA((DP,)), DMA((DP,)), DMA((2,)), DMA((2,)),
            DMA((SEQ,)), DMA((SEQ,)), DMA((6,)), DMA((7,)),
        ],
        compiler_params=pltpu.CompilerParams(collective_id=4, has_side_effects=True, vmem_limit_bytes=62 << 20),
        cost_estimate=pl.CostEstimate(flops=5 * G * D * WP, bytes_accessed=100 << 20, transcendentals=0),
        name="close",
    )(part, normed, both, adj_out, mixed, extra, s1, tok, adj_middle, gains, gain_two)


def finish_kernel(mix, feed, gate, chan, gain, mix_out, feed_out, gate_out, chan_out, gain_out):
    me = Place()
    for p in range(3):
        for j in range(SEQ):
            value = mix[j, :, p * WP : (p + 1) * WP].astype(f32)
            mix_out[:, p * W + j * WL : p * W + (j + 1) * WL] = value[:, :WL]

    def widen(i, c):
        here = lanes_of(i * 2048, 2048)
        feed_out[:, here] = feed[:, here].astype(f32)
        return c

    lax.fori_loop(0, 9, widen, 0)
    value = jnp.concatenate([gate[0:48].astype(f32)[0:40], gate[48:96].astype(f32)[0:40]], 1)
    gate_out[...] = jnp.where(me.sq < 4, value[:, :BW], value[:, BW - 128 : 2 * BW - 128])
    value = jnp.concatenate([chan[0:16].astype(f32)[0:8], chan[16:32].astype(f32)[0:8]], 1)
    first = (8 * (me.dp % 2) + me.sq) * 20
    first = first - jnp.where(first >= 128, 128, 0)
    chan_out[...] = pltpu.roll(value, (256 - first) % 256, 1)[:, :20]
    gain_out[...] = pltpu.roll(gain[...], (128 - me.sq * 16) % 128, 1)[0:2, 0:16]


def finish_call(mix, feed, gate, chan, gain):
    sds = jax.ShapeDtypeStruct
    vmem = pl.BlockSpec(memory_space=VMEM)
    return pl.pallas_call(
        finish_kernel,
        out_shape=(
            sds((16, 3 * W), f32), sds((16, 3 * FF), f32),
            sds((40, BW), f32), sds((8, 20), f32), sds((2, 16), f32),
        ),
        in_specs=[vmem] * 5,
        out_specs=[vmem] * 5,
        compiler_params=pltpu.CompilerParams(vmem_limit_bytes=62 << 20),
        name="finish",
    )(mix, feed, gate, chan, gain)


def shards(tokens, segments, mixer_weights, norm_gains, gate_weights, channel_terms, feed_weights, cotangent):
    (
        cot_all, w, normed, *saved, mixed, hidden, adj_gu, back_part, feed_part, norm_two,
        gates, terms, gains, lab, middle,
    ) = forward_call(
        tokens, cotangent, mixer_weights, feed_weights, segments[None], norm_gains.T, gate_weights, channel_terms.T
    )
    adj_all, s1, both, in_part, adj_middle, activations, gain_two, extra = turn_call(
        back_part, feed_part, norm_two, cot_all, hidden, adj_gu, saved, w, middle, cotangent, gains, gates, terms, lab
    )
    input_gradient, mix_out, feed_out, gate_out, chan_out, gain_out = close_call(
        in_part, normed, both, adj_all, mixed, extra.reshape(4, 4, 128, 128), s1, tokens, adj_middle, gains, gain_two
    )
    mixer_gradient, feed_gradient, gate_gradient, channel_gradient, gain_gradient = finish_call(
        mix_out, feed_out, gate_out, chan_out, gain_out
    )
    return (
        activations, input_gradient, mixer_gradient, gain_gradient.T, gate_gradient, channel_gradient.T, feed_gradient
    )


def solution(mesh):
    one = P(("dp", "seq"))
    two = P(("dp", "seq"), None)
    placed = (two, one, two, two, two, two, two, two)
    return jax.shard_map(shards, mesh=mesh, in_specs=placed, out_specs=(two,) * 7, check_vma=False)
```

```python
import functools

import jax
import jax.numpy as jnp
from jax import lax
from jax.experimental import pallas as pl
from jax.experimental.pallas import tpu as pltpu
from jax.sharding import PartitionSpec as P

D = 2048
W = 2560
FF = 6144
CONV = 4
BW = 160
SEQ = 8
DP = 16
T = 128
G = 1024
WL = W // SEQ
WP = 384
MW = 3 * WP
FL = FF // SEQ
FW = 3 * FL
HALF = T // 2
MINOR = 192

epsilon = 1e-06
rate_scale = 8.0
f32 = jnp.float32
bf16 = jnp.bfloat16
MESH = pl.DeviceIdType.MESH
ANY = pl.ANY
VMEM = pltpu.VMEM
DMA = pltpu.SemaphoreType.DMA


class Place:
    def __init__(self):
        self.dp = lax.axis_index("dp")
        self.sq = lax.axis_index("seq")
        self.x, self.y = self.dp // 4, self.dp % 4
        self.z, self.c = self.sq // 2, self.sq % 2

    def chip(self, k):
        return (self.z + k) % 4

    def slot(self, k, c):
        return 2 * self.chip(k) + c

    def z_peer(self, k):
        return (self.dp, 2 * self.chip(k) + self.c)

    def sibling(self):
        return (self.dp, 2 * self.z + 1 - self.c)

    def x_dp(self, k):
        return (self.x + k) % 4 * 4 + self.y

    def y_dp(self, k):
        return self.x * 4 + (self.y + k) % 4

    def dp_peer(self, dp):
        return (dp, self.sq)

    def seq_peer(self, k):
        return (self.dp, (self.sq + k) % SEQ)


def remote(src, dst, send, recv, device):
    return pltpu.make_async_remote_copy(
        src_ref=src, dst_ref=dst, send_sem=send, recv_sem=recv, device_id=device, device_id_type=MESH
    )


def greet(peers):
    barrier = pltpu.get_barrier_semaphore()
    for device in peers:
        pl.semaphore_signal(barrier, inc=1, device_id=device, device_id_type=MESH)
    return barrier, len(peers)


def z_peers(me):
    return [me.z_peer(1), me.z_peer(3), me.sibling()]


def ring_peers(me):
    return [me.dp_peer(me.x_dp(1)), me.dp_peer(me.x_dp(3)), me.dp_peer(me.y_dp(1)), me.dp_peer(me.y_dp(3))]


def dp_peers(me):
    return [me.dp_peer((me.dp + k) % DP) for k in range(1, DP)]


def seq_peers(me):
    return [me.seq_peer(k) for k in range(1, SEQ)]


class Gather:
    @staticmethod
    def scratch(n):
        return [VMEM((G, n), bf16), DMA((10,)), DMA((10,)), DMA((SEQ,))]

    def __init__(self, me, own, out, full, send, recv, keep):
        self.me, self.own, self.out, self.full = me, own, out, full
        self.send, self.recv, self.keep = send, recv, keep

    def block(self, k, c, half=None):
        base = self.me.slot(k, c) * T
        if half is None:
            return self.full.at[pl.ds(pl.multiple_of(base, T), T)]
        return self.full.at[pl.ds(pl.multiple_of(base + half * HALF, HALF), HALF)]

    def push(self, n, src, dst, device):
        remote(src, dst, self.send.at[n], self.recv.at[n], device).start()

    def arrived(self, n, dst):
        remote(dst, dst, self.send.at[n], self.recv.at[n], self.me.sibling()).wait_recv()

    def kept(self, k, other):
        c = 1 - self.me.c if other else self.me.c
        there = self.out.at[pl.ds(pl.multiple_of(self.me.slot(k, c) * T, T), T)]
        return pltpu.make_async_copy(self.block(k, c), there, self.keep.at[2 * k + other])

    def store(self, k, other):
        if self.out is not None:
            self.kept(k, other).start()

    def start(self):
        me = self.me
        right, left = me.z_peer(1), me.z_peer(3)
        mine = self.block(0, me.c)
        a, b = self.block(0, me.c, 0), self.block(0, me.c, 1)
        self.push(0, a, a, right)
        self.push(1, b, b, left)
        self.push(2, b, b, right)
        self.push(3, a, a, left)
        self.push(4, mine, mine, me.sibling())
        self.store(0, 0)

    def forward(self):
        me = self.me
        right, left = me.z_peer(1), me.z_peer(3)
        a, b = self.block(3, me.c, 0), self.block(1, me.c, 1)
        self.arrived(0, a)
        self.push(5, a, a, right)
        self.arrived(1, b)
        self.push(6, b, b, left)

    def hand_over(self, n, k):
        whole = self.block(k, self.me.c)
        self.push(n, whole, whole, self.me.sibling())
        self.store(k, 0)

    def across_left(self):
        self.arrived(2, self.block(3, self.me.c, 1))
        self.hand_over(7, 3)

    def across_right(self):
        self.arrived(3, self.block(1, self.me.c, 0))
        self.hand_over(8, 1)

    def across_far(self):
        self.arrived(5, self.block(2, self.me.c, 0))
        self.arrived(6, self.block(2, self.me.c, 1))
        self.hand_over(9, 2)

    def across(self):
        self.across_left()
        self.across_right()
        self.across_far()

    def taken(self, n, k):
        self.arrived(n, self.block(k, 1 - self.me.c))
        self.store(k, 1)

    def own_pair(self):
        self.taken(4, 0)

    def left_pair(self):
        self.taken(7, 3)

    def right_pair(self):
        self.taken(8, 1)

    def far_pair(self):
        self.taken(9, 2)

    def drain(self):
        for n in range(10):
            part = n in (0, 1, 2, 3, 5, 6)
            size = self.block(0, self.me.c, 0) if part else self.block(0, self.me.c)
            remote(size, size, self.send.at[n], self.recv.at[n], self.me.sibling()).wait_send()
        if self.out is not None:
            for k in range(4):
                self.kept(k, 0).wait()
                self.kept(k, 1).wait()

    def finish(self):
        self.own_pair()
        self.left_pair()
        self.right_pair()
        self.far_pair()
        self.drain()


class Spread:
    sems = 40

    def __init__(self, me, full, rows, send, recv):
        self.me, self.full, self.rows, self.send, self.recv = me, full, rows, send, recv

    def at(self, h, i, j):
        me = self.me
        dx, dy = (i, j) if h == 0 else (j, i)
        return (me.x + dx + 4) % 4 * 4 + (me.y + dy + 4) % 4

    def block(self, h, i, j, q=None):
        half = self.rows // 2
        base = self.at(h, i, j) * self.rows + h * half
        if q is None:
            return self.full.at[pl.ds(pl.multiple_of(base, 16), half)]
        return self.full.at[pl.ds(pl.multiple_of(base + q * (half // 2), 16), half // 2)]

    def push(self, h, n, block, i, j):
        n = 20 * h + n
        remote(block, block, self.send.at[n], self.recv.at[n], self.me.dp_peer(self.at(h, i, j))).start()

    def arrived(self, h, n, block):
        n = 20 * h + n
        remote(block, block, self.send.at[n], self.recv.at[n], self.me.sibling()).wait_recv()

    def second(self, t, i):
        for h in range(2):
            block = self.block(h, i, 0)
            self.push(h, 4 + 4 * t, block, 0, 1)
            self.push(h, 5 + 4 * t, block, 0, -1)

    def start(self):
        for h in range(2):
            block = self.block(h, 0, 0)
            self.push(h, 0, block, 1, 0)
            self.push(h, 1, block, -1, 0)
        self.second(0, 0)

    def turn(self):
        for h in range(2):
            self.arrived(h, 0, self.block(h, -1, 0))
            self.push(h, 2, self.block(h, -1, 0, 0), 1, 0)
            self.arrived(h, 1, self.block(h, 1, 0))
            self.push(h, 3, self.block(h, 1, 0, 1), -1, 0)
        self.second(1, -1)
        self.second(2, 1)

    def far(self):
        for h in range(2):
            self.arrived(h, 2, self.block(h, 2, 0, 0))
            self.arrived(h, 3, self.block(h, 2, 0, 1))
        self.second(3, 2)

    def hand_on(self, t):
        i = (0, -1, 1, 2)[t]
        for h in range(2):
            self.arrived(h, 4 + 4 * t, self.block(h, i, -1))
            self.push(h, 6 + 4 * t, self.block(h, i, -1, 0), 0, 1)
            self.arrived(h, 5 + 4 * t, self.block(h, i, 1))
            self.push(h, 7 + 4 * t, self.block(h, i, 1, 1), 0, -1)

    def finish(self):
        for t, i in enumerate((0, -1, 1, 2)):
            for h in range(2):
                self.arrived(h, 6 + 4 * t, self.block(h, i, 2, 0))
                self.arrived(h, 7 + 4 * t, self.block(h, i, 2, 1))

    def drain(self):
        for h in range(2):
            for n in range(20):
                handed = n in (2, 3) or (n >= 4 and n % 4 >= 2)
                block = self.block(h, 0, 0, 0 if handed else None)
                n = 20 * h + n
                remote(block, block, self.send.at[n], self.recv.at[n], self.me.sibling()).wait_send()


def add_rows(out, at, terms, rows, step=32):
    def body(i, carry):
        here = pl.ds(pl.multiple_of(i * step, step), step)
        total = terms[0](here)
        for term in terms[1:]:
            total = total + term(here)
        there = pl.ds(pl.multiple_of(at + i * step, step), step)
        out[there] = total.astype(out.dtype)
        return carry

    lax.fori_loop(0, rows // step, body, 0)


def reads(ref, start=0):
    def term(here):
        return ref[pl.ds(pl.multiple_of(here.start + start, 16), here.size)].astype(f32)

    return term


class Scatter:
    sems = 10

    @staticmethod
    def scratch(n):
        return [
            VMEM((4, T, n), bf16),
            VMEM((2, HALF, n), bf16),
            VMEM((2, HALF, n), bf16),
            VMEM((4, HALF, n), bf16),
            DMA((10,)),
            DMA((10,)),
        ]

    def __init__(self, me, part, other, through, passed, final, send, recv):
        self.me, self.part = me, part
        self.other, self.through, self.passed, self.final = other, through, passed, final
        self.send, self.recv = send, recv

    def piece(self, k, c):
        return self.part.at[pl.ds(pl.multiple_of(self.me.slot(k, c) * T, T), T)]

    def pair(self, k, q):
        base = self.me.slot(k, self.me.c) * T + q * HALF
        return self.part.at[pl.ds(pl.multiple_of(base, HALF), HALF)]

    def push(self, n, src, dst, device):
        remote(src, dst, self.send.at[n], self.recv.at[n], device).start()

    def arrived(self, n, dst):
        remote(dst, dst, self.send.at[n], self.recv.at[n], self.me.sibling()).wait_recv()

    def start(self):
        me = self.me
        for k in (2, 1, 3, 0):
            self.push(k, self.piece(k, 1 - me.c), self.other.at[k], me.sibling())

    def join(self):
        me = self.me
        right, left = me.z_peer(1), me.z_peer(3)
        for k in (2, 1, 3, 0):
            self.arrived(k, self.other.at[k])
            add_rows(
                self.piece(k, me.c), 0, [reads(self.piece(k, me.c)), reads(self.other.at[k])], T
            )
            if k == 2:
                self.push(4, self.pair(2, 0), self.through.at[0], right)
                self.push(5, self.pair(2, 1), self.through.at[1], left)
            if k == 1:
                self.push(6, self.pair(1, 1), self.final.at[0], right)
            if k == 3:
                self.push(7, self.pair(3, 0), self.final.at[1], left)

    def relay(self):
        me = self.me
        right, left = me.z_peer(1), me.z_peer(3)
        self.arrived(4, self.through.at[0])
        add_rows(self.passed.at[0], 0, [reads(self.through.at[0]), reads(self.pair(1, 0))], HALF)
        self.push(8, self.passed.at[0], self.final.at[2], right)
        self.arrived(5, self.through.at[1])
        add_rows(self.passed.at[1], 0, [reads(self.through.at[1]), reads(self.pair(3, 1))], HALF)
        self.push(9, self.passed.at[1], self.final.at[3], left)

    def finish(self, out, extra=None):
        me = self.me
        for n, k in ((6, 0), (7, 1), (8, 2), (9, 3)):
            self.arrived(n, self.final.at[k])
        more = [] if extra is None else [reads(extra)]
        add_rows(
            out, 0, [reads(self.pair(0, 0)), reads(self.final.at[1]), reads(self.final.at[2])] + more, HALF
        )
        more = [] if extra is None else [reads(extra, HALF)]
        add_rows(
            out,
            HALF,
            [reads(self.pair(0, 1)), reads(self.final.at[0]), reads(self.final.at[3])] + more,
            HALF,
        )
        for n in range(10):
            size = self.other.at[n] if n < 4 else self.final.at[0]
            remote(size, size, self.send.at[n], self.recv.at[n], me.sibling()).wait_send()


class RingSum:
    @staticmethod
    def scratch(shape):
        return [
            VMEM((2, *shape), bf16), VMEM((2, *shape), bf16), VMEM((4, *shape), bf16), DMA((6,)), DMA((6,)),
        ]

    def __init__(self, me, right, left, piece, through, passed, final, send, recv):
        self.me, self.right, self.left, self.piece = me, right, left, piece
        self.through, self.passed, self.final, self.send, self.recv = through, passed, final, send, recv

    def push(self, n, src, dst, device):
        remote(src, dst, self.send.at[n], self.recv.at[n], device).start()

    def arrived(self, n, dst):
        remote(dst, dst, self.send.at[n], self.recv.at[n], self.me.sibling()).wait_recv()

    def start(self):
        self.start_far()
        self.start_near()

    def start_far(self):
        self.push(0, self.piece(2, 0), self.through.at[0], self.right)
        self.push(1, self.piece(2, 1), self.through.at[1], self.left)

    def start_near(self):
        self.push(2, self.piece(1, 1), self.final.at[0], self.right)
        self.push(3, self.piece(3, 0), self.final.at[1], self.left)

    def add(self, out, terms):
        count, rows = terms[0].shape[0], terms[0].shape[1]

        def body(i, carry):
            m, here = i // (rows // 16), pl.ds(pl.multiple_of(i % (rows // 16) * 16, 16), 16)
            total = terms[0][m, here].astype(f32)
            for term in terms[1:]:
                total = total + term[m, here].astype(f32)
            out[m, here] = total.astype(out.dtype)
            return carry

        lax.fori_loop(0, count * (rows // 16), body, 0)

    def relay(self):
        self.arrived(0, self.through.at[0])
        self.add(self.passed.at[0], [self.through.at[0], self.piece(1, 0)])
        self.push(4, self.passed.at[0], self.final.at[2], self.right)
        self.arrived(1, self.through.at[1])
        self.add(self.passed.at[1], [self.through.at[1], self.piece(3, 1)])
        self.push(5, self.passed.at[1], self.final.at[3], self.left)

    def finish(self, out):
        for n, k in ((2, 0), (3, 1), (4, 2), (5, 3)):
            self.arrived(n, self.final.at[k])
        self.add(out(0), [self.piece(0, 0), self.final.at[1], self.final.at[2]])
        self.add(out(1), [self.piece(0, 1), self.final.at[0], self.final.at[3]])
        for n in range(6):
            size = self.final.at[0]
            remote(size, size, self.send.at[n], self.recv.at[n], self.me.sibling()).wait_send()


def norm_rows(value, gain):
    return value * lax.rsqrt(jnp.mean(value * value, axis=-1, keepdims=True) + epsilon) * gain


def norm_pull(value, gain, incoming):
    r = lax.rsqrt(jnp.mean(value * value, axis=-1, keepdims=True) + epsilon)
    scaled = incoming * gain
    inner = jnp.mean(value * scaled, axis=-1, keepdims=True)
    normed = value * r
    return r * (scaled - normed * (inner * r)), incoming * normed


CHUNK = 256
STEPS = G // CHUNK
contract_last = (((1,), (1,)), ((), ()))
contract_first = (((0,), (0,)), ((), ()))
gelu_c = 0.7978845608028654
gelu_k = 0.044715


def gelu_parts(v):
    square = v * v
    t = jnp.tanh(gelu_c * (v + gelu_k * square * v))
    half = 0.5 * (1.0 + t)
    slope = half + 0.5 * v * (1.0 - t * t) * (gelu_c * (1.0 + 3.0 * gelu_k * square))
    return v * half, slope


def minus_expm1(z):
    series = -z * (1.0 + z * (1 / 2 + z * (1 / 6 + z * (1 / 24 + z * (1 / 120 + z * (1 / 720))))))
    return jnp.where(z > -0.25, series, 1.0 - jnp.exp(z))


def recur(conv, raw_a, raw_x, terms, start):
    recall = jax.nn.sigmoid(raw_a + terms[5:6])
    admit = jax.nn.sigmoid(raw_x + terms[6:7])
    lograte = terms[7:8] * recall
    decay = jnp.exp(lograte) * (1.0 - start)
    root = jnp.sqrt(minus_expm1(2.0 * lograte))
    scale = start + (1.0 - start) * root
    return recall, admit, lograte, decay, root, scale


def nt(left, right):
    return lax.dot_general(left, right, contract_last, preferred_element_type=f32)


def tn(left, right):
    return lax.dot_general(left, right, contract_first, preferred_element_type=f32)


def nn(left, right):
    return jnp.dot(left, right, preferred_element_type=f32)


def rows_of(base, size):
    return pl.ds(pl.multiple_of(base, 16), size)


def lanes_of(base, size):
    return pl.ds(pl.multiple_of(base, 128), size)


def windows(lab, base):
    return lab[pl.ds(pl.multiple_of(base, 8), CHUNK + 16)]


def same(window, k):
    here = window[8 : 8 + CHUNK, 0:1]
    there = window[8 - k : 8 - k + CHUNK, 0:1]
    return (here == there).astype(f32)


def log_one_plus(x):
    z = x / (2.0 + x)
    s = z * z
    return 2.0 * z * (1.0 + s * (1 / 3 + s * (1 / 5 + s * (1 / 7 + s * (1 / 9 + s * (1 / 11 + s * (1 / 13)))))))


def forward_kernel(
    tok, cot, mixer, feed, numbers, gain_in, gate_in, chan_in,
    cot_out, mix_out, normed_out, x_out, y_out, conv_out, prior_out, mixed_out,
    hidden_out, gu_out, back_out, ff_out, n2_out, gate_out, term_out, gain_out, lab_out, middle,
    mixw, feedw, part, xs, ys, convs, priors, mixeds, hiddens, gus,
    mix, small, gates, chan, small_in, minor, gate_f,
    xpad, dec, drv, sts, carry, *rest,
):
    tg, cg, ng, sc = rest[:4], rest[4:8], rest[8:12], rest[12:18]
    ms, mr, fs, fr, ss, sr, ps, pr, qs, qr, es, er, hs, hr, ls, os = rest[18:]
    me = Place()
    quarter, at = me.dp // 8, me.dp % 8
    gate_to = (8 * quarter + me.sq, at)
    gate_self = me.sq == at
    chan_to = (8 * (me.dp % 2) + me.sq, me.dp // 2)
    chan_from = (2 * me.sq + me.dp // 8, me.dp % 8)
    chan_self = jnp.logical_and(chan_to[0] == me.dp, chan_to[1] == me.sq)
    barrier, count = greet(seq_peers(me) + ring_peers(me))

    @pl.when(jnp.logical_not(gate_self))
    def _():
        pl.semaphore_signal(barrier, inc=1, device_id=gate_to, device_id_type=MESH)

    @pl.when(jnp.logical_not(chan_self))
    def _():
        pl.semaphore_signal(barrier, inc=1, device_id=chan_from, device_id_type=MESH)

    tokg, cotg, n2g = tg[0], cg[0], ng[0]
    own_rows = rows_of(me.dp * T + me.sq * 16, 16)

    def feed_columns(p, j):
        return lanes_of(p * FF + j * FL, FL)

    local = [
        pltpu.make_async_copy(tok, tokg.at[rows_of(me.sq * T, T)], ls.at[0]),
        pltpu.make_async_copy(cot, cotg.at[rows_of(me.sq * T, T)], ls.at[1]),
    ] + [
        pltpu.make_async_copy(feed.at[:, feed_columns(p, me.sq)], feedw.at[own_rows, pl.ds(p * FL, FL)], ls.at[4 + p])
        for p in range(3)
    ]
    for copy in local:
        copy.start()

    for j in range(SEQ):
        for p in range(3):
            value = mixer[:, p * W + j * WL : p * W + (j + 1) * WL]
            mix[j, :, p * WP : (p + 1) * WP] = jnp.concatenate([value, jnp.zeros((16, WP - WL), bf16)], 1)
    row = jnp.concatenate([gain_in[...].astype(f32), jnp.zeros((2, 112), f32)], 1)
    row = pltpu.roll(row, me.sq * 16, 1)
    small[0:16] = jnp.concatenate([row, jnp.zeros((14, 128), f32)], 0).astype(bf16)
    small[16:32] = jnp.concatenate([numbers[...].astype(f32), jnp.zeros((15, 128), f32)], 0).astype(bf16)
    value = gate_in[...].astype(f32)
    value = jnp.where(
        me.sq < 4,
        jnp.concatenate([value, jnp.zeros((40, 256 - BW), f32)], 1),
        jnp.concatenate([jnp.zeros((40, BW - 128), f32), value, jnp.zeros((40, 384 - 2 * BW), f32)], 1),
    )
    for n in range(2):
        half = jnp.concatenate([value[:, n * 128 : n * 128 + 128], jnp.zeros((8, 128), f32)], 0)
        gates[n * 48 : n * 48 + 48] = half.astype(bf16)
    value = jnp.concatenate([chan_in[...].astype(f32), jnp.zeros((8, WP - 20), f32)], 1)
    value = pltpu.roll(value, (8 * (me.dp % 2) + me.sq) * 20, 1)
    for n in range(3):
        part_rows = jnp.concatenate([value[:, n * 128 : n * 128 + 128], jnp.zeros((8, 128), f32)], 0)
        chan[n * 16 : n * 16 + 16] = part_rows.astype(bf16)
    mixw[own_rows] = mix[me.sq]
    small_in[me.sq] = small[...]

    pl.semaphore_wait(barrier, count + jnp.where(gate_self, 0, 1) + jnp.where(chan_self, 0, 1))

    sent = []

    def push(src, dst, send, recv, device):
        sent.append(remote(src, dst, send, recv, device))
        sent[-1].start()

    def arrived(dst, send, recv):
        remote(dst, dst, send, recv, me.sibling()).wait_recv()

    order = (4, 3, 5, 2, 6, 1, 7)
    for k in order:
        to = (me.sq + k) % SEQ
        push(mix.at[to], mixw.at[own_rows], ms.at[k], mr.at[k], me.seq_peer(k))
        push(small, small_in.at[me.sq], ss.at[k], sr.at[k], me.seq_peer(k))

    def minor_rows(dp, start, size):
        return minor.at[rows_of(dp * MINOR + start, size)]

    gate_copy = remote(gates, minor_rows(gate_to[0], 16, 96), hs.at[0], hr.at[0], gate_to)
    chan_copy = remote(chan, minor_rows(chan_to[0], 112, 48), hs.at[1], hr.at[1], chan_to)
    gate_local = pltpu.make_async_copy(gates, minor_rows(me.dp, 16, 96), ls.at[7])
    chan_local = pltpu.make_async_copy(chan, minor_rows(me.dp, 112, 48), ls.at[8])
    gate_here = remote(gates, minor_rows(me.dp, 16, 96), hs.at[0], hr.at[0], gate_to)
    chan_here = remote(chan, minor_rows(me.dp, 112, 48), hs.at[1], hr.at[1], chan_to)

    @pl.when(jnp.logical_not(gate_self))
    def _():
        gate_copy.start()

    @pl.when(gate_self)
    def _():
        gate_local.start()

    @pl.when(jnp.logical_not(chan_self))
    def _():
        chan_copy.start()

    @pl.when(chan_self)
    def _():
        chan_local.start()

    local[0].wait()
    tokens = Gather(me, None, None, *tg)
    tokens.start()
    for copy in local[1:]:
        copy.wait()

    def seq_rows(k):
        return rows_of(me.dp * T + (me.sq - k + SEQ) % SEQ * 16, 16)

    mixes = Spread(me, mixw, T, ps, pr)
    feeds = Spread(me, feedw, T, qs, qr)
    minors = Spread(me, minor, MINOR, es, er)

    for k in range(1, SEQ):
        arrived(small_in.at[(me.sq - k + SEQ) % SEQ], ss.at[k], sr.at[k])
    gain = small_in[0, 0:16].astype(f32)
    for k in range(1, SEQ):
        gain = gain + small_in[k, 0:16].astype(f32)
    minor[rows_of(me.dp * MINOR, 16)] = gain.astype(bf16)
    minor[rows_of(me.dp * MINOR + 160, 32)] = jnp.zeros((32, 128), bf16)

    @pl.when(jnp.logical_not(gate_self))
    def _():
        gate_copy.wait_send()
        gate_here.wait_recv()

    @pl.when(gate_self)
    def _():
        gate_local.wait()

    @pl.when(jnp.logical_not(chan_self))
    def _():
        chan_copy.wait_send()
        chan_here.wait_recv()

    @pl.when(chan_self)
    def _():
        chan_local.wait()

    minors.start()
    for k in range(1, SEQ):
        arrived(mixw.at[seq_rows(k)], ms.at[k], mr.at[k])
    mixes.start()
    tokens.forward()
    for k in order:
        to = (me.sq + k) % SEQ
        for p in range(3):
            push(feed.at[:, feed_columns(p, to)], feedw.at[own_rows, pl.ds(p * FL, FL)],
                 fs.at[p, k], fr.at[p, k], me.seq_peer(k))

    lab_out[0:8] = jnp.full((8, 128), -1.0, f32)
    lab_out[G + 8 :] = jnp.full((8, 128), -2.0, f32)
    for k in range(SEQ):
        row = small_in[k, 16:32].astype(f32)[0:1]
        lab_out[8 + k * T : 8 + (k + 1) * T] = jnp.broadcast_to(row, (128, 128)).T

    minors.turn()
    mixes.turn()
    minors.far()
    mixes.far()
    tokens.across_left()
    tokens.across_right()
    for t in range(4):
        minors.hand_on(t)
    mixes.hand_on(0)
    tokens.across_far()
    cots = Gather(me, None, cot_out, *cg)
    cots.start()
    minors.finish()
    for k in range(DP):
        gain_out[:, k * 128 : (k + 1) * 128] = minor[k * MINOR : k * MINOR + 16].astype(f32)[0:8]

    def normed_copy(k, other):
        c = 1 - me.c if other else me.c
        rows = rows_of(me.slot(k, c) * T, T)
        return pltpu.make_async_copy(part.at[rows], normed_out.at[rows], os.at[23 + 2 * k + other])

    def normalise(k, other):
        base = me.slot(k, 1 - me.c if other else me.c) * T

        def body(i, c):
            here = rows_of(base + i * 16, 16)
            part[here] = norm_rows(tokg[here].astype(f32), gain_out[0:1]).astype(bf16)
            return c

        lax.fori_loop(0, T // 16, body, 0, unroll=2)
        normed_copy(k, other).start()

    normalise(0, 0)
    tokens.own_pair()
    normalise(0, 1)
    mixes.hand_on(1)
    mixes.hand_on(2)
    normalise(3, 0)
    normalise(1, 0)
    tokens.left_pair()
    normalise(3, 1)
    tokens.right_pair()
    normalise(1, 1)
    mixes.hand_on(3)
    for k in range(1, SEQ):
        for p in range(3):
            arrived(feedw.at[seq_rows(k), pl.ds(p * FL, FL)], fs.at[p, k], fr.at[p, k])
    feeds.start()
    normalise(2, 0)
    tokens.far_pair()
    normalise(2, 1)
    tokens.drain()
    terms = minor[112:160].astype(f32)
    for k in range(1, DP):
        terms = terms + minor[k * MINOR + 112 : k * MINOR + 160].astype(f32)
    for n in range(3):
        group = terms[16 * n : 16 * n + 16]
        lanes = slice(128 * n, 128 * n + 128)
        term_out[:, lanes] = group
        lam = group[7:8]
        small_exp = jnp.exp(-jnp.abs(lam))
        term_out[7:8, lanes] = -rate_scale * (jnp.maximum(-lam, 0.0) + log_one_plus(small_exp))
        term_out[8:9, lanes] = rate_scale * jax.nn.sigmoid(-lam)
    gate_f[...] = jnp.zeros(gate_f.shape, f32)
    for k in range(DP):
        base = k // 8 * WP + k % 8 * 40
        for n in range(2):
            lanes = k % 8 // 4 * 128 + n * 128
            start = k * MINOR + 16 + 48 * n
            gate_f[base : base + 40, lanes : lanes + 128] = minor[start : start + 48].astype(f32)[0:40]
    gate_out[0] = gate_f[:WP].astype(bf16)
    gate_out[1] = gate_f[WP:].astype(bf16)
    for k in range(4):
        normed_copy(k, 0).wait()
        normed_copy(k, 1).wait()
    mixes.finish()
    writes = [pltpu.make_async_copy(mixw, mix_out, os.at[1])]
    writes[0].start()

    xpad[0:8] = jnp.zeros((8, WP), f32)
    carry[...] = jnp.zeros((8, WP), f32)
    row = lax.broadcasted_iota(jnp.int32, (8, WP), 0)

    def mix_chunk(step, c):
        @pl.when(step == 1)
        def _():
            cots.forward()
            feeds.turn()

        @pl.when(step == 2)
        def _():
            feeds.far()

        @pl.when(step == 3)
        def _():
            cots.across()
            feeds.hand_on(0)

        base = step * CHUNK
        rows = rows_of(base, CHUNK)
        both = nn(part[rows], mixw[:, : 2 * WP])
        x, y = both[:, :WP], both[:, WP:]
        xs[rows] = x
        ys[rows] = y
        xpad[8:] = x
        terms = term_out[...]
        window = windows(lab_out, base)
        start = 1.0 - same(window, 1)
        conv = terms[4:5] + terms[0:1] * x
        for k in range(1, CONV):
            conv = conv + terms[k : k + 1] * (same(window, k) * xpad[8 - k : 8 - k + CHUNK])
        xpad[0:8] = x[CHUNK - 8 :]
        convs[rows] = conv
        lowered = conv.astype(bf16)
        raw_a, raw_x = nn(lowered, gate_out[0]), nn(lowered, gate_out[1])
        recall, admit, lograte, decay, root, scale = recur(conv, raw_a, raw_x, terms, start)
        dec[...] = decay
        drv[...] = scale * admit * conv

        def scan(i, before):
            here = pl.ds(pl.multiple_of(i * 8, 8), 8)
            a, b = dec[here], drv[here]
            for s in (1, 2, 4):
                b = b + a * jnp.where(row >= s, pltpu.roll(b, s, 0), 0.0)
                a = a * jnp.where(row >= s, pltpu.roll(a, s, 0), 1.0)
            state = b + a * before
            sts[here] = state
            priors[pl.ds(pl.multiple_of(base + i * 8, 8), 8)] = jnp.where(row >= 1, pltpu.roll(state, 1, 0), before)
            return jnp.broadcast_to(state[7:8], (8, WP))

        carry[...] = lax.fori_loop(0, CHUNK // 8, scan, carry[...], unroll=4)
        value, _ = gelu_parts(ys[rows])
        mixed = (value * sts[...]).astype(bf16)
        mixeds[rows] = mixed
        part[rows] = nt(mixed, mixw[:, 2 * WP :]).astype(bf16)
        return c

    lax.fori_loop(0, STEPS, mix_chunk, 0)

    total = Scatter(me, part, *sc)
    total.start()
    for n, (src, dst) in enumerate(((xs, x_out), (ys, y_out), (convs, conv_out), (priors, prior_out), (mixeds, mixed_out))):
        writes.append(pltpu.make_async_copy(src, dst, os.at[2 + n]))
        writes[-1].start()
    total.join()
    feeds.hand_on(1)
    feeds.hand_on(2)
    total.relay()
    feeds.hand_on(3)
    total.finish(middle, tok)

    def second_norm(i, c):
        here = pl.ds(pl.multiple_of(i * 16, 16), 16)
        n2g[rows_of(me.sq * T + i * 16, 16)] = norm_rows(middle[here], gain_out[1:2]).astype(bf16)
        return c

    lax.fori_loop(0, T // 16, second_norm, 0, unroll=2)
    seconds = Gather(me, None, n2_out, *ng)
    seconds.start()
    cots.finish()
    feeds.finish()

    def feed_chunk(k, n):
        rows = rows_of(me.chip(k) * CHUNK, CHUNK)
        gu = nn(n2g[rows], feedw[:, : 2 * FL])
        gate, up = gu[:, :FL], gu[:, FL:]
        adj_hidden = nn(cotg[rows], feedw[:, 2 * FL :])
        value, slope = gelu_parts(gate)
        hidden = (value * up).astype(bf16)
        hiddens[rows] = hidden
        gus[rows, :FL] = (adj_hidden * up * slope).astype(bf16)
        gus[rows, FL:] = (adj_hidden * value).astype(bf16)
        tokg[rows] = nt(hidden, feedw[:, 2 * FL :]).astype(bf16)
        part[rows] = nt(gus[rows], feedw[:, : 2 * FL]).astype(bf16)

    def feed_store(k, n):
        rows = rows_of(me.chip(k) * CHUNK, CHUNK)
        for m, (src, dst) in enumerate(((hiddens, hidden_out), (gus, gu_out), (tokg, ff_out), (part, back_out))):
            writes.append(pltpu.make_async_copy(src.at[rows], dst.at[rows], os.at[7 + 4 * n + m]))
            writes[-1].start()

    seconds.own_pair()
    feed_chunk(0, 0)
    feed_store(0, 0)
    seconds.forward()
    seconds.across_left()
    seconds.across_right()
    seconds.left_pair()
    feed_chunk(3, 1)
    feed_store(3, 1)
    seconds.across_far()
    seconds.right_pair()
    feed_chunk(1, 2)
    feed_store(1, 2)
    seconds.far_pair()
    feed_chunk(2, 3)
    feed_store(2, 3)
    seconds.drain()
    for copy in writes:
        copy.wait()
    for copy in sent:
        copy.wait_send()
    mixes.drain()
    minors.drain()
    feeds.drain()


def forward_call(tok, cot, mixer, feed, numbers, gain, gates, chan):
    sds = jax.ShapeDtypeStruct
    hbm, vmem = pl.BlockSpec(memory_space=ANY), pl.BlockSpec(memory_space=VMEM)
    return pl.pallas_call(
        forward_kernel,
        out_shape=(
            sds((G, D), bf16), sds((D, MW), bf16), sds((G, D), bf16),
            sds((G, WP), f32), sds((G, WP), f32), sds((G, WP), f32), sds((G, WP), f32), sds((G, WP), bf16),
            sds((G, FL), bf16), sds((G, 2 * FL), bf16), sds((G, D), bf16), sds((G, D), bf16), sds((G, D), bf16),
            sds((2, WP, WP), bf16), sds((16, WP), f32), sds((8, D), f32), sds((G + 16, 128), f32), sds((T, D), f32),
        ),
        in_specs=[vmem, hbm, vmem, hbm, vmem, vmem, vmem, vmem],
        out_specs=[hbm] * 13 + [vmem] * 5,
        scratch_shapes=[
            VMEM((D, MW), bf16), VMEM((D, FW), bf16), VMEM((G, D), bf16),
            VMEM((G, WP), f32), VMEM((G, WP), f32), VMEM((G, WP), f32), VMEM((G, WP), f32), VMEM((G, WP), bf16),
            VMEM((G, FL), bf16), VMEM((G, 2 * FL), bf16),
            VMEM((SEQ, 16, MW), bf16), VMEM((32, 128), bf16), VMEM((96, 128), bf16), VMEM((48, 128), bf16),
            VMEM((SEQ, 32, 128), bf16), VMEM((DP * MINOR, 128), bf16), VMEM((2 * WP, WP), f32),
            VMEM((CHUNK + 8, WP), f32), VMEM((CHUNK, WP), f32), VMEM((CHUNK, WP), f32), VMEM((CHUNK, WP), f32),
            VMEM((8, WP), f32),
            *Gather.scratch(D), *Gather.scratch(D), *Gather.scratch(D), *Scatter.scratch(D),
            DMA((SEQ,)), DMA((SEQ,)), DMA((3, SEQ)), DMA((3, SEQ)), DMA((SEQ,)), DMA((SEQ,)),
            DMA((40,)), DMA((40,)), DMA((40,)), DMA((40,)), DMA((40,)), DMA((40,)),
            DMA((2,)), DMA((2,)), DMA((9,)), DMA((31,)),
        ],
        compiler_params=pltpu.CompilerParams(collective_id=1, has_side_effects=True, vmem_limit_bytes=(63 << 20) + (900 << 10)),
        cost_estimate=pl.CostEstimate(flops=30 * G * D * WP, bytes_accessed=100 << 20, transcendentals=0),
        name="forward",
    )(tok, cot, mixer, feed, numbers, gain, gates, chan)


def turn_kernel(
    back_in, ff_in, n2_in, cot_in, hid_in, gu_in, x_in, y_in, conv_in, prior_in, w_in,
    middle, cot, gains, gates, terms_ref, lab,
    adj_all, s1_out, both_out, part_out, adj_middle, act, gain_grad, extra,
    part, ffp, mg, s1, both, dec, adjs, acp, carry, gate_grad, sums, *rest,
):
    one, two, gathering, ring_a, ring_b = rest[:6], rest[6:12], rest[12:16], rest[16:21], rest[21:26]
    ls, os = rest[26:]
    me = Place()
    first = [pltpu.make_async_copy(back_in, part, ls.at[0]), pltpu.make_async_copy(ff_in, ffp, ls.at[1])]
    first[0].start()
    barrier, count = greet(z_peers(me) + ring_peers(me))
    pl.semaphore_wait(barrier, count)
    xs, ys = (me.dp_peer(me.x_dp(1)), me.dp_peer(me.x_dp(3))), (me.dp_peer(me.y_dp(1)), me.dp_peer(me.y_dp(3)))
    upper = RingSum(
        me, *ys, lambda k, q: mg.at[:, (me.y + k) % 4, pl.ds(q * 32, 32)], *ring_a
    )
    lower = RingSum(
        me, *xs, lambda k, q: mg.at[(me.x + k) % 4, :, pl.ds(HALF + q * 32, 32)], *ring_b
    )
    mine = me.sq * T

    def grads(n2, cots, gu, hid):
        loads = [
            pltpu.make_async_copy(src, dst, ls.at[2 + n])
            for n, (src, dst) in enumerate(((n2_in, n2), (cot_in, cots), (gu_in, gu), (hid_in, hid)))
        ]
        first[0].wait()
        inner = Scatter(me, part, *one)
        inner.start()
        for copy in loads:
            copy.start()
        first[1].start()
        inner.join()
        for copy in loads:
            copy.wait()

        def tile(i, c):
            here = pl.ds(pl.multiple_of(i * 256, 256), 256)
            left = tn(n2[:, here], gu[...]).astype(bf16)
            right = tn(cots[:, here], hid[...]).astype(bf16)
            for h in range(2):
                mg[i // 2, i % 2 * 2 + h, :, : 2 * FL] = left[h * T : (h + 1) * T]
                mg[i // 2, i % 2 * 2 + h, :, 2 * FL :] = right[h * T : (h + 1) * T]

            @pl.when(i == 3)
            def _():
                inner.relay()

            return c

        lax.fori_loop(0, 8, tile, 0)
        upper.start()
        lower.start()
        inner.finish(adj_middle)

    pl.run_scoped(grads, VMEM((G, D), bf16), VMEM((G, D), bf16), VMEM((G, 2 * FL), bf16), VMEM((G, FL), bf16))

    def pull(i, c):
        here = pl.ds(pl.multiple_of(i * 16, 16), 16)
        pulled, terms = norm_pull(middle[here], gains[1:2], adj_middle[here])
        value = cot[here].astype(f32) + pulled
        adj_middle[here] = value
        gathering[0][rows_of(mine + i * 16, 16)] = value.astype(bf16)
        return c + jnp.sum(terms, axis=0, keepdims=True)

    gain_grad[...] = lax.fori_loop(0, T // 16, pull, jnp.zeros((1, D), f32), unroll=2)
    gather = Gather(me, None, adj_all, *gathering)
    gather.start()
    first[1].wait()
    outer = Scatter(me, ffp, *two)

    def unmix(x_all, y_all, conv_all, prior_all, w):
        loads = [
            pltpu.make_async_copy(src, dst, ls.at[2 + n])
            for n, (src, dst) in enumerate(
                ((x_in, x_all), (y_in, y_all), (conv_in, conv_all), (prior_in, prior_all), (w_in, w))
            )
        ]
        for copy in loads:
            copy.start()
        gather.forward()
        upper.relay()
        lower.relay()
        gather.across()
        dec[CHUNK:] = jnp.zeros((8, WP), f32)
        acp[CHUNK:] = jnp.zeros((8, WP), f32)
        carry[...] = jnp.zeros((8, WP), f32)
        gate_grad[...] = jnp.zeros(gate_grad.shape, f32)
        sums[...] = jnp.zeros(sums.shape, f32)
        for copy in loads:
            copy.wait()
        gather.finish()
        outer.start()
        row = lax.broadcasted_iota(jnp.int32, (8, WP), 0)

        def chunk(step, c):
            @pl.when(step == 1)
            def _():
                outer.join()

            @pl.when(step == 3)
            def _():
                outer.relay()

            base = (STEPS - 1 - step) * CHUNK
            rows = rows_of(base, CHUNK)
            window = windows(lab, base)
            terms = terms_ref[...]
            start = 1.0 - same(window, 1)
            conv, prior = conv_all[rows], prior_all[rows]
            lowered = conv.astype(bf16)
            raw_a, raw_x = nn(lowered, gates[0]), nn(lowered, gates[1])
            recall, admit, lograte, decay, root, scale = recur(conv, raw_a, raw_x, terms, start)
            dec[0:CHUNK] = decay
            states = decay * prior + scale * admit * conv
            adj_mixed = nn(gathering[0][rows], w[:, 2 * WP :])
            value, slope = gelu_parts(y_all[rows])
            adjs[...] = adj_mixed * value
            both[rows, WP:] = (adj_mixed * states * slope).astype(bf16)

            def scan(i, after):
                at = pl.multiple_of((CHUNK // 8 - 1 - i) * 8, 8)
                here = pl.ds(at, 8)
                later = dec[pl.ds(pl.multiple_of(at + 8, 8), 8)]
                a = jnp.where(row < 7, pltpu.roll(dec[here], 7, 0), later[0:1])
                b = adjs[here]
                for s in (1, 2, 4):
                    b = b + a * jnp.where(row < 8 - s, pltpu.roll(b, 8 - s, 0), 0.0)
                    a = a * jnp.where(row < 8 - s, pltpu.roll(a, 8 - s, 0), 1.0)
                value = b + a * after
                adjs[here] = value
                return jnp.broadcast_to(value[0:1], (8, WP))

            carry[...] = lax.fori_loop(0, CHUNK // 8, scan, carry[...], unroll=4)
            adjoint = adjs[...]
            flow = adjoint * admit * conv
            adj_lograte = adjoint * prior * decay - (1.0 - start) * flow * (jnp.exp(2.0 * lograte) / root)
            adj_ra = adj_lograte * terms[7:8] * (recall * (1.0 - recall))
            adj_rx = flow * scale * (1.0 - admit)

            def total(v):
                return jnp.sum(v, axis=0, keepdims=True)

            sums[5:6] += total(adj_ra)
            sums[6:7] += total(adj_rx)
            sums[7:8] += total(adj_lograte * recall) * terms[8:9]
            low_a, low_x = adj_ra.astype(bf16), adj_rx.astype(bf16)
            adj_conv = adjoint * scale * admit + nt(low_a, gates[0]) + nt(low_x, gates[1])
            gate_grad[0] += tn(lowered, low_a)
            gate_grad[1] += tn(lowered, low_x)
            acp[0:CHUNK] = adj_conv
            x = x_all[rows]
            adj_x = terms[0:1] * adj_conv
            sums[4:5] += total(adj_conv)
            sums[0:1] += total(adj_conv * x)
            for k in range(1, CONV):
                moved = same(window, -k) * acp[k : k + CHUNK]
                adj_x = adj_x + terms[k : k + 1] * moved
                sums[k : k + 1] += total(moved * x)
            dec[CHUNK:] = dec[0:8]
            acp[CHUNK:] = acp[0:8]
            both[rows, :WP] = adj_x.astype(bf16)
            part[rows] = nt(both[rows], w[:, : 2 * WP]).astype(bf16)
            return c

        lax.fori_loop(0, STEPS, chunk, 0)

    wide = VMEM((G, WP), f32)
    pl.run_scoped(unmix, wide, wide, wide, wide, VMEM((D, MW), bf16))
    writes = [pltpu.make_async_copy(part, part_out, os.at[0]), pltpu.make_async_copy(both, both_out, os.at[1])]
    for copy in writes:
        copy.start()
    for k in range(DP):
        rows = slice(k % 8 * 40, k % 8 * 40 + 40)
        for n in range(2):
            lanes = slice(k % 8 // 4 * 128 + n * 128, k % 8 // 4 * 128 + n * 128 + 128)
            piece = jnp.concatenate([gate_grad[k // 8, rows, lanes], jnp.zeros((8, 128), f32)], 0)
            extra[k, 48 * n : 48 * n + 48] = piece.astype(bf16)
            lanes = slice(channel_window(k) + n * 128, channel_window(k) + n * 128 + 128)
            piece = jnp.concatenate([sums[:, lanes], jnp.zeros((8, 128), f32)], 0)
            extra[k, 96 + 16 * n : 112 + 16 * n] = piece.astype(bf16)
    upper.finish(lambda q: s1.at[0, :, pl.ds(q * 32, 32)])
    lower.finish(lambda q: s1.at[1, :, pl.ds(q * 32, 32)])
    writes.append(pltpu.make_async_copy(s1, s1_out, os.at[2]))
    writes[2].start()
    outer.finish(act, middle)
    for copy in writes:
        copy.wait()


def channel_window(k):
    return min(k * 20 // 128, 1) * 128


def turn_call(back, ff, n2, cots, hid, gu, saved, w, middle, cot, gains, gates, terms, lab):
    sds = jax.ShapeDtypeStruct
    hbm, vmem = pl.BlockSpec(memory_space=ANY), pl.BlockSpec(memory_space=VMEM)
    return pl.pallas_call(
        turn_kernel,
        out_shape=(
            sds((G, D), bf16), sds((2, 4, HALF, FW), bf16), sds((G, 2 * WP), bf16), sds((G, D), bf16),
            sds((T, D), f32), sds((T, D), bf16), sds((1, D), f32), sds((DP, 128, 128), bf16),
        ),
        in_specs=[hbm] * 11 + [vmem] * 6,
        out_specs=[hbm] * 4 + [vmem] * 4,
        scratch_shapes=[
            VMEM((G, D), bf16), VMEM((G, D), bf16), VMEM((4, 4, T, FW), bf16),
            VMEM((2, 4, HALF, FW), bf16), VMEM((G, 2 * WP), bf16),
            VMEM((CHUNK + 8, WP), f32), VMEM((CHUNK, WP), f32), VMEM((CHUNK + 8, WP), f32), VMEM((8, WP), f32),
            VMEM((2, WP, WP), f32), VMEM((8, WP), f32),
            *Scatter.scratch(D), *Scatter.scratch(D), *Gather.scratch(D),
            *RingSum.scratch((4, 32, FW)), *RingSum.scratch((4, 32, FW)), DMA((8,)), DMA((3,)),
        ],
        compiler_params=pltpu.CompilerParams(collective_id=2, has_side_effects=True, vmem_limit_bytes=(63 << 20) + (900 << 10)),
        cost_estimate=pl.CostEstimate(flops=30 * G * D * WP, bytes_accessed=100 << 20, transcendentals=0),
        name="turn",
    )(back, ff, n2, cots, hid, gu, *saved, w, middle, cot, gains, gates, terms, lab)


def close_kernel(
    part_in, normed_in, both_in, adj_in, mixed_in, extra_in, s1_in, tok, adj_middle, gains, gain_two,
    in_grad, mix_out, feed_out, gate_out, chan_out, gain_out,
    part, normed, both, adj_out, mixed, mg, s1f, s1, lastf, last, adj, gp, gp_in, gain_sum, gain_in, *rest,
):
    one, fa, fb, ma, mb, na, nb = rest[:6], *(rest[6 + 5 * n : 11 + 5 * n] for n in range(6))
    m3s, m3r, f3s, f3r, gs, gr, hs, hr, qs, qr, ls, ws = rest[36:]
    me = Place()
    loads = [
        pltpu.make_async_copy(src, dst, ws.at[n])
        for n, (src, dst) in enumerate(
            ((part_in, part), (s1_in, s1f), (normed_in, normed), (both_in, both), (adj_in, adj_out),
             (mixed_in, mixed), (extra_in, mg.at[:, :, :, pl.ds(MW, 128)]))
        )
    ]
    loads[0].start()
    quarter, at = me.dp // 8, me.dp % 8
    gate_to = (8 * quarter + me.sq, at)
    gate_self = me.sq == at
    chan_from = (8 * (me.dp % 2) + me.sq, me.dp // 2)
    chan_to = (2 * me.sq + me.dp // 8, me.dp % 8)
    chan_self = jnp.logical_and(chan_from[0] == me.dp, chan_from[1] == me.sq)
    barrier, count = greet(seq_peers(me) + dp_peers(me))

    @pl.when(jnp.logical_not(gate_self))
    def _():
        pl.semaphore_signal(barrier, inc=1, device_id=gate_to, device_id_type=MESH)

    @pl.when(jnp.logical_not(chan_self))
    def _():
        pl.semaphore_signal(barrier, inc=1, device_id=chan_from, device_id_type=MESH)

    pl.semaphore_wait(barrier, count + jnp.where(gate_self, 0, 1) + jnp.where(chan_self, 0, 1))

    sent = []

    def push(src, dst, send, recv, device):
        sent.append(remote(src, dst, send, recv, device))
        sent[-1].start()

    def arrived(dst, send, recv):
        remote(dst, dst, send, recv, me.sibling()).wait_recv()

    xs, ys = (me.dp_peer(me.x_dp(1)), me.dp_peer(me.x_dp(3))), (me.dp_peer(me.y_dp(1)), me.dp_peer(me.y_dp(3)))
    feed_up = RingSum(me, *xs, lambda k, q: s1f.at[0, pl.ds((me.x + k) % 4, 1), pl.ds(q * 32, 32)], *fa)
    feed_low = RingSum(me, *ys, lambda k, q: s1f.at[1, pl.ds((me.y + k) % 4, 1), pl.ds(q * 32, 32)], *fb)
    mix_up = RingSum(me, *ys, lambda k, q: mg.at[:, (me.y + k) % 4, pl.ds(q * 32, 32)], *ma)
    mix_low = RingSum(me, *xs, lambda k, q: mg.at[(me.x + k) % 4, :, pl.ds(HALF + q * 32, 32)], *mb)
    last_up = RingSum(me, *xs, lambda k, q: s1.at[0, pl.ds((me.x + k) % 4, 1), pl.ds(q * 32, 32)], *na)
    last_low = RingSum(me, *ys, lambda k, q: s1.at[1, pl.ds((me.y + k) % 4, 1), pl.ds(q * 32, 32)], *nb)

    inner = Scatter(me, part, *one)
    loads[0].wait()
    inner.start()
    for copy in loads[1:]:
        copy.start()
    loads[1].wait()
    feed_up.start()
    feed_low.start()
    inner.join()
    for copy in loads[2:]:
        copy.wait()

    def tile(i, carry):
        tx, ty = (me.x + 2 + i) % 4, ((me.y + 2) // 2 + i // 4) % 2
        here = pl.ds(pl.multiple_of((tx * 2 + ty) * 256, 256), 256)
        left = tn(normed[:, here], both[...]).astype(bf16)
        right = tn(adj_out[:, here], mixed[...]).astype(bf16)
        for h in range(2):
            mg[tx, ty * 2 + h, :, : 2 * WP] = left[h * T : (h + 1) * T]
            mg[tx, ty * 2 + h, :, 2 * WP : MW] = right[h * T : (h + 1) * T]

        @pl.when(i == 3)
        def _():
            mix_up.start_far()
            inner.relay()
            feed_up.relay()
            feed_low.relay()

        @pl.when(i == 4)
        def _():
            mix_low.start_far()

        return carry

    lax.fori_loop(0, 8, tile, 0)
    mix_up.start_near()
    mix_low.start_near()
    mix_up.relay()
    mix_low.relay()
    inner.finish(adj)

    def pull(i, carry):
        here = pl.ds(pl.multiple_of(i * 16, 16), 16)
        pulled, terms = norm_pull(tok[here].astype(f32), gains[0:1], adj[here])
        in_grad[here] = adj_middle[here] + pulled
        return carry + jnp.sum(terms, axis=0, keepdims=True)

    gain_one = lax.fori_loop(0, T // 16, pull, jnp.zeros((1, D), f32), unroll=2)
    gp[...] = jnp.zeros(gp.shape, f32)
    for k in range(DP):
        gp[k, 0:1] = gain_one[:, k * 128 : (k + 1) * 128]
        gp[k, 1:2] = gain_two[:, k * 128 : (k + 1) * 128]
    for k in range(1, DP):
        to = (me.dp + k) % DP
        push(gp.at[to], gp_in.at[k], gs.at[k], gr.at[k], me.dp_peer(to))

    feed_up.finish(lambda q: lastf.at[:, pl.ds(q * 32, 32)])
    feed_low.finish(lambda q: lastf.at[:, pl.ds(HALF + q * 32, 32)])

    def feed_columns(p, j):
        return lanes_of(p * FF + j * FL, FL)

    keeps = [
        pltpu.make_async_copy(
            lastf.at[0, rows_of(me.sq * 16, 16), pl.ds(p * FL, FL)], feed_out.at[:, feed_columns(p, me.sq)], ls.at[p]
        )
        for p in range(3)
    ]
    for copy in keeps:
        copy.start()
    order = (4, 3, 5, 2, 6, 1, 7)
    for k in order:
        to = (me.sq + k) % SEQ
        for p in range(3):
            push(lastf.at[0, rows_of(to * 16, 16), pl.ds(p * FL, FL)], feed_out.at[:, feed_columns(p, me.sq)],
                 f3s.at[p, k], f3r.at[p, k], me.seq_peer(k))

    mix_up.finish(lambda q: s1.at[0, :, pl.ds(q * 32, 32)])
    last_up.start()
    mix_low.finish(lambda q: s1.at[1, :, pl.ds(q * 32, 32)])
    last_low.start()
    for k in range(1, DP):
        arrived(gp_in.at[k], gs.at[k], gr.at[k])

    def sum_gains(k, total):
        return total + gp_in[k]

    gain_sum[...] = lax.fori_loop(1, DP, sum_gains, gp[me.dp])
    for k in range(1, SEQ):
        push(gain_sum, gain_in.at[k], qs.at[k], qr.at[k], me.seq_peer(k))

    last_up.relay()
    last_low.relay()
    last_up.finish(lambda q: last.at[:, pl.ds(q * 32, 32)])
    last_low.finish(lambda q: last.at[:, pl.ds(HALF + q * 32, 32)])

    columns = pl.ds(0, MW)
    keeps.append(pltpu.make_async_copy(last.at[0, rows_of(me.sq * 16, 16), columns], mix_out.at[me.sq], ls.at[3]))
    keeps[-1].start()
    for k in order:
        to = (me.sq + k) % SEQ
        push(last.at[0, rows_of(to * 16, 16), columns], mix_out.at[me.sq], m3s.at[k], m3r.at[k], me.seq_peer(k))
    gate_sum, chan_sum = last.at[0, pl.ds(0, 96), pl.ds(MW, 128)], last.at[0, pl.ds(96, 32), pl.ds(MW, 128)]
    gate_copy = remote(gate_sum, gate_out, hs.at[0], hr.at[0], gate_to)
    chan_copy = remote(chan_sum, chan_out, hs.at[1], hr.at[1], chan_to)
    gate_local = pltpu.make_async_copy(gate_sum, gate_out, ls.at[4])
    chan_local = pltpu.make_async_copy(chan_sum, chan_out, ls.at[5])

    @pl.when(jnp.logical_not(gate_self))
    def _():
        gate_copy.start()

    @pl.when(gate_self)
    def _():
        gate_local.start()

    @pl.when(jnp.logical_not(chan_self))
    def _():
        chan_copy.start()

    @pl.when(chan_self)
    def _():
        chan_local.start()

    for k in range(1, SEQ):
        arrived(gain_in.at[k], qs.at[k], qr.at[k])
    total = gain_sum[...]
    for k in range(1, SEQ):
        total = total + gain_in[k]
    gain_out[...] = total
    for k in range(1, SEQ):
        source = (me.sq - k + SEQ) % SEQ
        for p in range(3):
            arrived(feed_out.at[:, feed_columns(p, source)], f3s.at[p, k], f3r.at[p, k])
        arrived(mix_out.at[source], m3s.at[k], m3r.at[k])

    @pl.when(jnp.logical_not(gate_self))
    def _():
        gate_copy.wait()

    @pl.when(gate_self)
    def _():
        gate_local.wait()

    @pl.when(jnp.logical_not(chan_self))
    def _():
        chan_copy.wait()

    @pl.when(chan_self)
    def _():
        chan_local.wait()

    for copy in keeps:
        copy.wait()
    for copy in sent:
        copy.wait_send()


def close_call(part, normed, both, adj_out, mixed, extra, s1, tok, adj_middle, gains, gain_two):
    sds = jax.ShapeDtypeStruct
    hbm, vmem = pl.BlockSpec(memory_space=ANY), pl.BlockSpec(memory_space=VMEM)
    wide = MW + 128
    return pl.pallas_call(
        close_kernel,
        out_shape=(
            sds((T, D), f32), sds((SEQ, 16, MW), bf16), sds((16, 3 * FF), bf16),
            sds((96, 128), bf16), sds((32, 128), bf16), sds((8, 128), f32),
        ),
        in_specs=[hbm] * 7 + [vmem] * 4,
        out_specs=[vmem] * 6,
        scratch_shapes=[
            VMEM((G, D), bf16), VMEM((G, D), bf16), VMEM((G, 2 * WP), bf16), VMEM((G, D), bf16), VMEM((G, WP), bf16),
            VMEM((4, 4, T, wide), bf16), VMEM((2, 4, HALF, FW), bf16), VMEM((2, 4, HALF, wide), bf16),
            VMEM((1, T, FW), bf16), VMEM((1, T, wide), bf16), VMEM((T, D), f32),
            VMEM((DP, 8, 128), f32), VMEM((DP, 8, 128), f32), VMEM((8, 128), f32), VMEM((SEQ, 8, 128), f32),
            *Scatter.scratch(D),
            *RingSum.scratch((1, 32, FW)), *RingSum.scratch((1, 32, FW)),
            *RingSum.scratch((4, 32, wide)), *RingSum.scratch((4, 32, wide)),
            *RingSum.scratch((1, 32, wide)), *RingSum.scratch((1, 32, wide)),
            DMA((8,)), DMA((8,)), DMA((3, 8)), DMA((3, 8)), DMA((DP,)), DMA((DP,)), DMA((2,)), DMA((2,)),
            DMA((SEQ,)), DMA((SEQ,)), DMA((6,)), DMA((7,)),
        ],
        compiler_params=pltpu.CompilerParams(collective_id=4, has_side_effects=True, vmem_limit_bytes=62 << 20),
        cost_estimate=pl.CostEstimate(flops=5 * G * D * WP, bytes_accessed=100 << 20, transcendentals=0),
        name="close",
    )(part, normed, both, adj_out, mixed, extra, s1, tok, adj_middle, gains, gain_two)


def finish_kernel(in_grad, act, mix, feed, gate, chan, gain, in_out, act_out, mix_out, feed_out, gate_out, chan_out, gain_out):
    me = Place()

    def keep(i, c):
        here = pl.ds(pl.multiple_of(i * 16, 16), 16)
        in_out[here] = in_grad[here]
        act_out[here] = act[here]
        return c

    lax.fori_loop(0, T // 16, keep, 0)
    for p in range(3):
        for j in range(SEQ):
            value = mix[j, :, p * WP : (p + 1) * WP].astype(f32)
            mix_out[:, p * W + j * WL : p * W + (j + 1) * WL] = value[:, :WL]

    def widen(i, c):
        here = lanes_of(i * 2048, 2048)
        feed_out[:, here] = feed[:, here].astype(f32)
        return c

    lax.fori_loop(0, 9, widen, 0)
    value = jnp.concatenate([gate[0:48].astype(f32)[0:40], gate[48:96].astype(f32)[0:40]], 1)
    gate_out[...] = jnp.where(me.sq < 4, value[:, :BW], value[:, BW - 128 : 2 * BW - 128])
    value = jnp.concatenate([chan[0:16].astype(f32)[0:8], chan[16:32].astype(f32)[0:8]], 1)
    first = (8 * (me.dp % 2) + me.sq) * 20
    first = first - jnp.where(first >= 128, 128, 0)
    chan_out[...] = pltpu.roll(value, (256 - first) % 256, 1)[:, :20]
    gain_out[...] = pltpu.roll(gain[...], (128 - me.sq * 16) % 128, 1)[0:2, 0:16]


def finish_call(in_grad, act, mix, feed, gate, chan, gain):
    sds = jax.ShapeDtypeStruct
    vmem = pl.BlockSpec(memory_space=VMEM)
    return pl.pallas_call(
        finish_kernel,
        out_shape=(
            sds((T, D), f32), sds((T, D), bf16), sds((16, 3 * W), f32), sds((16, 3 * FF), f32),
            sds((40, BW), f32), sds((8, 20), f32), sds((2, 16), f32),
        ),
        in_specs=[vmem] * 7,
        out_specs=[vmem] * 7,
        compiler_params=pltpu.CompilerParams(vmem_limit_bytes=62 << 20),
        name="finish",
    )(in_grad, act, mix, feed, gate, chan, gain)


def shards(tokens, segments, mixer_weights, norm_gains, gate_weights, channel_terms, feed_weights, cotangent):
    (
        cot_all, w, normed, *saved, mixed, hidden, adj_gu, back_part, feed_part, norm_two,
        gates, terms, gains, lab, middle,
    ) = forward_call(
        tokens, cotangent, mixer_weights, feed_weights, segments[None], norm_gains.T, gate_weights, channel_terms.T
    )
    adj_all, s1, both, in_part, adj_middle, activations, gain_two, extra = turn_call(
        back_part, feed_part, norm_two, cot_all, hidden, adj_gu, saved, w, middle, cotangent, gains, gates, terms, lab
    )
    input_gradient, mix_out, feed_out, gate_out, chan_out, gain_out = close_call(
        in_part, normed, both, adj_all, mixed, extra.reshape(4, 4, 128, 128), s1, tokens, adj_middle, gains, gain_two
    )
    input_gradient, activations, mixer_gradient, feed_gradient, gate_gradient, channel_gradient, gain_gradient = (
        finish_call(input_gradient, activations, mix_out, feed_out, gate_out, chan_out, gain_out)
    )
    return (
        activations, input_gradient, mixer_gradient, gain_gradient.T, gate_gradient, channel_gradient.T, feed_gradient
    )


def solution(mesh):
    one = P(("dp", "seq"))
    two = P(("dp", "seq"), None)
    placed = (two, one, two, two, two, two, two, two)
    return jax.shard_map(shards, mesh=mesh, in_specs=placed, out_specs=(two,) * 7, check_vma=False)
```
